32 devices in a mesh: groups: 2 (over x), pat: 16 (over z, y, core), cov: 1.
Axes of the slice: x: 2, y: 2, z: 4, core: 2. Of those that a mesh axis runs over, the one named last changes fastest.
Arguments:
- covariates: bfloat16 [4096, 19968], P(('groups', 'pat'), 'cov'), parts along dimension 0, may hold values from -13 to 13
- weights: bfloat16 [4096, 16], P(('groups', 'pat')), parts along dimension 0, may hold values from 0.19921875 to 5
- arms: int32 [4096, 48], P(('groups', 'pat'), 'cov'), parts along dimension 0, may hold values from 0 to 1, as said below
- pick: int32 [48], replicated, may hold values from 0 to 15
Outputs:
- balance: float32 [96, 1, 19968], P('groups', 'cov', 'pat'), parts along dimension 0
The draws below stay inside these ranges and needn't reach their ends.
There are 2 independent parts, one for each index of `groups`. The reference program is written for one: setup_inputs(seed, part) draws one part's arguments, and reference() takes and returns one part's arrays. A program takes and returns all parts, laid end to end along the dimension named above; an argument that names none is the same for every part. Nothing has to cross between parts.
Inputs may be any that keep to these rules, and one draw needn't show every extreme that they name: Every comparison has patients in both arms.
All inputs are finite; a program needn't handle non-finite values.
Results may differ from the reference program's by a relative error of at most 0.0003.
Values may be sent and summed in bfloat16 or wider, within the bound.
No kernel may reach another device: no remote copies, remote signals or barrier semaphores. Data moves between devices by JAX's collectives and lax.ppermute only.
A program may use at most 128 MiB of HBM per device.

```python
import math
import jax
import jax.numpy as jnp
from jax import lax

C = 19968
Q = 48
K = 16
PATIENTS = 2048
N_COV = 1


def shared_propensity(key):
    rows = jnp.arange(PATIENTS, dtype=jnp.int32)
    base = jax.random.randint(key, (PATIENTS,), 10, 30)
    return base + 60 * rows // PATIENTS


def draw_arms(key, part):
    level = shared_propensity(key)
    key = jax.random.fold_in(key, 1)
    key_scores, key_factor = jax.random.split(key, 2)
    factor = jax.random.randint(key_factor, (Q,), 6, 25)
    threshold = level[:, None] * factor[None, :] // 10
    scores = jax.random.randint(key_scores, (PATIENTS, Q), 0, 200)
    return (scores < threshold).astype(jnp.int32)


def draw_covariates(key, part):
    level = shared_propensity(key).astype(jnp.float32)
    key = jax.random.fold_in(key, 2)
    key_scale, key_offset, key_beta, key_noise = jax.random.split(key, 4)
    scale = jnp.exp(jax.random.uniform(key_scale, (C,), jnp.float32, jnp.log(0.05), jnp.log(2.0)))
    offset = scale * jax.random.uniform(key_offset, (C,), jnp.float32, -1.0, 1.0)
    beta = scale * jax.random.uniform(key_beta, (C,), jnp.float32, 0.3, 1.5)
    latent = level / 40.0 - 1.25
    noise = jnp.clip(jax.random.normal(key_noise, (PATIENTS, C), jnp.float32), -4.0, 4.0)
    values = offset[None, :] + beta[None, :] * latent[:, None] + scale[None, :] * noise
    return values.astype(jnp.bfloat16)


def plant(result, key, low, largest):
    spot = [jax.random.randint(jax.random.fold_in(key, axis), (), 0, length) for axis, length in enumerate(result.shape)]
    longest = result.shape.index(max(result.shape))
    next_to = spot[:longest] + [(spot[longest] + 1) % result.shape[longest]] + spot[longest + 1:]
    return result.at[tuple(spot)].set(low).at[tuple(next_to)].set(largest)


def shard_levels(stream_key, shape, shards, smallest, high):
    factor_of, own = 1.0, jax.random.fold_in(stream_key, 6)
    for dim, shards_of in shards:
        steps = jnp.exp(jax.random.uniform(jax.random.fold_in(own, dim), (shards_of,), jnp.float32, smallest / len(shards), high / len(shards)))
        factor_of = factor_of * jnp.repeat(steps, shape[dim] // shards_of).reshape([-1 if axis == dim else 1 for axis in range(len(shape))])
    return factor_of


def setup_inputs(seed: int = 0, part: int = 0) -> dict:
    splits = jax.random.split(jax.random.key(seed), 5)
    own_keys = jax.random.split(jax.random.fold_in(splits[4], part), 5)
    return {
        "covariates": draw_covariates(jax.random.fold_in(jax.random.fold_in(splits[4], part), 71), part),
        "weights": jnp.clip(jnp.exp(math.log(5.0) - 3.2227897 * jax.random.uniform(own_keys[1], (PATIENTS, K), jnp.float32) ** shard_levels(own_keys[1], (PATIENTS, K), ((0, 16),), -0.2, 0.2)), 0.19921875, 5.0).astype(jnp.bfloat16),
        "arms": draw_arms(jax.random.fold_in(jax.random.fold_in(splits[4], part), 71), part),
        "pick": plant(jax.random.randint(splits[3], (Q,), 0, K), jax.random.fold_in(splits[3], 1), 0, K - 1).astype(jnp.int32),
    }


def reference(covariates, weights, arms, pick):
    onehot = (jnp.arange(K)[:, None] == pick[None, :]).astype(weights.dtype)
    picked = jnp.dot(weights, onehot, preferred_element_type=jnp.float32).astype(weights.dtype)
    arm_vals = arms.astype(weights.dtype)
    target = picked * arm_vals
    comparator = picked * (1 - arm_vals)
    panel = jnp.concatenate([target, comparator], axis=1)
    squares = (covariates.astype(jnp.float32) * covariates.astype(jnp.float32)).astype(covariates.dtype)
    first = jnp.dot(panel.T, covariates, preferred_element_type=jnp.float32)
    second = jnp.dot(panel.T, squares, preferred_element_type=jnp.float32)
    totals = lax.optimization_barrier(jnp.sum(panel.astype(jnp.float32), axis=0))
    means = first / totals[:, None]
    spread = second / totals[:, None] - means * means
    pooled = jnp.maximum((spread[:Q] + spread[Q:]) / 2.0, 0.01)
    balance = (means[:Q] - means[Q:]) / jnp.sqrt(pooled)
    return balance.reshape(Q, N_COV, C // N_COV)
```

```python
import functools

import jax
import jax.numpy as jnp
from jax import lax
from jax.experimental import pallas as pl
from jax.experimental.pallas import tpu as pltpu
from jax.sharding import PartitionSpec as P

LANES = 128
VMEM_BYTES = 48 * 1024 * 1024


def round_up(value, multiple):
    return -(-value // multiple) * multiple


def pick_bits(value, bits):
    result = 0
    for place, bit in enumerate(bits):
        result = result + ((value >> bit) & 1) * (1 << place)
    return result


def spread_bits(value, bits):
    result = 0
    for place, bit in enumerate(bits):
        result += ((value >> place) & 1) << bit
    return result


class Half:
    def __init__(self, start, width, raw_bits, all_bits):
        self.start = start
        self.width = width
        self.padded = round_up(width, LANES)
        self.raw_bits = raw_bits
        self.sum_bits = [bit for bit in all_bits if bit not in raw_bits]
        self.members = [spread_bits(r, raw_bits) for r in range(1 << len(raw_bits))]


def halves_of(n, block):
    all_bits = list(range(n.bit_length() - 1))
    first = min(round_up(block // 2, LANES), block)
    return [
        Half(0, first, [0, 1], all_bits),
        Half(first, block - first, [0, 2], all_bits),
    ]


def pack_kernel(n, block, group, halves, x_ref, *refs):
    members = [len(half.members) for half in halves]
    outs = [refs[:members[0]], refs[members[0]:sum(members)]]
    buffers = refs[sum(members):sum(members) + 2]
    sems = refs[-1]
    step = pl.program_id(0)
    me = lax.axis_index("pat")
    rows = x_ref.shape[0]
    for i in range(group):
        owner = step * group + i
        relative = owner ^ me
        for h, half in enumerate(halves):
            left = i * block + half.start
            for row in range(0, rows, 32):
                piece = x_ref[row:row + 32, left:left + half.width]
                if half.padded > half.width:
                    piece = jnp.concatenate(
                        [piece, jnp.zeros((32, half.padded - half.width), piece.dtype)], axis=1
                    )
                buffers[h][owner, row:row + 32, :] = piece
            member = pick_bits(relative, half.raw_bits)
            place = pick_bits(relative, half.sum_bits)
            for r in range(members[h]):

                @pl.when(member == r)
                def _():
                    pltpu.make_async_copy(
                        buffers[h].at[owner], outs[h][r].at[place], sems.at[h, owner]
                    ).start()

    @pl.when(step == pl.num_programs(0) - 1)
    def _():
        for h in range(2):
            for owner in range(n):
                pltpu.make_async_copy(
                    buffers[h].at[owner], outs[h][0].at[0], sems.at[h, owner]
                ).wait()


def pack(covariates, n, halves):
    rows, columns = covariates.shape
    block = columns // n
    group = 4
    while group < n and (group * block) % LANES:
        group *= 2
    out_shape = [
        jax.ShapeDtypeStruct((n // len(half.members), rows, half.padded), covariates.dtype)
        for half in halves
        for _ in half.members
    ]
    outs = pl.pallas_call(
        functools.partial(pack_kernel, n, block, group, halves),
        grid=(n // group,),
        in_specs=[pl.BlockSpec((rows, group * block), lambda s: (0, s))],
        out_specs=[pl.BlockSpec(memory_space=pl.ANY)] * len(out_shape),
        out_shape=out_shape,
        scratch_shapes=[
            pltpu.VMEM((n, rows, half.padded), covariates.dtype) for half in halves
        ]
        + [pltpu.SemaphoreType.DMA((2, n))],
        compiler_params=pltpu.CompilerParams(vmem_limit_bytes=VMEM_BYTES),
        cost_estimate=pl.CostEstimate(
            flops=0, bytes_accessed=4 * covariates.size, transcendentals=0
        ),
        name="pack",
    )(covariates)
    first = len(halves[0].members)
    return outs[:first], outs[first:]


def panel_kernel(n, weightings, halves, gathered_ref, pick_ref, *out_refs):
    panels, stats_ref = out_refs[:-1], out_refs[-1]
    me = lax.axis_index("pat")
    comps = pick_ref.shape[0]
    rows = gathered_ref.shape[2]
    index = lax.broadcasted_iota(jnp.int32, (comps, weightings), 1)
    onehot = jnp.where(index == pick_ref[...], 1.0, 0.0).astype(jnp.bfloat16)

    def columns_of(device):
        weights = gathered_ref[device, 0:weightings, :]
        arms = gathered_ref[device, weightings:weightings + comps, :].astype(jnp.float32)
        picked = jnp.dot(onehot, weights, preferred_element_type=jnp.float32)
        return weights, picked * arms, picked * (1.0 - arms)

    target_sum = jnp.zeros((comps, rows), jnp.float32)
    other_sum = jnp.zeros((comps, rows), jnp.float32)
    for device in range(n):
        _, target, other = columns_of(device)
        target_sum += target
        other_sum += other
    total_target = jnp.sum(target_sum, axis=1, keepdims=True)
    total_other = jnp.sum(other_sum, axis=1, keepdims=True)
    light = jnp.where(total_target <= total_other, 1.0, 0.0)
    stats_ref[0] = jnp.broadcast_to(1.0 / total_target, (comps, LANES))
    stats_ref[1] = jnp.broadcast_to(1.0 / total_other, (comps, LANES))
    stats_ref[2] = jnp.broadcast_to(light, (comps, LANES))
    for h, half in enumerate(halves):
        first_ref, second_ref = panels[2 * h], panels[2 * h + 1]
        for r, member in enumerate(half.members):
            weights, target, other = columns_of(me ^ member)
            here = slice(r * rows, (r + 1) * rows)
            lighter = light * target + (1.0 - light) * other
            first_ref[0:comps, here] = lighter.astype(jnp.bfloat16)
            first_ref[comps:comps + weightings, here] = weights
            second_ref[0:comps, here] = target.astype(jnp.bfloat16)
            second_ref[comps:2 * comps, here] = other.astype(jnp.bfloat16)


def make_panels(gathered, pick, weightings, halves):
    n, _, rows = gathered.shape
    comps = pick.shape[0]
    out_shape = []
    for half in halves:
        count = len(half.members) * rows
        out_shape.append(jax.ShapeDtypeStruct((comps + weightings, count), jnp.bfloat16))
        out_shape.append(jax.ShapeDtypeStruct((2 * comps, count), jnp.bfloat16))
    out_shape.append(jax.ShapeDtypeStruct((3, comps, LANES), jnp.float32))
    return pl.pallas_call(
        functools.partial(panel_kernel, n, weightings, halves),
        in_specs=[pl.BlockSpec(memory_space=pltpu.VMEM)] * 2,
        out_specs=[pl.BlockSpec(memory_space=pltpu.VMEM)] * len(out_shape),
        out_shape=out_shape,
        compiler_params=pltpu.CompilerParams(vmem_limit_bytes=VMEM_BYTES),
        cost_estimate=pl.CostEstimate(
            flops=2 * gathered.size * comps, bytes_accessed=4 * gathered.size, transcendentals=0
        ),
        name="panels",
    )(gathered, pick.reshape(comps, 1))


def moments_kernel(x_count, *refs):
    xs = refs[:x_count]
    first_ref, second_ref, stats_ref = refs[x_count:x_count + 3]
    outs = refs[x_count + 3:]
    first_rows = first_ref.shape[0]
    comps = second_ref.shape[0] // 2
    inverse_target = stats_ref[0][:, 0:1]
    inverse_other = stats_ref[1][:, 0:1]
    for place, out_ref in enumerate(outs):
        x = jnp.concatenate([ref[place] for ref in xs], axis=0)
        first = jnp.dot(first_ref[...], x, preferred_element_type=jnp.float32)
        squares = (x.astype(jnp.float32) * x.astype(jnp.float32)).astype(jnp.bfloat16)
        second = jnp.dot(second_ref[...], squares, preferred_element_type=jnp.float32)
        out_ref[0, 0:first_rows, :] = first
        out_ref[0, first_rows:first_rows + comps, :] = (
            second[0:comps] * inverse_target + second[comps:2 * comps] * inverse_other
        )


def moments(xs, first, second, stats):
    places, rows, width = xs[0].shape
    comps = second.shape[0] // 2
    out_rows = first.shape[0] + comps
    whole = lambda s: (0, 0)
    return pl.pallas_call(
        functools.partial(moments_kernel, len(xs)),
        grid=(places // 2,),
        in_specs=[pl.BlockSpec((2, rows, width), lambda s: (s, 0, 0))] * len(xs)
        + [
            pl.BlockSpec(first.shape, whole),
            pl.BlockSpec(second.shape, whole),
            pl.BlockSpec(stats.shape, lambda s: (0, 0, 0)),
        ],
        out_specs=[pl.BlockSpec((1, out_rows, width), lambda s: (s, 0, 0))] * 2,
        out_shape=[jax.ShapeDtypeStruct((places // 2, out_rows, width), jnp.float32)] * 2,
        compiler_params=pltpu.CompilerParams(vmem_limit_bytes=VMEM_BYTES),
        cost_estimate=pl.CostEstimate(
            flops=2 * places * len(xs) * rows * width * (first.shape[0] + second.shape[0]),
            bytes_accessed=places * width * (2 * len(xs) * rows + 4 * out_rows),
            transcendentals=0,
        ),
        name="moments",
    )(*xs, first, second, stats)


def finish_kernel(weightings, widths, pick_ref, stats_ref, *refs):
    out_ref = refs[-1]
    comps = pick_ref.shape[0]
    index = lax.broadcasted_iota(jnp.int32, (comps, weightings), 1)
    onehot = jnp.where(index == pick_ref[...], 1.0, 0.0)
    inverse_target = stats_ref[0][:, 0:1]
    inverse_other = stats_ref[1][:, 0:1]
    light = stats_ref[2][:, 0:1] > 0.5
    start = 0
    for h, width in enumerate(widths):
        kept, arrived = refs[2 * h], refs[2 * h + 1]
        sums = kept[...] + arrived[...]
        lighter = sums[0:comps]
        both = jnp.dot(
            onehot,
            sums[comps:comps + weightings],
            precision=lax.Precision.HIGHEST,
            preferred_element_type=jnp.float32,
        )
        spread = sums[comps + weightings:2 * comps + weightings]
        heavier = both - lighter
        mean_target = jnp.where(light, lighter, heavier) * inverse_target
        mean_other = jnp.where(light, heavier, lighter) * inverse_other
        variance = spread - mean_target * mean_target - mean_other * mean_other
        pooled = jnp.maximum(variance / 2.0, 0.01)
        balance = (mean_target - mean_other) / jnp.sqrt(pooled)
        out_ref[:, 0, start:start + width] = balance[:, 0:width]
        start += width


def finish(parts, pick, stats, weightings, widths):
    comps = pick.shape[0]
    operands = [array for pair in parts for array in pair]
    return pl.pallas_call(
        functools.partial(finish_kernel, weightings, widths),
        in_specs=[pl.BlockSpec(memory_space=pltpu.VMEM)] * (2 + len(operands)),
        out_specs=pl.BlockSpec(memory_space=pltpu.VMEM),
        out_shape=jax.ShapeDtypeStruct((comps, 1, sum(widths)), jnp.float32),
        compiler_params=pltpu.CompilerParams(vmem_limit_bytes=VMEM_BYTES),
        cost_estimate=pl.CostEstimate(
            flops=20 * comps * sum(widths),
            bytes_accessed=4 * sum(2 * part[0].size for part in parts),
            transcendentals=comps * sum(widths),
        ),
        name="finish",
    )(pick.reshape(comps, 1), stats, *operands)


def swap(array, n, mask):
    return lax.ppermute(array, "pat", [(d, d ^ mask) for d in range(n)])


def on_device(n, covs, covariates, weights, arms, pick):
    weightings = weights.shape[1]
    block = covariates.shape[1] // n
    halves = halves_of(n, block)
    arm_rows = arms.T.astype(weights.dtype)
    if covs > 1:
        arm_rows = lax.all_gather(arm_rows, "cov", axis=0, tiled=True)
    gathered = lax.all_gather(jnp.concatenate([weights.T, arm_rows], axis=0), "pat")
    packed = pack(covariates, n, halves)
    shares = [
        [arrays[0]] + [swap(arrays[r], n, half.members[r]) for r in range(1, len(arrays))]
        for half, arrays in zip(halves, packed)
    ]
    *panels, stats = make_panels(gathered, pick, weightings, halves)
    parts = []
    for h, half in enumerate(halves):
        kept, sent = moments(shares[h], panels[2 * h], panels[2 * h + 1], stats)
        arrived = swap(sent, n, 1 << half.sum_bits[0])
        parts.append((kept, arrived))
    for level in range(1, len(halves[0].sum_bits)):
        for h, half in enumerate(halves):
            kept, arrived = parts[h]
            sent = kept[1::2] + arrived[1::2]
            parts[h] = (kept[0::2] + arrived[0::2], swap(sent, n, 1 << half.sum_bits[level]))
    parts = [(kept[0], arrived[0]) for kept, arrived in parts]
    return finish(parts, pick, stats, weightings, [half.width for half in halves])


def solution(mesh):
    placed = (
        P(("groups", "pat"), "cov"),
        P(("groups", "pat"), None),
        P(("groups", "pat"), "cov"),
        P(),
    )
    body = functools.partial(on_device, mesh.shape["pat"], mesh.shape["cov"])
    return jax.shard_map(
        body, mesh=mesh, in_specs=placed, out_specs=P("groups", "cov", "pat"), check_vma=False
    )
```

```python
import functools

import jax
import jax.numpy as jnp
from jax import lax
from jax.experimental import pallas as pl
from jax.experimental.pallas import tpu as pltpu
from jax.sharding import PartitionSpec as P

LANES = 128
VMEM_BYTES = 48 * 1024 * 1024


def round_up(value, multiple):
    return -(-value // multiple) * multiple


def pick_bits(value, bits):
    result = 0
    for place, bit in enumerate(bits):
        result = result + ((value >> bit) & 1) * (1 << place)
    return result


def spread_bits(value, bits):
    result = 0
    for place, bit in enumerate(bits):
        result += ((value >> place) & 1) << bit
    return result


class Plan:
    def __init__(self, n, block):
        self.n = n
        self.block = block
        self.tiles = round_up(block, LANES) // LANES
        self.share = (self.tiles + 1) // 2
        self.high_bits = list(range(3, n.bit_length() - 1))
        first = (3 * self.share + 4) // 5
        self.chunks = [(0, first)]
        if self.share > first:
            self.chunks.append((first, self.share - first))

    def width(self, chunk):
        return self.chunks[chunk][1] * LANES

    def ring(self, side, chunk):
        start, count = self.chunks[chunk]
        low = side * self.share + start
        return range(low, min(low + count, self.tiles if side else self.share))

    def folded(self, owner):
        first = owner * self.block // LANES
        return (owner * self.block + self.block - 1) // LANES - first == self.tiles

    def folds(self, chunk):
        return [] if chunk else [owner for owner in range(self.n) if self.folded(owner)]

    def panel_rows(self, height):
        return round_up(-(-height // self.chunks[0][1]), 16)

    def place_bits(self, side):
        return [2 - side] + self.high_bits + [0]

    def by_rows(self):
        return [(d, d ^ (2 + 2 * (d & 1))) for d in range(self.n)]

    def by_sums(self):
        return [(d, d ^ (4 - 2 * (d & 1))) for d in range(self.n)]

    def by_mask(self, mask):
        return [(d, d ^ mask) for d in range(self.n)]


def pack_kernel(plan, chunk, x_ref, mine_ref, *refs):
    outs, (ends, fold, end_sems, sems) = refs[-8:-4], refs[-4:]
    me = lax.axis_index("pat")
    rows = x_ref.shape[0]
    folded = plan.folds(chunk)

    def tile(index, count=1):
        return x_ref.at[:, pl.ds(index * LANES, count * LANES)]

    def end_copies(number):
        first = folded[number] * plan.block // LANES
        return [
            pltpu.make_async_copy(
                tile(first + which * plan.tiles), ends.at[number, which], end_sems.at[number, which]
            )
            for which in range(2)
        ]

    def move(source, side, owner, lane, sem):
        away = (me & 1) ^ side
        relative = owner ^ me ^ away
        target = 2 * away + ((relative >> (1 + side)) & 1)
        place = pick_bits(relative, plan.place_bits(side))
        lanes = pl.ds(lane, source.shape[-1])
        for t in range(4):

            @pl.when(target == t)
            def _():
                here = pl.ds(pl.multiple_of(place * rows, rows), rows)
                pltpu.make_async_copy(source, outs[t].at[here, lanes], sem).start()

        return pltpu.make_async_copy(source, outs[0].at[pl.ds(0, rows), lanes], sem)

    for number in range(len(folded)):
        for copy in end_copies(number):
            copy.start()
    waits = []
    for owner in range(plan.n):
        first = owner * plan.block // LANES
        for side in range(2):
            places = plan.ring(side, chunk)
            skip = int(0 in places and owner in folded)
            if len(places) > skip:
                source = tile(first + places[skip], len(places) - skip)
                waits.append(move(source, side, owner, skip * LANES, sems.at[len(waits)]))
    if chunk == 0:
        height = plan.panel_rows(mine_ref.shape[0])
        for piece in range(mine_ref.shape[0] // height):
            for out in outs[1::2]:
                copy = pltpu.make_async_copy(
                    mine_ref.at[pl.ds(piece * height, height), :],
                    out.at[pl.ds(plan.n // 2 * rows, height), pl.ds(piece * LANES, LANES)],
                    sems.at[len(waits)],
                )
                copy.start()
                waits.append(copy)
    for number, owner in enumerate(folded):
        for copy in end_copies(number):
            copy.wait()
        edge = owner * plan.block % LANES
        lane = lax.broadcasted_iota(jnp.int32, (16, LANES), 1)
        for row in range(0, rows, 16):
            here = slice(row, row + 16)
            head = ends[number, 0, here, :].astype(jnp.float32)
            tail = ends[number, 1, here, :].astype(jnp.float32)
            fold[number, here, :] = jnp.where(lane >= edge, head, tail).astype(fold.dtype)
        waits.append(move(fold.at[number], 0, owner, 0, sems.at[len(waits)]))
    for copy in waits:
        copy.wait()


def pack(covariates, mine, plan, chunk, after):
    rows = covariates.shape[0]
    tail = 0 if chunk else plan.panel_rows(mine.shape[0])
    out_shape = [
        jax.ShapeDtypeStruct((plan.n // 2 * rows + sent * tail, plan.width(chunk)), covariates.dtype)
        for sent in (0, 1, 0, 1)
    ]
    folds = max(1, len(plan.folds(chunk)))
    moves = 2 * plan.n + folds + 2 * (mine.shape[0] // 16)
    return pl.pallas_call(
        functools.partial(pack_kernel, plan, chunk),
        in_specs=[pl.BlockSpec(memory_space=pl.ANY)] * (2 + len(after)),
        out_specs=[pl.BlockSpec(memory_space=pl.ANY)] * 4,
        out_shape=out_shape,
        scratch_shapes=[
            pltpu.VMEM((folds, 2, rows, LANES), covariates.dtype),
            pltpu.VMEM((folds, rows, LANES), covariates.dtype),
            pltpu.SemaphoreType.DMA((folds, 2)),
            pltpu.SemaphoreType.DMA((moves,)),
        ],
        compiler_params=pltpu.CompilerParams(vmem_limit_bytes=VMEM_BYTES),
        cost_estimate=pl.CostEstimate(
            flops=0, bytes_accessed=2 * covariates.size, transcendentals=0
        ),
        name="pack",
    )(covariates, mine, *after)


def onehot_of(pick_ref, weightings, dtype):
    index = lax.broadcasted_iota(jnp.int32, (pick_ref.shape[0], weightings), 1)
    return jnp.where(index == pick_ref[...], 1.0, 0.0).astype(dtype)


def arm_columns(tail_ref, onehot):
    comps, weightings = onehot.shape
    height, width = tail_ref.shape
    pieces = [tail_ref[:, lane:lane + LANES] for lane in range(0, width, LANES)]
    panel = jnp.concatenate(pieces[:(weightings + comps) // height], axis=0)
    weights = panel[0:weightings]
    arms = panel[weightings:weightings + comps].astype(jnp.float32)
    picked = jnp.dot(onehot, weights, preferred_element_type=jnp.float32)
    return weights, picked * arms, picked * (1.0 - arms)


def tail_specs(arrays, height):
    return [
        pl.BlockSpec((height, array.shape[1]), lambda s, at=array.shape[0] // height - 1: (at, 0))
        for array in arrays
    ]


def whole_spec(shape):
    return pl.BlockSpec(shape, lambda s: (0,) * len(shape))


def totals_kernel(weightings, pick_ref, *refs):
    tail_refs, out_ref = refs[:-1], refs[-1]
    onehot = onehot_of(pick_ref, weightings, jnp.bfloat16)
    target_sum, other_sum = 0.0, 0.0
    for ref in tail_refs:
        _, target, other = arm_columns(ref, onehot)
        target_sum += target
        other_sum += other
    lane = lax.broadcasted_iota(jnp.int32, out_ref.shape, 1)
    out_ref[...] = jnp.where(
        lane == 0,
        jnp.sum(target_sum, axis=1, keepdims=True),
        jnp.sum(other_sum, axis=1, keepdims=True),
    )


def group_totals(rows, pick_column, weightings, height):
    comps = pick_column.shape[0]
    return pl.pallas_call(
        functools.partial(totals_kernel, weightings),
        grid=(1,),
        in_specs=[whole_spec(pick_column.shape)] + tail_specs(rows, height),
        out_specs=whole_spec((comps, LANES)),
        out_shape=jax.ShapeDtypeStruct((comps, LANES), jnp.float32),
        cost_estimate=pl.CostEstimate(flops=0, bytes_accessed=1 << 18, transcendentals=0),
        name="totals",
    )(pick_column, *rows)


def panel_kernel(weightings, pick_ref, totals_ref, *refs):
    tail_refs, (first_ref, second_ref, stats_ref) = refs[:-3], refs[-3:]
    comps = pick_ref.shape[0]
    onehot = onehot_of(pick_ref, weightings, jnp.bfloat16)
    totals = totals_ref[...]
    total_target, total_other = totals[:, 0:1], totals[:, 1:2]
    light = jnp.where(total_target <= total_other, 1.0, 0.0)
    stats_ref[0] = jnp.broadcast_to(1.0 / total_target, (comps, LANES))
    stats_ref[1] = jnp.broadcast_to(1.0 / total_other, (comps, LANES))
    stats_ref[2] = jnp.broadcast_to(light, (comps, LANES))
    for place, ref in enumerate(tail_refs):
        weights, target, other = arm_columns(ref, onehot)
        lighter = light * target + (1.0 - light) * other
        here = slice(place * LANES, (place + 1) * LANES)
        first_ref[0:comps, here] = lighter.astype(jnp.bfloat16)
        first_ref[comps:comps + weightings, here] = weights
        second_ref[0:comps, here] = target.astype(jnp.bfloat16)
        second_ref[comps:2 * comps, here] = other.astype(jnp.bfloat16)


def make_panels(rows, totals, pick_column, weightings, height):
    comps = pick_column.shape[0]
    shapes = [
        ((comps + weightings, len(rows) * LANES), jnp.bfloat16),
        ((2 * comps, len(rows) * LANES), jnp.bfloat16),
        ((3, comps, LANES), jnp.float32),
    ]
    return pl.pallas_call(
        functools.partial(panel_kernel, weightings),
        grid=(1,),
        in_specs=[whole_spec(pick_column.shape), whole_spec(totals.shape)]
        + tail_specs(rows, height),
        out_specs=[whole_spec(shape) for shape, _ in shapes],
        out_shape=[jax.ShapeDtypeStruct(shape, dtype) for shape, dtype in shapes],
        cost_estimate=pl.CostEstimate(flops=0, bytes_accessed=1 << 19, transcendentals=0),
        name="panels",
    )(pick_column, totals, *rows)


def moments_kernel(rows, x_count, *refs):
    xs = refs[:x_count]
    first_ref, second_ref, stats_ref = refs[x_count:x_count + 3]
    outs = refs[-2:]
    first_rows = first_ref.shape[0]
    comps = second_ref.shape[0] // 2
    inverse_target = stats_ref[0][:, 0:1]
    inverse_other = stats_ref[1][:, 0:1]
    for place, out_ref in enumerate(outs):
        x = jnp.concatenate([ref[place * rows:(place + 1) * rows, :] for ref in xs], axis=0)
        first = jnp.dot(first_ref[...], x, preferred_element_type=jnp.float32)
        squares = (x.astype(jnp.float32) * x.astype(jnp.float32)).astype(jnp.bfloat16)
        second = jnp.dot(second_ref[...], squares, preferred_element_type=jnp.float32)
        out_ref[0, 0:first_rows, :] = first
        out_ref[0, first_rows:first_rows + comps, :] = (
            second[0:comps] * inverse_target + second[comps:2 * comps] * inverse_other
        )


def moments(xs, first, second, stats, places, after):
    rows = first.shape[1] // len(xs)
    width = xs[0].shape[1]
    comps = second.shape[0] // 2
    out_rows = first.shape[0] + comps
    return pl.pallas_call(
        functools.partial(moments_kernel, rows, len(xs)),
        grid=(places // 2,),
        in_specs=[pl.BlockSpec((2 * rows, width), lambda s: (s, 0))] * len(xs)
        + [whole_spec(array.shape) for array in (first, second, stats)]
        + [pl.BlockSpec(memory_space=pl.ANY)] * len(after),
        out_specs=[pl.BlockSpec((1, out_rows, width), lambda s: (s, 0, 0))] * 2,
        out_shape=[jax.ShapeDtypeStruct((places // 2, out_rows, width), jnp.float32)] * 2,
        compiler_params=pltpu.CompilerParams(vmem_limit_bytes=VMEM_BYTES),
        cost_estimate=pl.CostEstimate(
            flops=2 * places * len(xs) * rows * width * (first.shape[0] + second.shape[0]),
            bytes_accessed=places * width * (2 * len(xs) * rows + 4 * out_rows),
            transcendentals=0,
        ),
        name="moments",
    )(*xs, first, second, stats, *after)


def finish_kernel(plan, weightings, pick_ref, stats_ref, *refs):
    out_ref, ring_ref = refs[-2:]
    per_chunk = (len(refs) - 2) // len(plan.chunks)
    comps = pick_ref.shape[0]
    onehot = onehot_of(pick_ref, weightings, jnp.float32)
    inverse_target = stats_ref[0][:, 0:1]
    inverse_other = stats_ref[1][:, 0:1]
    light = stats_ref[2][:, 0:1] > 0.5
    me = lax.axis_index("pat")
    my_side = me & 1
    for chunk in range(len(plan.chunks)):
        arrays = refs[chunk * per_chunk:(chunk + 1) * per_chunk]
        for away in range(2):
            sums = arrays[away][...]
            for more in arrays[2 + away::2]:
                sums += more[...]
            lighter = sums[0:comps]
            both = jnp.dot(
                onehot,
                sums[comps:comps + weightings],
                precision=lax.Precision.HIGHEST,
                preferred_element_type=jnp.float32,
            )
            spread = sums[comps + weightings:2 * comps + weightings]
            heavier = both - lighter
            mean_target = jnp.where(light, lighter, heavier) * inverse_target
            mean_other = jnp.where(light, heavier, lighter) * inverse_other
            variance = spread - mean_target * mean_target - mean_other * mean_other
            pooled = jnp.maximum(variance / 2.0, 0.01)
            balance = (mean_target - mean_other) / jnp.sqrt(pooled)
            for side in range(2):
                places = plan.ring(side, chunk)
                if places:
                    lanes = slice(places[0] * LANES, places[-1] * LANES + LANES)

                    @pl.when(my_side ^ away == side)
                    def _():
                        ring_ref[:, lanes] = balance[:, 0:len(places) * LANES]
    width = plan.tiles * LANES
    shift = width - lax.rem(me * plan.block, LANES)
    out_ref[:, 0, :] = pltpu.roll(ring_ref[...], shift, 1)[:, 0:plan.block]


def finish(plan, parts, pick_column, stats, weightings):
    comps = pick_column.shape[0]
    operands = [array for part in parts for array in part]
    return pl.pallas_call(
        functools.partial(finish_kernel, plan, weightings),
        in_specs=[pl.BlockSpec(memory_space=pltpu.VMEM)] * (2 + len(operands)),
        out_specs=pl.BlockSpec(memory_space=pltpu.VMEM),
        out_shape=jax.ShapeDtypeStruct((comps, 1, plan.block), jnp.float32),
        scratch_shapes=[pltpu.VMEM((comps, plan.tiles * LANES), jnp.float32)],
        compiler_params=pltpu.CompilerParams(vmem_limit_bytes=VMEM_BYTES),
        cost_estimate=pl.CostEstimate(
            flops=20 * comps * plan.block,
            bytes_accessed=4 * sum(operand.size for operand in operands),
            transcendentals=comps * plan.block,
        ),
        name="finish",
    )(pick_column, stats, *operands)


def swap(array, pairs):
    return lax.ppermute(array, "pat", pairs)


def on_device(n, covs, covariates, weights, arms, pick):
    weightings = weights.shape[1]
    pick_column = pick.reshape(pick.shape[0], 1)
    plan = Plan(n, covariates.shape[1] // n)
    to_other_side = plan.by_mask(1)

    arm_rows = arms.T.astype(weights.dtype)
    if covs > 1:
        arm_rows = lax.all_gather(arm_rows, "cov", axis=0, tiled=True)
    mine = jnp.concatenate([weights.T, arm_rows], axis=0)

    rows, after = [], []
    for chunk in range(len(plan.chunks)):
        kept, sent, other_kept, other_sent = pack(covariates, mine, plan, chunk, after)
        passed = swap(other_sent, to_other_side)
        arrived = swap(sent, plan.by_rows())
        rows.append([kept, swap(other_kept, to_other_side), arrived, swap(passed, plan.by_rows())])
        if chunk == 0:
            tails = [sent, passed] + rows[0][2:]
        after = [passed]

    height = plan.panel_rows(mine.shape[0])
    totals = group_totals(tails, pick_column, weightings, height)
    totals += swap(totals, plan.by_sums())
    for bit in plan.high_bits:
        totals += swap(totals, plan.by_mask(1 << bit))
    first, second, stats = make_panels(tails, totals, pick_column, weightings, height)

    parts, after = [], []
    for chunk in range(len(plan.chunks)):
        kept, sent = moments(rows[chunk], first, second, stats, n // 2, after)
        after = [kept]
        arrived = swap(sent, plan.by_sums())
        for bit in plan.high_bits[:-1]:
            sent = kept[1::2] + arrived[1::2]
            kept = kept[0::2] + arrived[0::2]
            arrived = swap(sent, plan.by_mask(1 << bit))
        part = []
        for bit in plan.high_bits[-1:]:
            last = plan.by_mask(1 << bit)
            last_other = plan.by_mask((1 << bit) | 1)
            part = [
                swap(kept[1] + arrived[1], last),
                swap(kept[3] + arrived[3], last_other),
            ]
            kept, arrived = kept[0::2], arrived[0::2]
        part = [kept[0] + arrived[0], swap(kept[1] + arrived[1], to_other_side)] + part
        parts.append(part)
    return finish(plan, parts, pick_column, stats, weightings)


def solution(mesh):
    placed = (
        P(("groups", "pat"), "cov"),
        P(("groups", "pat"), None),
        P(("groups", "pat"), "cov"),
        P(),
    )
    body = functools.partial(on_device, mesh.shape["pat"], mesh.shape["cov"])
    return jax.shard_map(
        body, mesh=mesh, in_specs=placed, out_specs=P("groups", "cov", "pat"), check_vma=False
    )
```

```python
import functools

import jax
import jax.numpy as jnp
from jax import lax
from jax.experimental import pallas as pl
from jax.experimental.pallas import tpu as pltpu
from jax.sharding import PartitionSpec as P

LANES = 128


def round_up(value, multiple):
    return -(-value // multiple) * multiple


def pick_bits(value, bits):
    result = 0
    for place, bit in enumerate(bits):
        result = result + ((value >> bit) & 1) * (1 << place)
    return result


def spread_bits(value, bits):
    result = 0
    for place, bit in enumerate(bits):
        result += ((value >> place) & 1) << bit
    return result


class Plan:
    def __init__(self, n, block):
        self.n = n
        self.block = block
        self.tiles = round_up(block, LANES) // LANES
        self.share = (self.tiles + 1) // 2
        self.high_bits = list(range(3, n.bit_length() - 1))
        first = (3 * self.share + 4) // 5
        self.chunks = [(0, first)]
        if self.share > first:
            self.chunks.append((first, self.share - first))

    def width(self, chunk):
        return self.chunks[chunk][1] * LANES

    def ring(self, side, chunk):
        start, count = self.chunks[chunk]
        low = side * self.share + start
        return range(low, min(low + count, self.tiles if side else self.share))

    def folded(self, owner):
        first = owner * self.block // LANES
        return (owner * self.block + self.block - 1) // LANES - first == self.tiles

    def place_bits(self, side):
        return [2 - side] + self.high_bits + [0]

    def by_rows(self):
        return [(d, d ^ (2 + 2 * (d & 1))) for d in range(self.n)]

    def by_sums(self):
        return [(d, d ^ (4 - 2 * (d & 1))) for d in range(self.n)]

    def by_mask(self, mask):
        return [(d, d ^ mask) for d in range(self.n)]


def pack_kernel(plan, group, x_ref, *refs):
    count = len(plan.chunks)
    outs, buffers, sems = refs[:4 * count], refs[4 * count:5 * count], refs[-1]
    step = pl.program_id(0)
    me = lax.axis_index("pat")
    rows = x_ref.shape[0]
    for i in range(group):
        first = i * plan.block // LANES
        edge = i * plan.block % LANES
        owner = step * group + i
        for chunk, buffer in enumerate(buffers):
            for side in range(2):
                places = plan.ring(side, chunk)
                for slot, place in enumerate(places):
                    here = slice(slot * LANES, (slot + 1) * LANES)
                    tile = slice((first + place) * LANES, (first + place + 1) * LANES)
                    if place == 0 and plan.folded(i):
                        last = slice((first + plan.tiles) * LANES, (first + plan.tiles + 1) * LANES)
                        lane = lax.broadcasted_iota(jnp.int32, (rows, LANES), 1)
                        head = x_ref[:, tile].astype(jnp.float32)
                        tail = x_ref[:, last].astype(jnp.float32)
                        buffer[side, owner, :, here] = jnp.where(lane >= edge, head, tail).astype(
                            buffer.dtype
                        )
                    else:
                        buffer[side, owner, :, here] = x_ref[:, tile]
                for slot in range(len(places), plan.chunks[chunk][1]):
                    here = slice(slot * LANES, (slot + 1) * LANES)
                    buffer[side, owner, :, here] = jnp.zeros((rows, LANES), buffer.dtype)
                away = (me & 1) ^ side
                relative = owner ^ me ^ away
                target = 2 * away + ((relative >> (1 + side)) & 1)
                place = pick_bits(relative, plan.place_bits(side))
                for t in range(4):

                    @pl.when(target == t)
                    def _():
                        pltpu.make_async_copy(
                            buffer.at[side, owner],
                            outs[4 * chunk + t].at[pl.ds(pl.multiple_of(place * rows, rows), rows)],
                            sems.at[chunk, side, owner],
                        ).start()

    @pl.when(step == pl.num_programs(0) - 1)
    def _():
        for chunk, buffer in enumerate(buffers):
            for side in range(2):
                for owner in range(plan.n):
                    pltpu.make_async_copy(
                        buffer.at[side, owner],
                        outs[4 * chunk].at[pl.ds(0, rows)],
                        sems.at[chunk, side, owner],
                    ).wait()


def pack(covariates, plan):
    rows = covariates.shape[0]
    group = 4
    while group < plan.n and (group * plan.block) % LANES:
        group *= 2
    chunks = range(len(plan.chunks))
    outs = pl.pallas_call(
        functools.partial(pack_kernel, plan, group),
        grid=(plan.n // group,),
        in_specs=[pl.BlockSpec((rows, group * plan.block), lambda s: (0, s))],
        out_specs=[pl.BlockSpec(memory_space=pl.ANY)] * (4 * len(plan.chunks)),
        out_shape=[
            jax.ShapeDtypeStruct((plan.n // 2 * rows, plan.width(chunk)), covariates.dtype)
            for chunk in chunks
            for _ in range(4)
        ],
        scratch_shapes=[
            pltpu.VMEM((2, plan.n, rows, plan.width(chunk)), covariates.dtype) for chunk in chunks
        ]
        + [pltpu.SemaphoreType.DMA((len(plan.chunks), 2, plan.n))],
        compiler_params=pltpu.CompilerParams(vmem_limit_bytes=12 << 20),
        cost_estimate=pl.CostEstimate(
            flops=0, bytes_accessed=4 * covariates.size, transcendentals=0
        ),
        name="pack",
    )(covariates)
    return [outs[4 * chunk:4 * chunk + 4] for chunk in chunks]


def onehot_of(pick_ref, weightings, dtype):
    index = lax.broadcasted_iota(jnp.int32, (pick_ref.shape[0], weightings), 1)
    return jnp.where(index == pick_ref[...], 1.0, 0.0).astype(dtype)


def arm_columns(panel_ref, onehot):
    comps, weightings = onehot.shape
    weights = panel_ref[0:weightings, :]
    arms = panel_ref[weightings:weightings + comps, :].astype(jnp.float32)
    picked = jnp.dot(onehot, weights, preferred_element_type=jnp.float32)
    return weights, picked * arms, picked * (1.0 - arms)


def small_call(kernel, shapes, operands, after, name):
    vmem = pl.BlockSpec(memory_space=pltpu.VMEM)
    return pl.pallas_call(
        kernel,
        in_specs=[vmem] * len(operands) + [pl.BlockSpec(memory_space=pl.ANY)] * len(after),
        out_specs=[vmem] * len(shapes),
        out_shape=[jax.ShapeDtypeStruct(shape, dtype) for shape, dtype in shapes],
        compiler_params=pltpu.CompilerParams(vmem_limit_bytes=4 << 20),
        cost_estimate=pl.CostEstimate(flops=0, bytes_accessed=1 << 18, transcendentals=0),
        name=name,
    )(*operands, *after)


def totals_kernel(weightings, count, pick_ref, *refs):
    out_ref = refs[-1]
    onehot = onehot_of(pick_ref, weightings, jnp.bfloat16)
    target_sum, other_sum = 0.0, 0.0
    for ref in refs[:count]:
        _, target, other = arm_columns(ref, onehot)
        target_sum += target
        other_sum += other
    lane = lax.broadcasted_iota(jnp.int32, out_ref.shape, 1)
    out_ref[...] = jnp.where(
        lane == 0,
        jnp.sum(target_sum, axis=1, keepdims=True),
        jnp.sum(other_sum, axis=1, keepdims=True),
    )


def group_totals(members, pick_column, weightings, after):
    return small_call(
        functools.partial(totals_kernel, weightings, len(members)),
        [((pick_column.shape[0], LANES), jnp.float32)],
        [pick_column, *members],
        after,
        "totals",
    )[0]


def panel_kernel(weightings, pick_ref, near_ref, far_ref, *refs):
    member_refs, (first_ref, second_ref, stats_ref) = refs[:-3], refs[-3:]
    comps = pick_ref.shape[0]
    onehot = onehot_of(pick_ref, weightings, jnp.bfloat16)
    totals = near_ref[...] + far_ref[...]
    total_target, total_other = totals[:, 0:1], totals[:, 1:2]
    light = jnp.where(total_target <= total_other, 1.0, 0.0)
    stats_ref[0] = jnp.broadcast_to(1.0 / total_target, (comps, LANES))
    stats_ref[1] = jnp.broadcast_to(1.0 / total_other, (comps, LANES))
    stats_ref[2] = jnp.broadcast_to(light, (comps, LANES))
    for place, ref in enumerate(member_refs):
        weights, target, other = arm_columns(ref, onehot)
        lighter = light * target + (1.0 - light) * other
        here = slice(place * LANES, (place + 1) * LANES)
        first_ref[0:comps, here] = lighter.astype(jnp.bfloat16)
        first_ref[comps:comps + weightings, here] = weights
        second_ref[0:comps, here] = target.astype(jnp.bfloat16)
        second_ref[comps:2 * comps, here] = other.astype(jnp.bfloat16)


def make_panels(members, near, far, pick_column, weightings):
    comps = pick_column.shape[0]
    return small_call(
        functools.partial(panel_kernel, weightings),
        [
            ((comps + weightings, len(members) * LANES), jnp.bfloat16),
            ((2 * comps, len(members) * LANES), jnp.bfloat16),
            ((3, comps, LANES), jnp.float32),
        ],
        [pick_column, near, far, *members],
        [],
        "panels",
    )


def whole_spec(shape):
    return pl.BlockSpec(shape, lambda s: (0,) * len(shape))


def moments_kernel(rows, x_count, *refs):
    xs = refs[:x_count]
    first_ref, second_ref, stats_ref = refs[x_count:x_count + 3]
    outs = refs[-2:]
    first_rows = first_ref.shape[0]
    comps = second_ref.shape[0] // 2
    inverse_target = stats_ref[0][:, 0:1]
    inverse_other = stats_ref[1][:, 0:1]
    for place, out_ref in enumerate(outs):
        x = jnp.concatenate([ref[place * rows:(place + 1) * rows, :] for ref in xs], axis=0)
        first = jnp.dot(first_ref[...], x, preferred_element_type=jnp.float32)
        squares = (x.astype(jnp.float32) * x.astype(jnp.float32)).astype(jnp.bfloat16)
        second = jnp.dot(second_ref[...], squares, preferred_element_type=jnp.float32)
        out_ref[0, 0:first_rows, :] = first
        out_ref[0, first_rows:first_rows + comps, :] = (
            second[0:comps] * inverse_target + second[comps:2 * comps] * inverse_other
        )


def moments(xs, first, second, stats, places, after):
    rows = first.shape[1] // len(xs)
    width = xs[0].shape[1]
    comps = second.shape[0] // 2
    out_rows = first.shape[0] + comps
    return pl.pallas_call(
        functools.partial(moments_kernel, rows, len(xs)),
        grid=(places // 2,),
        in_specs=[pl.BlockSpec((2 * rows, width), lambda s: (s, 0))] * len(xs)
        + [whole_spec(array.shape) for array in (first, second, stats)]
        + [pl.BlockSpec(memory_space=pl.ANY)] * len(after),
        out_specs=[pl.BlockSpec((1, out_rows, width), lambda s: (s, 0, 0))] * 2,
        out_shape=[jax.ShapeDtypeStruct((places // 2, out_rows, width), jnp.float32)] * 2,
        compiler_params=pltpu.CompilerParams(vmem_limit_bytes=12 << 20),
        cost_estimate=pl.CostEstimate(
            flops=2 * places * len(xs) * rows * width * (first.shape[0] + second.shape[0]),
            bytes_accessed=places * width * (2 * len(xs) * rows + 4 * out_rows),
            transcendentals=0,
        ),
        name="moments",
    )(*xs, first, second, stats, *after)


def finish_kernel(plan, weightings, pick_ref, stats_ref, *refs):
    out_ref, ring_ref = refs[-2:]
    per_chunk = (len(refs) - 2) // len(plan.chunks)
    comps = pick_ref.shape[0]
    onehot = onehot_of(pick_ref, weightings, jnp.float32)
    inverse_target = stats_ref[0][:, 0:1]
    inverse_other = stats_ref[1][:, 0:1]
    light = stats_ref[2][:, 0:1] > 0.5
    me = lax.axis_index("pat")
    my_side = me & 1
    for chunk in range(len(plan.chunks)):
        arrays = refs[chunk * per_chunk:(chunk + 1) * per_chunk]
        for away in range(2):
            sums = arrays[away][...]
            for more in arrays[2 + away::2]:
                sums += more[...]
            lighter = sums[0:comps]
            both = jnp.dot(
                onehot,
                sums[comps:comps + weightings],
                precision=lax.Precision.HIGHEST,
                preferred_element_type=jnp.float32,
            )
            spread = sums[comps + weightings:2 * comps + weightings]
            heavier = both - lighter
            mean_target = jnp.where(light, lighter, heavier) * inverse_target
            mean_other = jnp.where(light, heavier, lighter) * inverse_other
            variance = spread - mean_target * mean_target - mean_other * mean_other
            pooled = jnp.maximum(variance / 2.0, 0.01)
            balance = (mean_target - mean_other) / jnp.sqrt(pooled)
            for side in range(2):
                places = plan.ring(side, chunk)
                if places:
                    lanes = slice(places[0] * LANES, places[-1] * LANES + LANES)

                    @pl.when(my_side ^ away == side)
                    def _():
                        ring_ref[:, lanes] = balance[:, 0:len(places) * LANES]
    width = plan.tiles * LANES
    shift = width - lax.rem(me * plan.block, LANES)
    out_ref[:, 0, :] = pltpu.roll(ring_ref[...], shift, 1)[:, 0:plan.block]


def finish(plan, parts, pick_column, stats, weightings):
    comps = pick_column.shape[0]
    operands = [array for part in parts for array in part]
    return pl.pallas_call(
        functools.partial(finish_kernel, plan, weightings),
        in_specs=[pl.BlockSpec(memory_space=pltpu.VMEM)] * (2 + len(operands)),
        out_specs=pl.BlockSpec(memory_space=pltpu.VMEM),
        out_shape=jax.ShapeDtypeStruct((comps, 1, plan.block), jnp.float32),
        scratch_shapes=[pltpu.VMEM((comps, plan.tiles * LANES), jnp.float32)],
        compiler_params=pltpu.CompilerParams(vmem_limit_bytes=12 << 20),
        cost_estimate=pl.CostEstimate(
            flops=20 * comps * plan.block,
            bytes_accessed=4 * sum(operand.size for operand in operands),
            transcendentals=comps * plan.block,
        ),
        name="finish",
    )(pick_column, stats, *operands)


def swap(array, pairs):
    return lax.ppermute(array, "pat", pairs)


def on_device(n, covs, covariates, weights, arms, pick):
    weightings = weights.shape[1]
    pick_column = pick.reshape(pick.shape[0], 1)
    plan = Plan(n, covariates.shape[1] // n)
    to_other_side = plan.by_mask(1)

    arm_rows = arms.T.astype(weights.dtype)
    if covs > 1:
        arm_rows = lax.all_gather(arm_rows, "cov", axis=0, tiled=True)
    mine = jnp.concatenate([weights.T, arm_rows], axis=0)
    across = [(pair ^ 1, d) for d, pair in plan.by_rows()]
    members = [mine] + [swap(mine, pairs) for pairs in (to_other_side, plan.by_rows(), across)]

    rows = []
    for kept, sent, other_kept, other_sent in pack(covariates, plan):
        passed = swap(other_sent, to_other_side)
        arrived = swap(sent, plan.by_rows())
        rows.append([kept, swap(other_kept, to_other_side), arrived, swap(passed, plan.by_rows())])

    near = group_totals(members, pick_column, weightings, [rows[0][2]])
    far = swap(near, plan.by_sums())
    for bit in plan.high_bits:
        near = near + far
        far = swap(near, plan.by_mask(1 << bit))
    first, second, stats = make_panels(members, near, far, pick_column, weightings)

    parts, after = [], []
    for chunk in range(len(plan.chunks)):
        kept, sent = moments(rows[chunk], first, second, stats, n // 2, after)
        after = [kept]
        arrived = swap(sent, plan.by_sums())
        for bit in plan.high_bits[:-1]:
            sent = kept[1::2] + arrived[1::2]
            kept = kept[0::2] + arrived[0::2]
            arrived = swap(sent, plan.by_mask(1 << bit))
        part = []
        for bit in plan.high_bits[-1:]:
            last = plan.by_mask(1 << bit)
            last_other = plan.by_mask((1 << bit) | 1)
            part = [
                swap(kept[1] + arrived[1], last),
                swap(kept[3] + arrived[3], last_other),
            ]
            kept, arrived = kept[0::2], arrived[0::2]
        part = [kept[0] + arrived[0], swap(kept[1] + arrived[1], to_other_side)] + part
        parts.append(part)
    return finish(plan, parts, pick_column, stats, weightings)


def solution(mesh):
    placed = (
        P(("groups", "pat"), "cov"),
        P(("groups", "pat"), None),
        P(("groups", "pat"), "cov"),
        P(),
    )
    body = functools.partial(on_device, mesh.shape["pat"], mesh.shape["cov"])
    return jax.shard_map(
        body, mesh=mesh, in_specs=placed, out_specs=P("groups", "cov", "pat"), check_vma=False
    )
```

```python
import functools

import jax
import jax.numpy as jnp
from jax import lax
from jax.experimental import pallas as pl
from jax.experimental.pallas import tpu as pltpu
from jax.sharding import PartitionSpec as P

LANES = 128


def round_up(value, multiple):
    return -(-value // multiple) * multiple


class Plan:
    def __init__(self, n, block):
        self.n = n
        self.block = block
        self.tiles = round_up(block, LANES) // LANES
        self.share = (self.tiles + 1) // 2
        self.width = self.share * LANES
        self.places = n // 4
        self.high_bits = list(range(3, n.bit_length() - 1))

    def by_rows(self):
        return [(d, d ^ (2 + 2 * (d & 1))) for d in range(self.n)]

    def by_sums(self):
        return [(d, d ^ (4 - 2 * (d & 1))) for d in range(self.n)]

    def by_mask(self, mask):
        return [(d, d ^ mask) for d in range(self.n)]


def pack_kernel(plan, x_ref, *refs):
    step = pl.program_id(0)
    me = lax.axis_index("pat")
    rows, columns = x_ref.shape
    last_tile = columns // LANES - 1
    lane = lax.broadcasted_iota(jnp.int32, (rows, LANES), 1)

    def tile(index):
        return pl.ds(pl.multiple_of(jnp.minimum(index, last_tile) * LANES, LANES), LANES)

    for away in range(2):
        side = (me & 1) ^ away
        holder = me ^ away
        for sent in range(2):
            for chunk in range(2):
                relative = (
                    chunk
                    | (sent << (1 + side))
                    | ((step & 1) << (2 - side))
                    | ((step >> 1) << 3)
                )
                column = (holder ^ relative) * plan.block
                first = column // LANES
                edge = (column - first * LANES) * (1 - side)
                head = x_ref[:, tile(first + side * plan.share)]
                tail = x_ref[:, tile(first + plan.tiles)]
                folded = jnp.where(lane >= edge, head.astype(jnp.float32), tail.astype(jnp.float32))
                if sent:
                    target = refs[2 + 2 * away + chunk]
                else:
                    target = refs[away].at[chunk]
                target[:, 0:LANES] = folded.astype(x_ref.dtype)
                for slot in range(1, plan.share):
                    here = slice(slot * LANES, (slot + 1) * LANES)
                    target[:, here] = x_ref[:, tile(first + side * plan.share + slot)]


def pack(covariates, plan):
    rows = covariates.shape[0]
    dtype = covariates.dtype
    length = plan.places * rows
    kept = jax.ShapeDtypeStruct((2, length, plan.width), dtype)
    sent = jax.ShapeDtypeStruct((length, plan.width), dtype)
    kept_spec = pl.BlockSpec((2, rows, plan.width), lambda s: (0, s, 0))
    sent_spec = pl.BlockSpec((rows, plan.width), lambda s: (s, 0))
    return pl.pallas_call(
        functools.partial(pack_kernel, plan),
        grid=(plan.places,),
        in_specs=[pl.BlockSpec(memory_space=pltpu.VMEM)],
        out_specs=[kept_spec] * 2 + [sent_spec] * 4,
        out_shape=[kept] * 2 + [sent] * 4,
        compiler_params=pltpu.CompilerParams(vmem_limit_bytes=12 << 20),
        cost_estimate=pl.CostEstimate(flops=0, bytes_accessed=1 << 14, transcendentals=0),
        name="pack",
    )(covariates)


def onehot_of(pick_ref, weightings, dtype):
    index = lax.broadcasted_iota(jnp.int32, (pick_ref.shape[0], weightings), 1)
    return jnp.where(index == pick_ref[...], 1.0, 0.0).astype(dtype)


def arm_columns(panel_ref, onehot):
    comps, weightings = onehot.shape
    weights = panel_ref[0:weightings, :]
    arms = panel_ref[weightings:weightings + comps, :].astype(jnp.float32)
    picked = jnp.dot(onehot, weights, preferred_element_type=jnp.float32)
    return weights, picked * arms, picked * (1.0 - arms)


def small_call(kernel, shapes, operands, after, name):
    vmem = pl.BlockSpec(memory_space=pltpu.VMEM)
    return pl.pallas_call(
        kernel,
        in_specs=[vmem] * len(operands) + [pl.BlockSpec(memory_space=pl.ANY)] * len(after),
        out_specs=[vmem] * len(shapes),
        out_shape=[jax.ShapeDtypeStruct(shape, dtype) for shape, dtype in shapes],
        compiler_params=pltpu.CompilerParams(vmem_limit_bytes=4 << 20),
        cost_estimate=pl.CostEstimate(flops=0, bytes_accessed=1 << 14, transcendentals=0),
        name=name,
    )(*operands, *after)


def totals_kernel(weightings, pick_ref, near_ref, far_ref, *refs):
    out_ref = refs[-1]
    onehot = onehot_of(pick_ref, weightings, jnp.bfloat16)
    target_sum, other_sum = 0.0, 0.0
    for ref in (near_ref.at[0], near_ref.at[1], far_ref.at[0], far_ref.at[1]):
        _, target, other = arm_columns(ref, onehot)
        target_sum += target
        other_sum += other
    lane = lax.broadcasted_iota(jnp.int32, out_ref.shape, 1)
    out_ref[...] = jnp.where(
        lane == 0,
        jnp.sum(target_sum, axis=1, keepdims=True),
        jnp.sum(other_sum, axis=1, keepdims=True),
    )


def group_totals(near, far, pick_column, weightings, after):
    return small_call(
        functools.partial(totals_kernel, weightings),
        [((pick_column.shape[0], LANES), jnp.float32)],
        [pick_column, near, far],
        after,
        "totals",
    )[0]


def panel_kernel(weightings, pick_ref, near_ref, far_ref, here_ref, there_ref, *refs):
    first_ref, second_ref, stats_ref = refs
    comps = pick_ref.shape[0]
    onehot = onehot_of(pick_ref, weightings, jnp.bfloat16)
    totals = here_ref[...] + there_ref[...]
    total_target, total_other = totals[:, 0:1], totals[:, 1:2]
    light = jnp.where(total_target <= total_other, 1.0, 0.0)
    stats_ref[0] = jnp.broadcast_to(1.0 / total_target, (comps, LANES))
    stats_ref[1] = jnp.broadcast_to(1.0 / total_other, (comps, LANES))
    stats_ref[2] = jnp.broadcast_to(light, (comps, LANES))
    members = (near_ref.at[0], near_ref.at[1], far_ref.at[1], far_ref.at[0])
    for place, ref in enumerate(members):
        weights, target, other = arm_columns(ref, onehot)
        lighter = light * target + (1.0 - light) * other
        here = slice(place * LANES, (place + 1) * LANES)
        first_ref[0:comps, here] = lighter.astype(jnp.bfloat16)
        first_ref[comps:comps + weightings, here] = weights
        second_ref[0:comps, here] = target.astype(jnp.bfloat16)
        second_ref[comps:2 * comps, here] = other.astype(jnp.bfloat16)


def make_panels(near, far, totals, others, pick_column, weightings):
    comps = pick_column.shape[0]
    return small_call(
        functools.partial(panel_kernel, weightings),
        [
            ((comps + weightings, 4 * LANES), jnp.bfloat16),
            ((2 * comps, 4 * LANES), jnp.bfloat16),
            ((3, comps, LANES), jnp.float32),
        ],
        [pick_column, near, far, totals, others],
        [],
        "panels",
    )


def whole_spec(shape):
    return pl.BlockSpec(shape, lambda s: (0,) * len(shape))


def moments_kernel(rows, *refs):
    xs, (first_ref, second_ref, stats_ref), outs = refs[:4], refs[4:7], refs[-2:]
    first_rows = first_ref.shape[0]
    comps = second_ref.shape[0] // 2
    inverse_target = stats_ref[0][:, 0:1]
    inverse_other = stats_ref[1][:, 0:1]
    for place, out_ref in enumerate(outs):
        here = slice(place * rows, (place + 1) * rows)
        x = jnp.concatenate([ref[here, :] for ref in xs], axis=0)
        first = jnp.dot(first_ref[...], x, preferred_element_type=jnp.float32)
        squares = (x.astype(jnp.float32) * x.astype(jnp.float32)).astype(jnp.bfloat16)
        second = jnp.dot(second_ref[...], squares, preferred_element_type=jnp.float32)
        out_ref[0, 0:first_rows, :] = first
        out_ref[0, first_rows:first_rows + comps, :] = (
            second[0:comps] * inverse_target + second[comps:2 * comps] * inverse_other
        )


def moments(plan, chunk, kept, swapped, first, second, stats, after):
    rows = first.shape[1] // 4
    out_rows = first.shape[0] + second.shape[0] // 2
    out = (plan.places // 2, out_rows, plan.width)
    return pl.pallas_call(
        functools.partial(moments_kernel, rows),
        grid=(plan.places // 2,),
        in_specs=[pl.BlockSpec((None, 2 * rows, plan.width), lambda s: (chunk, s, 0))] * 2
        + [pl.BlockSpec((2 * rows, plan.width), lambda s: (s, 0))] * 2
        + [whole_spec(array.shape) for array in (first, second, stats)]
        + [pl.BlockSpec(memory_space=pl.ANY)] * len(after),
        out_specs=[pl.BlockSpec((1, out_rows, plan.width), lambda s: (s, 0, 0))] * 2,
        out_shape=[jax.ShapeDtypeStruct(out, jnp.float32)] * 2,
        compiler_params=pltpu.CompilerParams(vmem_limit_bytes=16 << 20),
        cost_estimate=pl.CostEstimate(flops=0, bytes_accessed=1 << 14, transcendentals=0),
        name="moments",
    )(*kept, *swapped, first, second, stats, *after)


def finish_kernel(plan, weightings, counts, pick_ref, stats_ref, *refs):
    out_ref, ring_ref = refs[-2:]
    comps = pick_ref.shape[0]
    onehot = onehot_of(pick_ref, weightings, jnp.float32)
    inverse_target = stats_ref[0][:, 0:1]
    inverse_other = stats_ref[1][:, 0:1]
    light = stats_ref[2][:, 0:1] > 0.5
    me = lax.axis_index("pat")
    for away, count in enumerate(counts):
        sums = refs[0][...]
        for more in refs[1:count]:
            sums += more[...]
        refs = refs[count:]
        lighter = sums[0:comps]
        both = jnp.dot(
            onehot,
            sums[comps:comps + weightings],
            precision=lax.Precision.HIGHEST,
            preferred_element_type=jnp.float32,
        )
        spread = sums[comps + weightings:2 * comps + weightings]
        heavier = both - lighter
        mean_target = jnp.where(light, lighter, heavier) * inverse_target
        mean_other = jnp.where(light, heavier, lighter) * inverse_other
        variance = spread - mean_target * mean_target - mean_other * mean_other
        pooled = jnp.maximum(variance / 2.0, 0.01)
        balance = (mean_target - mean_other) / jnp.sqrt(pooled)
        for side in range(2):
            count = plan.tiles - plan.share if side else plan.share
            if count:
                lanes = slice(side * plan.width, side * plan.width + count * LANES)

                @pl.when((me & 1) ^ away == side)
                def _():
                    ring_ref[:, lanes] = balance[:, 0:count * LANES]
    width = plan.tiles * LANES
    shift = width - lax.rem(me * plan.block, LANES)
    out_ref[:, 0, :] = pltpu.roll(ring_ref[...], shift, 1)[:, 0:plan.block]


def finish(plan, parts, pick_column, stats, weightings):
    comps = pick_column.shape[0]
    operands = [array for part in parts for array in part]
    return pl.pallas_call(
        functools.partial(finish_kernel, plan, weightings, [len(part) for part in parts]),
        in_specs=[pl.BlockSpec(memory_space=pltpu.VMEM)] * (2 + len(operands)),
        out_specs=pl.BlockSpec(memory_space=pltpu.VMEM),
        out_shape=jax.ShapeDtypeStruct((comps, 1, plan.block), jnp.float32),
        scratch_shapes=[pltpu.VMEM((comps, plan.tiles * LANES), jnp.float32)],
        compiler_params=pltpu.CompilerParams(vmem_limit_bytes=12 << 20),
        cost_estimate=pl.CostEstimate(flops=0, bytes_accessed=1 << 14, transcendentals=0),
        name="finish",
    )(pick_column, stats, *operands)


def swap(array, pairs):
    return lax.ppermute(array, "pat", pairs)


def on_device(n, covs, covariates, weights, arms, pick):
    weightings = weights.shape[1]
    pick_column = pick.reshape(pick.shape[0], 1)
    plan = Plan(n, covariates.shape[1] // n)
    to_other_side = plan.by_mask(1)

    arm_rows = arms.T.astype(weights.dtype)
    if covs > 1:
        arm_rows = lax.all_gather(arm_rows, "cov", axis=0, tiled=True)
    mine = jnp.concatenate([weights.T, arm_rows], axis=0)
    near = jnp.stack([mine, swap(mine, to_other_side)])
    far = swap(near, [(pair ^ 1, d) for d, pair in plan.by_rows()])

    kept, other_kept, sent0, sent1, other_sent0, other_sent1 = pack(covariates, plan)
    swapped = {}
    for chunk, sent, other_sent in ((1, sent1, other_sent1), (0, sent0, other_sent0)):
        passed = swap(other_sent, to_other_side)
        swapped[chunk] = [swap(sent, plan.by_rows()), swap(passed, plan.by_rows())]
    kept = [kept, swap(other_kept, to_other_side)]

    totals = group_totals(near, far, pick_column, weightings, [swapped[1][0]])
    others = swap(totals, plan.by_sums())
    for bit in plan.high_bits:
        totals = totals + others
        others = swap(totals, plan.by_mask(1 << bit))
    first, second, stats = make_panels(near, far, totals, others, pick_column, weightings)

    parts, after = [[], []], []
    for chunk in (1, 0):
        even, odd = moments(plan, chunk, kept, swapped[chunk], first, second, stats, after)
        arrived = swap(odd, plan.by_sums())
        after = [arrived]
        for bit in plan.high_bits[:-1]:
            odd = even[1::2] + arrived[1::2]
            even = even[0::2] + arrived[0::2]
            arrived = swap(odd, plan.by_mask(1 << bit))
        for bit in plan.high_bits[-1:]:
            parts[chunk].append(swap(even[1] + arrived[1], plan.by_mask((1 << bit) | chunk)))
        own = even[0] + arrived[0]
        parts[chunk].append(swap(own, to_other_side) if chunk else own)
    return finish(plan, parts, pick_column, stats, weightings)


def solution(mesh):
    placed = (
        P(("groups", "pat"), "cov"),
        P(("groups", "pat"), None),
        P(("groups", "pat"), "cov"),
        P(),
    )
    body = functools.partial(on_device, mesh.shape["pat"], mesh.shape["cov"])
    return jax.shard_map(
        body, mesh=mesh, in_specs=placed, out_specs=P("groups", "cov", "pat"), check_vma=False
    )
```

```python
import functools

import jax
import jax.numpy as jnp
from jax import lax
from jax.experimental import pallas as pl
from jax.experimental.pallas import tpu as pltpu
from jax.sharding import PartitionSpec as P

LANES = 128


def round_up(value, multiple):
    return -(-value // multiple) * multiple


class Plan:
    def __init__(self, n, block):
        self.n = n
        self.block = block
        self.tiles = round_up(block, LANES) // LANES
        self.share = (self.tiles + 1) // 2
        self.width = self.share * LANES
        self.places = n // 4
        self.high_bits = list(range(3, n.bit_length() - 1))

    def by_rows(self):
        return [(d, d ^ (2 + 2 * (d & 1))) for d in range(self.n)]

    def by_sums(self):
        return [(d, d ^ (4 - 2 * (d & 1))) for d in range(self.n)]

    def by_mask(self, mask):
        return [(d, d ^ mask) for d in range(self.n)]


def pack_kernel(plan, x_ref, *refs):
    step = pl.program_id(0)
    me = lax.axis_index("pat")
    rows, columns = x_ref.shape
    last_tile = columns // LANES - 1
    lane = lax.broadcasted_iota(jnp.int32, (rows, LANES), 1)

    def tile(index):
        return pl.ds(pl.multiple_of(jnp.minimum(index, last_tile) * LANES, LANES), LANES)

    for away in range(2):
        side = (me & 1) ^ away
        holder = me ^ away
        for sent in range(2):
            for chunk in range(2):
                relative = (
                    chunk
                    | (sent << (1 + side))
                    | ((step & 1) << (2 - side))
                    | ((step >> 1) << 3)
                )
                column = (holder ^ relative) * plan.block
                first = column // LANES
                edge = (column - first * LANES) * (1 - side)
                head = x_ref[:, tile(first + side * plan.share)]
                tail = x_ref[:, tile(first + plan.tiles)]
                folded = jnp.where(lane >= edge, head.astype(jnp.float32), tail.astype(jnp.float32))
                if sent:
                    target = refs[2 + 2 * away + chunk]
                else:
                    target = refs[away].at[chunk]
                target[:, 0:LANES] = folded.astype(x_ref.dtype)
                for slot in range(1, plan.share):
                    here = slice(slot * LANES, (slot + 1) * LANES)
                    target[:, here] = x_ref[:, tile(first + side * plan.share + slot)]


def pack(covariates, plan):
    rows = covariates.shape[0]
    dtype = covariates.dtype
    length = plan.places * rows
    kept = jax.ShapeDtypeStruct((2, length, plan.width), dtype)
    sent = jax.ShapeDtypeStruct((length, plan.width), dtype)
    kept_spec = pl.BlockSpec((2, rows, plan.width), lambda s: (0, s, 0))
    sent_spec = pl.BlockSpec((rows, plan.width), lambda s: (s, 0))
    return pl.pallas_call(
        functools.partial(pack_kernel, plan),
        grid=(plan.places,),
        in_specs=[pl.BlockSpec(memory_space=pltpu.VMEM)],
        out_specs=[kept_spec] * 2 + [sent_spec] * 4,
        out_shape=[kept] * 2 + [sent] * 4,
        compiler_params=pltpu.CompilerParams(vmem_limit_bytes=12 << 20),
        cost_estimate=pl.CostEstimate(flops=0, bytes_accessed=1 << 14, transcendentals=0),
        name="pack",
    )(covariates)


def onehot_of(pick_ref, weightings, dtype):
    index = lax.broadcasted_iota(jnp.int32, (pick_ref.shape[0], weightings), 1)
    return jnp.where(index == pick_ref[...], 1.0, 0.0).astype(dtype)


def arm_columns(panel_ref, onehot):
    comps, weightings = onehot.shape
    weights = panel_ref[0:weightings, :]
    arms = panel_ref[weightings:weightings + comps, :].astype(jnp.float32)
    picked = jnp.dot(onehot, weights, preferred_element_type=jnp.float32)
    return weights, picked * arms, picked * (1.0 - arms)


def small_call(kernel, shapes, operands, after, name):
    vmem = pl.BlockSpec(memory_space=pltpu.VMEM)
    return pl.pallas_call(
        kernel,
        in_specs=[vmem] * len(operands) + [pl.BlockSpec(memory_space=pl.ANY)] * len(after),
        out_specs=[vmem] * len(shapes),
        out_shape=[jax.ShapeDtypeStruct(shape, dtype) for shape, dtype in shapes],
        compiler_params=pltpu.CompilerParams(vmem_limit_bytes=4 << 20),
        cost_estimate=pl.CostEstimate(flops=0, bytes_accessed=1 << 14, transcendentals=0),
        name=name,
    )(*operands, *after)


def totals_kernel(weightings, pick_ref, near_ref, far_ref, *refs):
    out_ref = refs[-1]
    onehot = onehot_of(pick_ref, weightings, jnp.bfloat16)
    target_sum, other_sum = 0.0, 0.0
    for ref in (near_ref.at[0], near_ref.at[1], far_ref.at[0], far_ref.at[1]):
        _, target, other = arm_columns(ref, onehot)
        target_sum += target
        other_sum += other
    lane = lax.broadcasted_iota(jnp.int32, out_ref.shape, 1)
    out_ref[...] = jnp.where(
        lane == 0,
        jnp.sum(target_sum, axis=1, keepdims=True),
        jnp.sum(other_sum, axis=1, keepdims=True),
    )


def group_totals(near, far, pick_column, weightings, after):
    return small_call(
        functools.partial(totals_kernel, weightings),
        [((pick_column.shape[0], LANES), jnp.float32)],
        [pick_column, near, far],
        after,
        "totals",
    )[0]


def panel_kernel(weightings, pick_ref, near_ref, far_ref, here_ref, told_ref, *refs):
    first_ref, second_ref, stats_ref = refs
    comps = pick_ref.shape[0]
    onehot = onehot_of(pick_ref, weightings, jnp.bfloat16)
    side = jnp.full(here_ref.shape, lax.axis_index("pat") & 1)
    totals = jnp.where(side == 0, here_ref[...], told_ref[...])
    total_target, total_other = totals[:, 0:1], totals[:, 1:2]
    light = jnp.where(total_target <= total_other, 1.0, 0.0)
    stats_ref[0] = jnp.broadcast_to(1.0 / total_target, (comps, LANES))
    stats_ref[1] = jnp.broadcast_to(1.0 / total_other, (comps, LANES))
    stats_ref[2] = jnp.broadcast_to(light, (comps, LANES))
    members = (near_ref.at[0], near_ref.at[1], far_ref.at[1], far_ref.at[0])
    for place, ref in enumerate(members):
        weights, target, other = arm_columns(ref, onehot)
        lighter = light * target + (1.0 - light) * other
        here = slice(place * LANES, (place + 1) * LANES)
        first_ref[0:comps, here] = lighter.astype(jnp.bfloat16)
        first_ref[comps:comps + weightings, here] = weights
        second_ref[0:comps, here] = target.astype(jnp.bfloat16)
        second_ref[comps:2 * comps, here] = other.astype(jnp.bfloat16)


def make_panels(near, far, totals, told, pick_column, weightings):
    comps = pick_column.shape[0]
    return small_call(
        functools.partial(panel_kernel, weightings),
        [
            ((comps + weightings, 4 * LANES), jnp.bfloat16),
            ((2 * comps, 4 * LANES), jnp.bfloat16),
            ((3, comps, LANES), jnp.float32),
        ],
        [pick_column, near, far, totals, told],
        [],
        "panels",
    )


def whole_spec(shape):
    return pl.BlockSpec(shape, lambda s: (0,) * len(shape))


def moments_kernel(rows, *refs):
    xs, (first_ref, second_ref, stats_ref), outs = refs[:4], refs[4:7], refs[-2:]
    first_rows = first_ref.shape[0]
    comps = second_ref.shape[0] // 2
    inverse_target = stats_ref[0][:, 0:1]
    inverse_other = stats_ref[1][:, 0:1]
    for place, out_ref in enumerate(outs):
        here = slice(place * rows, (place + 1) * rows)
        x = jnp.concatenate([ref[here, :] for ref in xs], axis=0)
        first = jnp.dot(first_ref[...], x, preferred_element_type=jnp.float32)
        squares = (x.astype(jnp.float32) * x.astype(jnp.float32)).astype(jnp.bfloat16)
        second = jnp.dot(second_ref[...], squares, preferred_element_type=jnp.float32)
        out_ref[0, 0:first_rows, :] = first
        out_ref[0, first_rows:first_rows + comps, :] = (
            second[0:comps] * inverse_target + second[comps:2 * comps] * inverse_other
        )


def moments(plan, chunk, kept, swapped, first, second, stats, after):
    rows = first.shape[1] // 4
    out_rows = first.shape[0] + second.shape[0] // 2
    out = (plan.places // 2, out_rows, plan.width)
    return pl.pallas_call(
        functools.partial(moments_kernel, rows),
        grid=(plan.places // 2,),
        in_specs=[pl.BlockSpec((None, 2 * rows, plan.width), lambda s: (chunk, s, 0))] * 2
        + [pl.BlockSpec((2 * rows, plan.width), lambda s: (s, 0))] * 2
        + [whole_spec(array.shape) for array in (first, second, stats)]
        + [pl.BlockSpec(memory_space=pl.ANY)] * len(after),
        out_specs=[pl.BlockSpec((1, out_rows, plan.width), lambda s: (s, 0, 0))] * 2,
        out_shape=[jax.ShapeDtypeStruct(out, jnp.float32)] * 2,
        compiler_params=pltpu.CompilerParams(vmem_limit_bytes=16 << 20),
        cost_estimate=pl.CostEstimate(flops=0, bytes_accessed=1 << 14, transcendentals=0),
        name="moments",
    )(*kept, *swapped, first, second, stats, *after)


def finish_kernel(plan, weightings, counts, pick_ref, stats_ref, *refs):
    out_ref, ring_ref = refs[-2:]
    comps = pick_ref.shape[0]
    onehot = onehot_of(pick_ref, weightings, jnp.float32)
    inverse_target = stats_ref[0][:, 0:1]
    inverse_other = stats_ref[1][:, 0:1]
    light = stats_ref[2][:, 0:1] > 0.5
    me = lax.axis_index("pat")
    for away, count in enumerate(counts):
        sums = refs[0][...]
        for more in refs[1:count]:
            sums += more[...]
        refs = refs[count:]
        lighter = sums[0:comps]
        both = jnp.dot(
            onehot,
            sums[comps:comps + weightings],
            precision=lax.Precision.HIGHEST,
            preferred_element_type=jnp.float32,
        )
        spread = sums[comps + weightings:2 * comps + weightings]
        heavier = both - lighter
        mean_target = jnp.where(light, lighter, heavier) * inverse_target
        mean_other = jnp.where(light, heavier, lighter) * inverse_other
        variance = spread - mean_target * mean_target - mean_other * mean_other
        pooled = jnp.maximum(variance / 2.0, 0.01)
        balance = (mean_target - mean_other) / jnp.sqrt(pooled)
        for side in range(2):
            count = plan.tiles - plan.share if side else plan.share
            if count:
                lanes = slice(side * plan.width, side * plan.width + count * LANES)

                @pl.when((me & 1) ^ away == side)
                def _():
                    ring_ref[:, lanes] = balance[:, 0:count * LANES]
    width = plan.tiles * LANES
    shift = width - lax.rem(me * plan.block, LANES)
    out_ref[:, 0, :] = pltpu.roll(ring_ref[...], shift, 1)[:, 0:plan.block]


def finish(plan, parts, pick_column, stats, weightings):
    comps = pick_column.shape[0]
    operands = [array for part in parts for array in part]
    return pl.pallas_call(
        functools.partial(finish_kernel, plan, weightings, [len(part) for part in parts]),
        in_specs=[pl.BlockSpec(memory_space=pltpu.VMEM)] * (2 + len(operands)),
        out_specs=pl.BlockSpec(memory_space=pltpu.VMEM),
        out_shape=jax.ShapeDtypeStruct((comps, 1, plan.block), jnp.float32),
        scratch_shapes=[pltpu.VMEM((comps, plan.tiles * LANES), jnp.float32)],
        compiler_params=pltpu.CompilerParams(vmem_limit_bytes=12 << 20),
        cost_estimate=pl.CostEstimate(flops=0, bytes_accessed=1 << 14, transcendentals=0),
        name="finish",
    )(pick_column, stats, *operands)


def swap(array, pairs):
    return lax.ppermute(array, "pat", pairs)


def on_device(n, covs, covariates, weights, arms, pick):
    weightings = weights.shape[1]
    pick_column = pick.reshape(pick.shape[0], 1)
    plan = Plan(n, covariates.shape[1] // n)
    to_other_side = plan.by_mask(1)

    arm_rows = arms.T.astype(weights.dtype)
    if covs > 1:
        arm_rows = lax.all_gather(arm_rows, "cov", axis=0, tiled=True)
    mine = jnp.concatenate([weights.T, arm_rows], axis=0)
    near = jnp.stack([mine, swap(mine, to_other_side)])
    far = swap(near, [(pair ^ 1, d) for d, pair in plan.by_rows()])

    kept, other_kept, sent0, sent1, other_sent0, other_sent1 = pack(covariates, plan)
    swapped = {}
    for chunk, sent, other_sent in ((1, sent1, other_sent1), (0, sent0, other_sent0)):
        passed = swap(other_sent, to_other_side)
        swapped[chunk] = [swap(sent, plan.by_rows()), swap(passed, plan.by_rows())]
    kept = [kept, swap(other_kept, to_other_side)]

    totals = group_totals(near, far, pick_column, weightings, [swapped[1][0]])
    totals = totals + swap(totals, plan.by_sums())
    for bit in plan.high_bits:
        totals = totals + swap(totals, plan.by_mask(1 << bit)[0::2])
    told = swap(totals, to_other_side[0::2])
    first, second, stats = make_panels(near, far, totals, told, pick_column, weightings)

    parts, after = [[], []], []
    for chunk in (1, 0):
        even, odd = moments(plan, chunk, kept, swapped[chunk], first, second, stats, after)
        arrived = swap(odd, plan.by_sums())
        after = [arrived]
        for bit in plan.high_bits[:-1]:
            odd = even[1::2] + arrived[1::2]
            even = even[0::2] + arrived[0::2]
            arrived = swap(odd, plan.by_mask(1 << bit))
        for bit in plan.high_bits[-1:]:
            parts[chunk].append(swap(even[1] + arrived[1], plan.by_mask((1 << bit) | chunk)))
        own = even[0] + arrived[0]
        parts[chunk].append(swap(own, to_other_side) if chunk else own)
    return finish(plan, parts, pick_column, stats, weightings)


def solution(mesh):
    placed = (
        P(("groups", "pat"), "cov"),
        P(("groups", "pat"), None),
        P(("groups", "pat"), "cov"),
        P(),
    )
    body = functools.partial(on_device, mesh.shape["pat"], mesh.shape["cov"])
    return jax.shard_map(
        body, mesh=mesh, in_specs=placed, out_specs=P("groups", "cov", "pat"), check_vma=False
    )
```

```python
import functools

import jax
import jax.numpy as jnp
from jax import lax
from jax.experimental import pallas as pl
from jax.experimental.pallas import tpu as pltpu
from jax.sharding import PartitionSpec as P

LANES = 128


def round_up(value, multiple):
    return -(-value // multiple) * multiple


class Plan:
    def __init__(self, n, block):
        self.n = n
        self.block = block
        self.tiles = round_up(block, LANES) // LANES
        self.share = (self.tiles + 1) // 2
        self.width = self.share * LANES
        self.places = n // 4
        *self.middle_bits, self.top_bit = range(3, n.bit_length() - 1)

    def by_rows(self):
        return [(d, d ^ (2 + 2 * (d & 1))) for d in range(self.n)]

    def by_sums(self):
        return [(d, d ^ (4 - 2 * (d & 1))) for d in range(self.n)]

    def by_mask(self, mask):
        return [(d, d ^ mask) for d in range(self.n)]


def pack_kernel(plan, chunk, x_hbm, *refs):
    kept_ref, sent_ref, other_ref, x_ref, sems = refs[-5:]
    step = pl.program_id(0)
    me = lax.axis_index("pat")
    rows, columns = x_ref.shape
    last_tile = columns // LANES - 1
    start = ((me >> plan.top_bit) ^ chunk) * columns
    lane = lax.broadcasted_iota(jnp.int32, (rows, LANES), 1)

    @pl.when(step == 0)
    def _():
        count = sems.shape[0]
        edges = [columns // LANES * piece // count * LANES for piece in range(count + 1)]
        copies = []
        for number in range(count):
            width = edges[number + 1] - edges[number]
            there = pl.ds(pl.multiple_of(start + edges[number], LANES), width)
            copies.append(
                pltpu.make_async_copy(
                    x_hbm.at[:, there], x_ref.at[:, pl.ds(edges[number], width)], sems.at[number]
                )
            )
        for copy in copies:
            copy.start()
        for copy in copies:
            copy.wait()

    def tile(index):
        return pl.ds(pl.multiple_of(jnp.minimum(index, last_tile) * LANES, LANES), LANES)

    middle = len(plan.middle_bits)
    for away in range(2):
        side = (me & 1) ^ away
        holder = me ^ away
        for sent in range(2):
            relative = (
                (step >> (1 + middle))
                | (sent << (1 + side))
                | ((step & 1) << (2 - side))
                | (((step >> 1) & ((1 << middle) - 1)) << 3)
                | (chunk << plan.top_bit)
            )
            column = (holder ^ relative) * plan.block - start
            first = column // LANES
            edge = (column - first * LANES) * (1 - side)
            head = x_ref[:, tile(first + side * plan.share)]
            tail = x_ref[:, tile(first + plan.tiles)]
            folded = jnp.where(lane >= edge, head.astype(jnp.float32), tail.astype(jnp.float32))
            target = other_ref.at[sent] if away else (kept_ref, sent_ref)[sent]
            target[:, 0:LANES] = folded.astype(x_ref.dtype)
            for slot in range(1, plan.share):
                here = slice(slot * LANES, (slot + 1) * LANES)
                target[:, here] = x_ref[:, tile(first + side * plan.share + slot)]


def pack(covariates, plan, chunk, after):
    rows, columns = covariates.shape
    dtype = covariates.dtype
    length = plan.places * rows
    mine = jax.ShapeDtypeStruct((length, plan.width), dtype)
    other = jax.ShapeDtypeStruct((2, length, plan.width), dtype)
    mine_spec = pl.BlockSpec((rows, plan.width), lambda s: (s, 0))
    other_spec = pl.BlockSpec((2, rows, plan.width), lambda s: (0, s, 0))
    return pl.pallas_call(
        functools.partial(pack_kernel, plan, chunk),
        grid=(plan.places,),
        in_specs=[pl.BlockSpec(memory_space=pl.ANY)] * (1 + len(after)),
        out_specs=[mine_spec] * 2 + [other_spec],
        out_shape=[mine] * 2 + [other],
        scratch_shapes=[
            pltpu.VMEM((rows, columns // 2), dtype), pltpu.SemaphoreType.DMA((3,))
        ],
        compiler_params=pltpu.CompilerParams(vmem_limit_bytes=(58 if chunk else 10) << 20),
        cost_estimate=pl.CostEstimate(
            flops=0, bytes_accessed=4 * covariates.size, transcendentals=0
        ),
        name="pack",
    )(covariates, *after)


def onehot_of(pick_ref, weightings, dtype):
    index = lax.broadcasted_iota(jnp.int32, (pick_ref.shape[0], weightings), 1)
    return jnp.where(index == pick_ref[...], 1.0, 0.0).astype(dtype)


def arm_columns(panel_ref, onehot):
    comps, weightings = onehot.shape
    weights = panel_ref[0:weightings, :]
    arms = panel_ref[weightings:weightings + comps, :].astype(jnp.float32)
    picked = jnp.dot(onehot, weights, preferred_element_type=jnp.float32)
    return weights, picked * arms, picked * (1.0 - arms)


def small_call(kernel, shapes, operands, after, name):
    vmem = pl.BlockSpec(memory_space=pltpu.VMEM)
    return pl.pallas_call(
        kernel,
        in_specs=[vmem] * len(operands) + [pl.BlockSpec(memory_space=pl.ANY)] * len(after),
        out_specs=[vmem] * len(shapes),
        out_shape=[jax.ShapeDtypeStruct(shape, dtype) for shape, dtype in shapes],
        compiler_params=pltpu.CompilerParams(vmem_limit_bytes=4 << 20),
        cost_estimate=pl.CostEstimate(flops=0, bytes_accessed=1 << 14, transcendentals=0),
        name=name,
    )(*operands, *after)


def totals_kernel(weightings, pick_ref, near_ref, far_ref, *refs):
    out_ref = refs[-1]
    onehot = onehot_of(pick_ref, weightings, jnp.bfloat16)
    target_sum, other_sum = 0.0, 0.0
    for ref in (near_ref.at[0], near_ref.at[1], far_ref.at[0], far_ref.at[1]):
        _, target, other = arm_columns(ref, onehot)
        target_sum += target
        other_sum += other
    lane = lax.broadcasted_iota(jnp.int32, out_ref.shape, 1)
    out_ref[...] = jnp.where(
        lane == 0,
        jnp.sum(target_sum, axis=1, keepdims=True),
        jnp.sum(other_sum, axis=1, keepdims=True),
    )


def group_totals(near, far, pick_column, weightings, after):
    return small_call(
        functools.partial(totals_kernel, weightings),
        [((pick_column.shape[0], LANES), jnp.float32)],
        [pick_column, near, far],
        after,
        "totals",
    )[0]


def panel_kernel(weightings, pick_ref, near_ref, far_ref, here_ref, told_ref, *refs):
    first_ref, second_ref, stats_ref = refs
    comps = pick_ref.shape[0]
    onehot = onehot_of(pick_ref, weightings, jnp.bfloat16)
    side = jnp.full(here_ref.shape, lax.axis_index("pat") & 1)
    totals = jnp.where(side == 0, here_ref[...], told_ref[...])
    total_target, total_other = totals[:, 0:1], totals[:, 1:2]
    light = jnp.where(total_target <= total_other, 1.0, 0.0)
    stats_ref[0] = jnp.broadcast_to(1.0 / total_target, (comps, LANES))
    stats_ref[1] = jnp.broadcast_to(1.0 / total_other, (comps, LANES))
    stats_ref[2] = jnp.broadcast_to(light, (comps, LANES))
    members = (near_ref.at[0], near_ref.at[1], far_ref.at[1], far_ref.at[0])
    for place, ref in enumerate(members):
        weights, target, other = arm_columns(ref, onehot)
        lighter = light * target + (1.0 - light) * other
        here = slice(place * LANES, (place + 1) * LANES)
        first_ref[0:comps, here] = lighter.astype(jnp.bfloat16)
        first_ref[comps:comps + weightings, here] = weights
        second_ref[0:comps, here] = target.astype(jnp.bfloat16)
        second_ref[comps:2 * comps, here] = other.astype(jnp.bfloat16)


def make_panels(near, far, totals, told, pick_column, weightings):
    comps = pick_column.shape[0]
    return small_call(
        functools.partial(panel_kernel, weightings),
        [
            ((comps + weightings, 4 * LANES), jnp.bfloat16),
            ((2 * comps, 4 * LANES), jnp.bfloat16),
            ((3, comps, LANES), jnp.float32),
        ],
        [pick_column, near, far, totals, told],
        [],
        "panels",
    )


def whole_spec(shape):
    return pl.BlockSpec(shape, lambda s: (0,) * len(shape))


def moments_kernel(rows, split, *refs):
    kept_ref, passed_ref, *swapped_refs, first_ref, second_ref, stats_ref = refs[:7]
    outs = refs[-(2 if split is None else split):]
    first_rows = first_ref.shape[0]
    comps = second_ref.shape[0] // 2
    inverse_target = stats_ref[0][:, 0:1]
    inverse_other = stats_ref[1][:, 0:1]
    for place in range(swapped_refs[0].shape[0] // rows):
        here = slice(place * rows, (place + 1) * rows)
        x = jnp.concatenate(
            [kept_ref[here, :], passed_ref[0, here, :]]
            + [ref[here, :] for ref in swapped_refs],
            axis=0,
        )
        first = jnp.dot(first_ref[...], x, preferred_element_type=jnp.float32)
        squares = (x.astype(jnp.float32) * x.astype(jnp.float32)).astype(jnp.bfloat16)
        second = jnp.dot(second_ref[...], squares, preferred_element_type=jnp.float32)
        out = outs[place % 2].at[place // 2] if split is None else outs[place]
        out[0:first_rows, :] = first
        out[first_rows:first_rows + comps, :] = (
            second[0:comps] * inverse_target + second[comps:2 * comps] * inverse_other
        )


def moments(plan, rows_here, first, second, stats, split, after):
    rows = first.shape[1] // 4
    sums = (first.shape[0] + second.shape[0] // 2, plan.width)
    if split:
        out_shape = [jax.ShapeDtypeStruct(sums, jnp.float32)] * plan.places
    else:
        out_shape = [jax.ShapeDtypeStruct((plan.places // 2,) + sums, jnp.float32)] * 2
    return pl.pallas_call(
        functools.partial(moments_kernel, rows, plan.places if split else None),
        in_specs=[pl.BlockSpec(memory_space=pltpu.VMEM)] * 7
        + [pl.BlockSpec(memory_space=pl.ANY)] * len(after),
        out_specs=[pl.BlockSpec(memory_space=pltpu.VMEM)] * len(out_shape),
        out_shape=out_shape,
        compiler_params=pltpu.CompilerParams(vmem_limit_bytes=20 << 20),
        cost_estimate=pl.CostEstimate(flops=0, bytes_accessed=6 << 20, transcendentals=0),
        name="moments",
    )(*rows_here, first, second, stats, *after)


def finish_kernel(plan, weightings, counts, pick_ref, stats_ref, *refs):
    out_ref, ring_ref = refs[-2:]
    comps = pick_ref.shape[0]
    onehot = onehot_of(pick_ref, weightings, jnp.float32)
    inverse_target = stats_ref[0][:, 0:1]
    inverse_other = stats_ref[1][:, 0:1]
    light = stats_ref[2][:, 0:1] > 0.5
    me = lax.axis_index("pat")
    for away, count in enumerate(counts):
        sums = refs[0][...]
        for more in refs[1:count]:
            sums += more[...]
        refs = refs[count:]
        lighter = sums[0:comps]
        both = jnp.dot(
            onehot,
            sums[comps:comps + weightings],
            precision=lax.Precision.HIGHEST,
            preferred_element_type=jnp.float32,
        )
        spread = sums[comps + weightings:2 * comps + weightings]
        heavier = both - lighter
        mean_target = jnp.where(light, lighter, heavier) * inverse_target
        mean_other = jnp.where(light, heavier, lighter) * inverse_other
        variance = spread - mean_target * mean_target - mean_other * mean_other
        pooled = jnp.maximum(variance / 2.0, 0.01)
        balance = (mean_target - mean_other) / jnp.sqrt(pooled)
        for side in range(2):
            count = plan.tiles - plan.share if side else plan.share
            if count:
                lanes = slice(side * plan.width, side * plan.width + count * LANES)

                @pl.when((me & 1) ^ away == side)
                def _():
                    ring_ref[:, lanes] = balance[:, 0:count * LANES]
    width = plan.tiles * LANES
    shift = width - lax.rem(me * plan.block, LANES)
    out_ref[:, 0, :] = pltpu.roll(ring_ref[...], shift, 1)[:, 0:plan.block]


def finish(plan, parts, pick_column, stats, weightings):
    comps = pick_column.shape[0]
    operands = [array for part in parts for array in part]
    return pl.pallas_call(
        functools.partial(finish_kernel, plan, weightings, [len(part) for part in parts]),
        in_specs=[pl.BlockSpec(memory_space=pltpu.VMEM)] * (2 + len(operands)),
        out_specs=pl.BlockSpec(memory_space=pltpu.VMEM),
        out_shape=jax.ShapeDtypeStruct((comps, 1, plan.block), jnp.float32),
        scratch_shapes=[pltpu.VMEM((comps, plan.tiles * LANES), jnp.float32)],
        compiler_params=pltpu.CompilerParams(vmem_limit_bytes=12 << 20),
        cost_estimate=pl.CostEstimate(flops=0, bytes_accessed=1 << 14, transcendentals=0),
        name="finish",
    )(pick_column, stats, *operands)


def add_kernel(left_ref, right_ref, *refs):
    refs[-1][...] = left_ref[...] + right_ref[...]


def add(left, right, after):
    return small_call(add_kernel, [(left.shape, left.dtype)], [left, right], after, "add")[0]


def swap(array, pairs):
    return lax.ppermute(array, "pat", pairs)


def on_device(n, covs, covariates, weights, arms, pick):
    weightings = weights.shape[1]
    pick_column = pick.reshape(pick.shape[0], 1)
    plan = Plan(n, covariates.shape[1] // n)
    to_other_side = plan.by_mask(1)

    arm_rows = arms.T.astype(weights.dtype)
    if covs > 1:
        arm_rows = lax.all_gather(arm_rows, "cov", axis=0, tiled=True)
    mine = jnp.concatenate([weights.T, arm_rows], axis=0)
    near = jnp.stack([mine, swap(mine, to_other_side)])
    far = swap(near, [(pair ^ 1, d) for d, pair in plan.by_rows()])

    rows_here, after = {}, []
    for chunk in (1, 0):
        kept, sent, other = pack(covariates, plan, chunk, after)
        passed = swap(other, to_other_side)
        rows_here[chunk] = [
            kept, passed, swap(sent, plan.by_rows()), swap(passed[1], plan.by_rows())
        ]
        after = [near]

    totals = group_totals(near, far, pick_column, weightings, [passed, rows_here[1][2]])
    totals = totals + swap(totals, plan.by_sums())
    for bit in plan.middle_bits + [plan.top_bit]:
        totals = totals + swap(totals, plan.by_mask(1 << bit)[0::2])
    told = swap(totals, to_other_side[0::2])
    first, second, stats = make_panels(near, far, totals, told, pick_column, weightings)

    even, odd = moments(plan, rows_here[1], first, second, stats, False, [])
    arrived = swap(odd, plan.by_sums())
    for bit in plan.middle_bits:
        odd = even[1::2] + arrived[1::2]
        even = even[0::2] + arrived[0::2]
        arrived = swap(odd, plan.by_mask(1 << bit))
    across = add(even, arrived, [rows_here[0][2]])
    top = swap(across, plan.by_mask(1 << plan.top_bit))

    last = not plan.middle_bits
    sums = moments(plan, rows_here[0], first, second, stats, last, [across])
    if last:
        even, odd = sums[0::2], sums[1::2]
        other_owner = [(d, pair ^ 1) for d, pair in plan.by_sums()]
        parts = [
            [even[0], top[0], swap(odd[0], plan.by_sums())],
            [swap(even[1] + top[1], to_other_side), swap(odd[1], other_owner)],
        ]
    else:
        even, odd = sums
        arrived = swap(odd, plan.by_sums())
        for bit in plan.middle_bits:
            odd = even[1::2] + arrived[1::2]
            even = even[0::2] + arrived[0::2]
            arrived = swap(odd, plan.by_mask(1 << bit))
        total = even + arrived + top
        parts = [[total[0]], [swap(total[1], to_other_side)]]
    return finish(plan, parts, pick_column, stats, weightings)


def solution(mesh):
    placed = (
        P(("groups", "pat"), "cov"),
        P(("groups", "pat"), None),
        P(("groups", "pat"), "cov"),
        P(),
    )
    body = functools.partial(on_device, mesh.shape["pat"], mesh.shape["cov"])
    return jax.shard_map(
        body, mesh=mesh, in_specs=placed, out_specs=P("groups", "cov", "pat"), check_vma=False
    )
```

```python
import functools

import jax
import jax.numpy as jnp
from jax import lax
from jax.experimental import pallas as pl
from jax.experimental.pallas import tpu as pltpu
from jax.sharding import PartitionSpec as P

LANES = 128


def round_up(value, multiple):
    return -(-value // multiple) * multiple


class Plan:
    def __init__(self, n, block):
        self.n = n
        self.block = block
        self.tiles = round_up(block, LANES) // LANES
        self.share = (self.tiles + 1) // 2
        self.width = self.share * LANES
        self.places = n // 4
        *self.middle_bits, self.top_bit = range(3, n.bit_length() - 1)

    def by_rows(self):
        return [(d, d ^ (2 + 2 * (d & 1))) for d in range(self.n)]

    def by_sums(self):
        return [(d, d ^ (4 - 2 * (d & 1))) for d in range(self.n)]

    def by_mask(self, mask):
        return [(d, d ^ mask) for d in range(self.n)]


def pack_kernel(
    plan, x_ref, kept0_ref, kept1_ref, sent0_ref, sent1_ref, other0_ref, other1_ref
):
    step = pl.program_id(0)
    me = lax.axis_index("pat")
    rows, columns = x_ref.shape
    last_tile = columns // LANES - 1
    lane = lax.broadcasted_iota(jnp.int32, (rows, LANES), 1)

    def tile(index):
        return pl.ds(pl.multiple_of(jnp.minimum(index, last_tile) * LANES, LANES), LANES)

    for away in range(2):
        side = (me & 1) ^ away
        holder = me ^ away
        for sent in range(2):
            for chunk in range(2):
                middle = len(plan.middle_bits)
                relative = (
                    (step >> (1 + middle))
                    | (sent << (1 + side))
                    | ((step & 1) << (2 - side))
                    | (((step >> 1) & ((1 << middle) - 1)) << 3)
                    | (chunk << plan.top_bit)
                )
                column = (holder ^ relative) * plan.block
                first = column // LANES
                edge = (column - first * LANES) * (1 - side)
                head = x_ref[:, tile(first + side * plan.share)]
                tail = x_ref[:, tile(first + plan.tiles)]
                folded = jnp.where(lane >= edge, head.astype(jnp.float32), tail.astype(jnp.float32))
                if away:
                    target = (other0_ref, other1_ref)[chunk].at[sent]
                elif sent:
                    target = (sent0_ref, sent1_ref)[chunk]
                else:
                    target = (kept0_ref, kept1_ref)[chunk]
                target[:, 0:LANES] = folded.astype(x_ref.dtype)
                for slot in range(1, plan.share):
                    here = slice(slot * LANES, (slot + 1) * LANES)
                    target[:, here] = x_ref[:, tile(first + side * plan.share + slot)]


def pack(covariates, plan):
    rows = covariates.shape[0]
    dtype = covariates.dtype
    length = plan.places * rows
    mine = jax.ShapeDtypeStruct((length, plan.width), dtype)
    other = jax.ShapeDtypeStruct((2, length, plan.width), dtype)
    mine_spec = pl.BlockSpec((rows, plan.width), lambda s: (s, 0))
    other_spec = pl.BlockSpec((2, rows, plan.width), lambda s: (0, s, 0))
    return pl.pallas_call(
        functools.partial(pack_kernel, plan),
        grid=(plan.places,),
        in_specs=[pl.BlockSpec(memory_space=pltpu.VMEM)],
        out_specs=[mine_spec] * 4 + [other_spec] * 2,
        out_shape=[mine] * 4 + [other] * 2,
        compiler_params=pltpu.CompilerParams(vmem_limit_bytes=12 << 20),
        cost_estimate=pl.CostEstimate(
            flops=0, bytes_accessed=4 * covariates.size, transcendentals=0
        ),
        name="pack",
    )(covariates)


def onehot_of(pick_ref, weightings, dtype):
    index = lax.broadcasted_iota(jnp.int32, (pick_ref.shape[0], weightings), 1)
    return jnp.where(index == pick_ref[...], 1.0, 0.0).astype(dtype)


def arm_columns(panel_ref, onehot):
    comps, weightings = onehot.shape
    weights = panel_ref[0:weightings, :]
    arms = panel_ref[weightings:weightings + comps, :].astype(jnp.float32)
    picked = jnp.dot(onehot, weights, preferred_element_type=jnp.float32)
    return weights, picked * arms, picked * (1.0 - arms)


def small_call(kernel, shapes, operands, after, name):
    vmem = pl.BlockSpec(memory_space=pltpu.VMEM)
    return pl.pallas_call(
        kernel,
        in_specs=[vmem] * len(operands) + [pl.BlockSpec(memory_space=pl.ANY)] * len(after),
        out_specs=[vmem] * len(shapes),
        out_shape=[jax.ShapeDtypeStruct(shape, dtype) for shape, dtype in shapes],
        compiler_params=pltpu.CompilerParams(vmem_limit_bytes=8 << 20),
        cost_estimate=pl.CostEstimate(flops=0, bytes_accessed=1 << 14, transcendentals=0),
        name=name,
    )(*operands, *after)


def lighter_of(totals):
    return jnp.where(totals[:, 0:1] <= totals[:, 1:2], 1.0, 0.0)


def lighter_panel(ref, members, onehot, light):
    comps, weightings = onehot.shape
    columns = []
    for place, member in enumerate(members):
        weights, target, other = arm_columns(member, onehot)
        here = slice(place * LANES, (place + 1) * LANES)
        lighter = light * target + (1.0 - light) * other
        ref[0:comps, here] = lighter.astype(jnp.bfloat16)
        ref[comps:comps + weightings, here] = weights
        columns.append((target, other))
    return columns


def members_of(near_ref, far_ref):
    return (near_ref.at[0], near_ref.at[1], far_ref.at[1], far_ref.at[0])


def group_kernel(weightings, pick_ref, near_ref, far_ref, totals_ref, panel_ref):
    onehot = onehot_of(pick_ref, weightings, jnp.bfloat16)
    target_sum, other_sum = 0.0, 0.0
    for member in members_of(near_ref, far_ref):
        _, target, other = arm_columns(member, onehot)
        target_sum += target
        other_sum += other
    lane = lax.broadcasted_iota(jnp.int32, totals_ref.shape, 1)
    totals = jnp.where(
        lane == 0,
        jnp.sum(target_sum, axis=1, keepdims=True),
        jnp.sum(other_sum, axis=1, keepdims=True),
    )
    totals_ref[...] = totals
    lighter_panel(panel_ref, members_of(near_ref, far_ref), onehot, lighter_of(totals))


def make_group(near, far, pick_column, weightings):
    comps = pick_column.shape[0]
    return small_call(
        functools.partial(group_kernel, weightings),
        [((comps, LANES), jnp.float32), ((comps + weightings, 4 * LANES), jnp.bfloat16)],
        [pick_column, near, far],
        [],
        "group",
    )


def panel_kernel(weightings, pick_ref, near_ref, far_ref, here_ref, told_ref, *refs):
    first_ref, second_ref, stats_ref = refs
    comps = pick_ref.shape[0]
    onehot = onehot_of(pick_ref, weightings, jnp.bfloat16)
    side = jnp.full(here_ref.shape, lax.axis_index("pat") & 1)
    totals = jnp.where(side == 0, here_ref[...], told_ref[...])
    light = lighter_of(totals)
    stats_ref[0] = jnp.broadcast_to(1.0 / totals[:, 0:1], (comps, LANES))
    stats_ref[1] = jnp.broadcast_to(1.0 / totals[:, 1:2], (comps, LANES))
    stats_ref[2] = jnp.broadcast_to(light, (comps, LANES))
    columns = lighter_panel(first_ref, members_of(near_ref, far_ref), onehot, light)
    for place, (target, other) in enumerate(columns):
        here = slice(place * LANES, (place + 1) * LANES)
        second_ref[0:comps, here] = target.astype(jnp.bfloat16)
        second_ref[comps:2 * comps, here] = other.astype(jnp.bfloat16)


def make_panels(near, far, totals, told, pick_column, weightings):
    comps = pick_column.shape[0]
    return small_call(
        functools.partial(panel_kernel, weightings),
        [
            ((comps + weightings, 4 * LANES), jnp.bfloat16),
            ((2 * comps, 4 * LANES), jnp.bfloat16),
            ((3, comps, LANES), jnp.float32),
        ],
        [pick_column, near, far, totals, told],
        [],
        "panels",
    )


def both_arms(sums, onehot, light):
    comps, weightings = onehot.shape
    lighter = sums[0:comps]
    both = jnp.dot(
        onehot,
        sums[comps:comps + weightings],
        precision=lax.Precision.HIGHEST,
        preferred_element_type=jnp.float32,
    )
    target = jnp.where(light, lighter, both - lighter)
    return target, jnp.where(light, both - lighter, lighter)


def meet_kernel(pick_ref, near_ref, far_ref, stats_ref, left_ref, right_ref, *refs):
    out_ref = refs[-1]
    comps = pick_ref.shape[0]
    rows = left_ref.shape[1] // 2
    onehot = onehot_of(pick_ref, rows - comps, jnp.float32)
    light = stats_ref[2][:, 0:1] > 0.5
    for block in range(left_ref.shape[0]):
        arms = []
        for moment in range(2):
            here = slice(moment * rows, (moment + 1) * rows)
            target, other = 0.0, 0.0
            for ref, totals_ref in ((left_ref, near_ref), (right_ref, far_ref)):
                more = both_arms(ref[block, here, :], onehot, lighter_of(totals_ref[...]) > 0.5)
                target, other = target + more[0], other + more[1]
            arms.append((target, other))
        out_ref[block, 0:comps, :] = jnp.where(light, arms[0][0], arms[0][1])
        out_ref[block, comps:rows, :] = (
            left_ref[block, comps:rows, :] + right_ref[block, comps:rows, :]
        )
        out_ref[block, rows:rows + comps, :] = (
            arms[1][0] * stats_ref[0][:, 0:1] + arms[1][1] * stats_ref[1][:, 0:1]
        )


def meet(pick_column, near_totals, far_totals, stats, left, right, after):
    blocks, rows, width = left.shape
    out = (blocks, rows // 2 + pick_column.shape[0], width)
    return small_call(
        meet_kernel,
        [(out, jnp.float32)],
        [pick_column, near_totals, far_totals, stats, left, right],
        after,
        "meet",
    )[0]


def whole_spec(shape):
    return pl.BlockSpec(shape, lambda s: (0,) * len(shape))


def moments_kernel(rows, split, *refs):
    kept_ref, passed_ref, *swapped_refs, first_ref, second_ref, stats_ref = refs[:7]
    outs = refs[-(2 if split is None else split):]
    first_rows = first_ref.shape[0]
    comps = second_ref.shape[0] // 2
    inverse_target = stats_ref[0][:, 0:1]
    inverse_other = stats_ref[1][:, 0:1]
    for place in range(swapped_refs[0].shape[0] // rows):
        here = slice(place * rows, (place + 1) * rows)
        x = jnp.concatenate(
            [kept_ref[here, :], passed_ref[0, here, :]]
            + [ref[here, :] for ref in swapped_refs],
            axis=0,
        )
        first = jnp.dot(first_ref[...], x, preferred_element_type=jnp.float32)
        squares = (x.astype(jnp.float32) * x.astype(jnp.float32)).astype(jnp.bfloat16)
        second = jnp.dot(second_ref[...], squares, preferred_element_type=jnp.float32)
        out = outs[place % 2].at[place // 2] if split is None else outs[place]
        out[0:first_rows, :] = first
        out[first_rows:first_rows + comps, :] = (
            second[0:comps] * inverse_target + second[comps:2 * comps] * inverse_other
        )


def group_moments_kernel(rows, *refs):
    kept_ref, passed_ref, *swapped_refs, panel_ref = refs[:5]
    outs = refs[-2:]
    height = panel_ref.shape[0]
    for place in range(kept_ref.shape[0] // rows):
        here = slice(place * rows, (place + 1) * rows)
        x = jnp.concatenate(
            [kept_ref[here, :], passed_ref[0, here, :]]
            + [ref[here, :] for ref in swapped_refs],
            axis=0,
        )
        squares = (x.astype(jnp.float32) * x.astype(jnp.float32)).astype(jnp.bfloat16)
        out = outs[place % 2].at[place // 2]
        out[0:height, :] = jnp.dot(panel_ref[...], x, preferred_element_type=jnp.float32)
        out[height:2 * height, :] = jnp.dot(
            panel_ref[...], squares, preferred_element_type=jnp.float32
        )


def group_moments(plan, rows_here, panel, after):
    rows = panel.shape[1] // 4
    out = jax.ShapeDtypeStruct(
        (plan.places // 2, 2 * panel.shape[0], plan.width), jnp.float32
    )
    return pl.pallas_call(
        functools.partial(group_moments_kernel, rows),
        in_specs=[pl.BlockSpec(memory_space=pltpu.VMEM)] * 5
        + [pl.BlockSpec(memory_space=pl.ANY)] * len(after),
        out_specs=[pl.BlockSpec(memory_space=pltpu.VMEM)] * 2,
        out_shape=[out] * 2,
        compiler_params=pltpu.CompilerParams(vmem_limit_bytes=20 << 20),
        cost_estimate=pl.CostEstimate(flops=0, bytes_accessed=6 << 20, transcendentals=0),
        name="group_moments",
    )(*rows_here, panel, *after)


def moments(plan, rows_here, first, second, stats, split, after):
    rows = first.shape[1] // 4
    sums = (first.shape[0] + second.shape[0] // 2, plan.width)
    if split:
        out_shape = [jax.ShapeDtypeStruct(sums, jnp.float32)] * plan.places
    else:
        out_shape = [jax.ShapeDtypeStruct((plan.places // 2,) + sums, jnp.float32)] * 2
    return pl.pallas_call(
        functools.partial(moments_kernel, rows, plan.places if split else None),
        in_specs=[pl.BlockSpec(memory_space=pltpu.VMEM)] * 7
        + [pl.BlockSpec(memory_space=pl.ANY)] * len(after),
        out_specs=[pl.BlockSpec(memory_space=pltpu.VMEM)] * len(out_shape),
        out_shape=out_shape,
        compiler_params=pltpu.CompilerParams(vmem_limit_bytes=20 << 20),
        cost_estimate=pl.CostEstimate(flops=0, bytes_accessed=6 << 20, transcendentals=0),
        name="moments",
    )(*rows_here, first, second, stats, *after)


def finish_kernel(plan, weightings, counts, pick_ref, stats_ref, *refs):
    out_ref, ring_ref = refs[-2:]
    comps = pick_ref.shape[0]
    onehot = onehot_of(pick_ref, weightings, jnp.float32)
    inverse_target = stats_ref[0][:, 0:1]
    inverse_other = stats_ref[1][:, 0:1]
    light = stats_ref[2][:, 0:1] > 0.5
    me = lax.axis_index("pat")
    for away, count in enumerate(counts):
        sums = refs[0][...]
        for more in refs[1:count]:
            sums += more[...]
        refs = refs[count:]
        target, other = both_arms(sums, onehot, light)
        spread = sums[comps + weightings:2 * comps + weightings]
        mean_target = target * inverse_target
        mean_other = other * inverse_other
        variance = spread - mean_target * mean_target - mean_other * mean_other
        pooled = jnp.maximum(variance / 2.0, 0.01)
        balance = (mean_target - mean_other) / jnp.sqrt(pooled)
        for side in range(2):
            count = plan.tiles - plan.share if side else plan.share
            if count:
                lanes = slice(side * plan.width, side * plan.width + count * LANES)

                @pl.when((me & 1) ^ away == side)
                def _():
                    ring_ref[:, lanes] = balance[:, 0:count * LANES]
    width = plan.tiles * LANES
    shift = width - lax.rem(me * plan.block, LANES)
    out_ref[:, 0, :] = pltpu.roll(ring_ref[...], shift, 1)[:, 0:plan.block]


def finish(plan, parts, pick_column, stats, weightings):
    comps = pick_column.shape[0]
    operands = [array for part in parts for array in part]
    return pl.pallas_call(
        functools.partial(finish_kernel, plan, weightings, [len(part) for part in parts]),
        in_specs=[pl.BlockSpec(memory_space=pltpu.VMEM)] * (2 + len(operands)),
        out_specs=pl.BlockSpec(memory_space=pltpu.VMEM),
        out_shape=jax.ShapeDtypeStruct((comps, 1, plan.block), jnp.float32),
        scratch_shapes=[pltpu.VMEM((comps, plan.tiles * LANES), jnp.float32)],
        compiler_params=pltpu.CompilerParams(vmem_limit_bytes=12 << 20),
        cost_estimate=pl.CostEstimate(flops=0, bytes_accessed=1 << 14, transcendentals=0),
        name="finish",
    )(pick_column, stats, *operands)


def swap(array, pairs):
    return lax.ppermute(array, "pat", pairs)


def on_device(n, covs, covariates, weights, arms, pick):
    weightings = weights.shape[1]
    pick_column = pick.reshape(pick.shape[0], 1)
    plan = Plan(n, covariates.shape[1] // n)
    to_other_side = plan.by_mask(1)

    arm_rows = arms.T.astype(weights.dtype)
    if covs > 1:
        arm_rows = lax.all_gather(arm_rows, "cov", axis=0, tiled=True)
    mine = jnp.concatenate([weights.T, arm_rows], axis=0)
    near = jnp.stack([mine, swap(mine, to_other_side)])
    far = swap(near, [(pair ^ 1, d) for d, pair in plan.by_rows()])

    kept0, kept1, sent0, sent1, other0, other1 = pack(covariates, plan)
    rows_here = {}
    for chunk, kept, sent, other in ((1, kept1, sent1, other1), (0, kept0, sent0, other0)):
        passed = swap(other, to_other_side)
        rows_here[chunk] = [
            kept, passed, swap(sent, plan.by_rows()), swap(passed[1], plan.by_rows())
        ]

    near_totals, panel = make_group(near, far, pick_column, weightings)
    far_totals = swap(near_totals, plan.by_sums())
    totals = near_totals + far_totals
    for bit in plan.middle_bits + [plan.top_bit]:
        totals = totals + swap(totals, plan.by_mask(1 << bit)[0::2])
    told = swap(totals, to_other_side[0::2])
    first, second, stats = make_panels(near, far, totals, told, pick_column, weightings)

    even, odd = group_moments(plan, rows_here[1], panel, [totals])
    arrived = swap(odd, plan.by_sums())
    across = meet(
        pick_column, near_totals, far_totals, stats, even, arrived, [rows_here[0][2]]
    )
    for bit in plan.middle_bits:
        across = across[0::2] + swap(across[1::2], plan.by_mask(1 << bit))
    top = swap(across, plan.by_mask(1 << plan.top_bit))

    last = not plan.middle_bits
    sums = moments(plan, rows_here[0], first, second, stats, last, [across])
    if last:
        even, odd = sums[0::2], sums[1::2]
        other_owner = [(d, pair ^ 1) for d, pair in plan.by_sums()]
        parts = [
            [even[0], top[0], swap(odd[0], plan.by_sums())],
            [swap(even[1] + top[1], to_other_side), swap(odd[1], other_owner)],
        ]
    else:
        even, odd = sums
        arrived = swap(odd, plan.by_sums())
        for bit in plan.middle_bits:
            odd = even[1::2] + arrived[1::2]
            even = even[0::2] + arrived[0::2]
            arrived = swap(odd, plan.by_mask(1 << bit))
        total = even + arrived + top
        parts = [[total[0]], [swap(total[1], to_other_side)]]
    return finish(plan, parts, pick_column, stats, weightings)


def solution(mesh):
    placed = (
        P(("groups", "pat"), "cov"),
        P(("groups", "pat"), None),
        P(("groups", "pat"), "cov"),
        P(),
    )
    body = functools.partial(on_device, mesh.shape["pat"], mesh.shape["cov"])
    return jax.shard_map(
        body, mesh=mesh, in_specs=placed, out_specs=P("groups", "cov", "pat"), check_vma=False
    )
```

```python
import functools

import jax
import jax.numpy as jnp
from jax import lax
from jax.experimental import pallas as pl
from jax.experimental.pallas import tpu as pltpu
from jax.sharding import PartitionSpec as P

LANES = 128


def round_up(value, multiple):
    return -(-value // multiple) * multiple


class Plan:
    def __init__(self, n, block):
        self.n = n
        self.block = block
        self.tiles = round_up(block, LANES) // LANES
        self.share = (self.tiles + 1) // 2
        self.width = self.share * LANES
        self.places = n // 4
        *self.middle_bits, self.top_bit = range(3, n.bit_length() - 1)

    def by_rows(self):
        return [(d, d ^ (2 + 2 * (d & 1))) for d in range(self.n)]

    def by_sums(self):
        return [(d, d ^ (4 - 2 * (d & 1))) for d in range(self.n)]

    def by_mask(self, mask):
        return [(d, d ^ mask) for d in range(self.n)]


def pack_kernel(
    plan, x_ref, kept0_ref, kept1_ref, sent0_ref, sent1_ref, other0_ref, other1_ref
):
    step = pl.program_id(0)
    me = lax.axis_index("pat")
    rows, columns = x_ref.shape
    last_tile = columns // LANES - 1
    lane = lax.broadcasted_iota(jnp.int32, (rows, LANES), 1)

    def tile(index):
        return pl.ds(pl.multiple_of(jnp.minimum(index, last_tile) * LANES, LANES), LANES)

    for away in range(2):
        side = (me & 1) ^ away
        holder = me ^ away
        for sent in range(2):
            for chunk in range(2):
                middle = len(plan.middle_bits)
                relative = (
                    (step >> (1 + middle))
                    | (sent << (1 + side))
                    | ((step & 1) << (2 - side))
                    | (((step >> 1) & ((1 << middle) - 1)) << 3)
                    | (chunk << plan.top_bit)
                )
                column = (holder ^ relative) * plan.block
                first = column // LANES
                edge = (column - first * LANES) * (1 - side)
                head = x_ref[:, tile(first + side * plan.share)]
                tail = x_ref[:, tile(first + plan.tiles)]
                folded = jnp.where(lane >= edge, head.astype(jnp.float32), tail.astype(jnp.float32))
                if away:
                    target = (other0_ref, other1_ref)[chunk].at[sent]
                elif sent:
                    target = (sent0_ref, sent1_ref)[chunk]
                else:
                    target = (kept0_ref, kept1_ref)[chunk]
                target[:, 0:LANES] = folded.astype(x_ref.dtype)
                for slot in range(1, plan.share):
                    here = slice(slot * LANES, (slot + 1) * LANES)
                    target[:, here] = x_ref[:, tile(first + side * plan.share + slot)]


def pack(covariates, plan):
    rows = covariates.shape[0]
    dtype = covariates.dtype
    length = plan.places * rows
    mine = jax.ShapeDtypeStruct((length, plan.width), dtype)
    other = jax.ShapeDtypeStruct((2, length, plan.width), dtype)
    mine_spec = pl.BlockSpec((rows, plan.width), lambda s: (s, 0))
    other_spec = pl.BlockSpec((2, rows, plan.width), lambda s: (0, s, 0))
    return pl.pallas_call(
        functools.partial(pack_kernel, plan),
        grid=(plan.places,),
        in_specs=[pl.BlockSpec(memory_space=pltpu.VMEM)],
        out_specs=[mine_spec] * 4 + [other_spec] * 2,
        out_shape=[mine] * 4 + [other] * 2,
        compiler_params=pltpu.CompilerParams(vmem_limit_bytes=12 << 20),
        cost_estimate=pl.CostEstimate(
            flops=0, bytes_accessed=4 * covariates.size, transcendentals=0
        ),
        name="pack",
    )(covariates)


def onehot_of(pick_ref, weightings, dtype):
    index = lax.broadcasted_iota(jnp.int32, (pick_ref.shape[0], weightings), 1)
    return jnp.where(index == pick_ref[...], 1.0, 0.0).astype(dtype)


def arm_columns(panel_ref, onehot):
    comps, weightings = onehot.shape
    weights = panel_ref[0:weightings, :]
    arms = panel_ref[weightings:weightings + comps, :].astype(jnp.float32)
    picked = jnp.dot(onehot, weights, preferred_element_type=jnp.float32)
    return weights, picked * arms, picked * (1.0 - arms)


def small_call(kernel, shapes, operands, after, name):
    vmem = pl.BlockSpec(memory_space=pltpu.VMEM)
    return pl.pallas_call(
        kernel,
        in_specs=[vmem] * len(operands) + [pl.BlockSpec(memory_space=pl.ANY)] * len(after),
        out_specs=[vmem] * len(shapes),
        out_shape=[jax.ShapeDtypeStruct(shape, dtype) for shape, dtype in shapes],
        compiler_params=pltpu.CompilerParams(vmem_limit_bytes=8 << 20),
        cost_estimate=pl.CostEstimate(flops=0, bytes_accessed=1 << 14, transcendentals=0),
        name=name,
    )(*operands, *after)


def lighter_of(totals):
    return jnp.where(totals[:, 0:1] <= totals[:, 1:2], 1.0, 0.0)


def lighter_panel(ref, members, onehot, light):
    comps, weightings = onehot.shape
    columns = []
    for place, member in enumerate(members):
        weights, target, other = arm_columns(member, onehot)
        here = slice(place * LANES, (place + 1) * LANES)
        lighter = light * target + (1.0 - light) * other
        ref[0:comps, here] = lighter.astype(jnp.bfloat16)
        ref[comps:comps + weightings, here] = weights
        columns.append((target, other))
    return columns


def members_of(near_ref, far_ref):
    return (near_ref.at[0], near_ref.at[1], far_ref.at[1], far_ref.at[0])


def group_kernel(weightings, pick_ref, near_ref, far_ref, totals_ref, panel_ref):
    onehot = onehot_of(pick_ref, weightings, jnp.bfloat16)
    target_sum, other_sum = 0.0, 0.0
    for member in members_of(near_ref, far_ref):
        _, target, other = arm_columns(member, onehot)
        target_sum += target
        other_sum += other
    lane = lax.broadcasted_iota(jnp.int32, totals_ref.shape, 1)
    totals = jnp.where(
        lane == 0,
        jnp.sum(target_sum, axis=1, keepdims=True),
        jnp.sum(other_sum, axis=1, keepdims=True),
    )
    totals_ref[...] = totals
    lighter_panel(panel_ref, members_of(near_ref, far_ref), onehot, lighter_of(totals))


def make_group(near, far, pick_column, weightings):
    comps = pick_column.shape[0]
    return small_call(
        functools.partial(group_kernel, weightings),
        [((comps, LANES), jnp.float32), ((comps + weightings, 4 * LANES), jnp.bfloat16)],
        [pick_column, near, far],
        [],
        "group",
    )


def panel_kernel(weightings, pick_ref, near_ref, far_ref, here_ref, told_ref, *refs):
    first_ref, second_ref, stats_ref = refs
    comps = pick_ref.shape[0]
    onehot = onehot_of(pick_ref, weightings, jnp.bfloat16)
    side = jnp.full(here_ref.shape, lax.axis_index("pat") & 1)
    totals = jnp.where(side == 0, here_ref[...], told_ref[...])
    light = lighter_of(totals)
    stats_ref[0] = jnp.broadcast_to(1.0 / totals[:, 0:1], (comps, LANES))
    stats_ref[1] = jnp.broadcast_to(1.0 / totals[:, 1:2], (comps, LANES))
    stats_ref[2] = jnp.broadcast_to(light, (comps, LANES))
    columns = lighter_panel(first_ref, members_of(near_ref, far_ref), onehot, light)
    for place, (target, other) in enumerate(columns):
        here = slice(place * LANES, (place + 1) * LANES)
        second_ref[0:comps, here] = target.astype(jnp.bfloat16)
        second_ref[comps:2 * comps, here] = other.astype(jnp.bfloat16)


def make_panels(near, far, totals, told, pick_column, weightings):
    comps = pick_column.shape[0]
    return small_call(
        functools.partial(panel_kernel, weightings),
        [
            ((comps + weightings, 4 * LANES), jnp.bfloat16),
            ((2 * comps, 4 * LANES), jnp.bfloat16),
            ((3, comps, LANES), jnp.float32),
        ],
        [pick_column, near, far, totals, told],
        [],
        "panels",
    )


def both_arms(sums, onehot, light):
    comps, weightings = onehot.shape
    lighter = sums[0:comps]
    both = jnp.dot(
        onehot,
        sums[comps:comps + weightings],
        precision=lax.Precision.HIGHEST,
        preferred_element_type=jnp.float32,
    )
    target = jnp.where(light, lighter, both - lighter)
    return target, jnp.where(light, both - lighter, lighter)


def meet_kernel(pick_ref, near_ref, far_ref, stats_ref, left_ref, right_ref, *refs):
    out_ref = refs[-1]
    comps = pick_ref.shape[0]
    rows = left_ref.shape[1] // 2
    onehot = onehot_of(pick_ref, rows - comps, jnp.float32)
    light = stats_ref[2][:, 0:1] > 0.5
    for block in range(left_ref.shape[0]):
        arms = []
        for moment in range(2):
            here = slice(moment * rows, (moment + 1) * rows)
            target, other = 0.0, 0.0
            for ref, totals_ref in ((left_ref, near_ref), (right_ref, far_ref)):
                more = both_arms(ref[block, here, :], onehot, lighter_of(totals_ref[...]) > 0.5)
                target, other = target + more[0], other + more[1]
            arms.append((target, other))
        out_ref[block, 0:comps, :] = jnp.where(light, arms[0][0], arms[0][1])
        out_ref[block, comps:rows, :] = (
            left_ref[block, comps:rows, :] + right_ref[block, comps:rows, :]
        )
        out_ref[block, rows:rows + comps, :] = (
            arms[1][0] * stats_ref[0][:, 0:1] + arms[1][1] * stats_ref[1][:, 0:1]
        )


def meet(pick_column, near_totals, far_totals, stats, left, right, after):
    blocks, rows, width = left.shape
    out = (blocks, rows // 2 + pick_column.shape[0], width)
    return small_call(
        meet_kernel,
        [(out, jnp.float32)],
        [pick_column, near_totals, far_totals, stats, left, right],
        after,
        "meet",
    )[0]


def whole_spec(shape):
    return pl.BlockSpec(shape, lambda s: (0,) * len(shape))


def moments_kernel(rows, split, *refs):
    kept_ref, passed_ref, *swapped_refs, first_ref, second_ref, stats_ref = refs[:7]
    outs = refs[-(2 if split is None else split):]
    first_rows = first_ref.shape[0]
    comps = second_ref.shape[0] // 2
    inverse_target = stats_ref[0][:, 0:1]
    inverse_other = stats_ref[1][:, 0:1]
    for place in range(swapped_refs[0].shape[0] // rows):
        here = slice(place * rows, (place + 1) * rows)
        x = jnp.concatenate(
            [kept_ref[here, :], passed_ref[0, here, :]]
            + [ref[here, :] for ref in swapped_refs],
            axis=0,
        )
        first = jnp.dot(first_ref[...], x, preferred_element_type=jnp.float32)
        squares = (x.astype(jnp.float32) * x.astype(jnp.float32)).astype(jnp.bfloat16)
        second = jnp.dot(second_ref[...], squares, preferred_element_type=jnp.float32)
        out = outs[place % 2].at[place // 2] if split is None else outs[place]
        out[0:first_rows, :] = first
        out[first_rows:first_rows + comps, :] = (
            second[0:comps] * inverse_target + second[comps:2 * comps] * inverse_other
        )


def group_moments_kernel(rows, count, *refs):
    kept_ref, passed_ref, *swapped_refs, panel_ref = refs[:5]
    outs = refs[-2 * count:]
    height = panel_ref.shape[0]
    places = kept_ref.shape[0] // rows
    for place in range(places):
        here = slice(place * rows, (place + 1) * rows)
        x = jnp.concatenate(
            [kept_ref[here, :], passed_ref[0, here, :]]
            + [ref[here, :] for ref in swapped_refs],
            axis=0,
        )
        squares = (x.astype(jnp.float32) * x.astype(jnp.float32)).astype(jnp.bfloat16)
        owner_side, middle = divmod(place // 2, places // 2 // count)
        out = outs[2 * owner_side + place % 2].at[middle]
        out[0:height, :] = jnp.dot(panel_ref[...], x, preferred_element_type=jnp.float32)
        out[height:2 * height, :] = jnp.dot(
            panel_ref[...], squares, preferred_element_type=jnp.float32
        )


def group_moments(plan, rows_here, panel, after):
    rows = panel.shape[1] // 4
    out = jax.ShapeDtypeStruct(
        (plan.places // 4, 2 * panel.shape[0], plan.width), jnp.float32
    )
    outs = pl.pallas_call(
        functools.partial(group_moments_kernel, rows, 2),
        in_specs=[pl.BlockSpec(memory_space=pltpu.VMEM)] * 5
        + [pl.BlockSpec(memory_space=pl.ANY)] * len(after),
        out_specs=[pl.BlockSpec(memory_space=pltpu.VMEM)] * 4,
        out_shape=[out] * 4,
        compiler_params=pltpu.CompilerParams(vmem_limit_bytes=20 << 20),
        cost_estimate=pl.CostEstimate(flops=0, bytes_accessed=6 << 20, transcendentals=0),
        name="group_moments",
    )(*rows_here, panel, *after)
    return outs[0:2], outs[2:4]


def moments(plan, rows_here, first, second, stats, split, after):
    rows = first.shape[1] // 4
    sums = (first.shape[0] + second.shape[0] // 2, plan.width)
    if split:
        out_shape = [jax.ShapeDtypeStruct(sums, jnp.float32)] * plan.places
    else:
        out_shape = [jax.ShapeDtypeStruct((plan.places // 2,) + sums, jnp.float32)] * 2
    return pl.pallas_call(
        functools.partial(moments_kernel, rows, plan.places if split else None),
        in_specs=[pl.BlockSpec(memory_space=pltpu.VMEM)] * 7
        + [pl.BlockSpec(memory_space=pl.ANY)] * len(after),
        out_specs=[pl.BlockSpec(memory_space=pltpu.VMEM)] * len(out_shape),
        out_shape=out_shape,
        compiler_params=pltpu.CompilerParams(vmem_limit_bytes=20 << 20),
        cost_estimate=pl.CostEstimate(flops=0, bytes_accessed=6 << 20, transcendentals=0),
        name="moments",
    )(*rows_here, first, second, stats, *after)


def finish_kernel(plan, weightings, counts, pick_ref, stats_ref, *refs):
    out_ref, ring_ref = refs[-2:]
    comps = pick_ref.shape[0]
    onehot = onehot_of(pick_ref, weightings, jnp.float32)
    inverse_target = stats_ref[0][:, 0:1]
    inverse_other = stats_ref[1][:, 0:1]
    light = stats_ref[2][:, 0:1] > 0.5
    me = lax.axis_index("pat")
    for away, count in enumerate(counts):
        sums = refs[0][...]
        for more in refs[1:count]:
            sums += more[...]
        refs = refs[count:]
        target, other = both_arms(sums, onehot, light)
        spread = sums[comps + weightings:2 * comps + weightings]
        mean_target = target * inverse_target
        mean_other = other * inverse_other
        variance = spread - mean_target * mean_target - mean_other * mean_other
        pooled = jnp.maximum(variance / 2.0, 0.01)
        balance = (mean_target - mean_other) / jnp.sqrt(pooled)
        for side in range(2):
            count = plan.tiles - plan.share if side else plan.share
            if count:
                lanes = slice(side * plan.width, side * plan.width + count * LANES)

                @pl.when((me & 1) ^ away == side)
                def _():
                    ring_ref[:, lanes] = balance[:, 0:count * LANES]
    width = plan.tiles * LANES
    shift = width - lax.rem(me * plan.block, LANES)
    out_ref[:, 0, :] = pltpu.roll(ring_ref[...], shift, 1)[:, 0:plan.block]


def finish(plan, parts, pick_column, stats, weightings):
    comps = pick_column.shape[0]
    operands = [array for part in parts for array in part]
    return pl.pallas_call(
        functools.partial(finish_kernel, plan, weightings, [len(part) for part in parts]),
        in_specs=[pl.BlockSpec(memory_space=pltpu.VMEM)] * (2 + len(operands)),
        out_specs=pl.BlockSpec(memory_space=pltpu.VMEM),
        out_shape=jax.ShapeDtypeStruct((comps, 1, plan.block), jnp.float32),
        scratch_shapes=[pltpu.VMEM((comps, plan.tiles * LANES), jnp.float32)],
        compiler_params=pltpu.CompilerParams(vmem_limit_bytes=12 << 20),
        cost_estimate=pl.CostEstimate(flops=0, bytes_accessed=1 << 14, transcendentals=0),
        name="finish",
    )(pick_column, stats, *operands)


def swap(array, pairs):
    return lax.ppermute(array, "pat", pairs)


def on_device(n, covs, covariates, weights, arms, pick):
    weightings = weights.shape[1]
    pick_column = pick.reshape(pick.shape[0], 1)
    plan = Plan(n, covariates.shape[1] // n)
    to_other_side = plan.by_mask(1)

    arm_rows = arms.T.astype(weights.dtype)
    if covs > 1:
        arm_rows = lax.all_gather(arm_rows, "cov", axis=0, tiled=True)
    mine = jnp.concatenate([weights.T, arm_rows], axis=0)
    near = jnp.stack([mine, swap(mine, to_other_side)])
    far = swap(near, [(pair ^ 1, d) for d, pair in plan.by_rows()])

    kept0, kept1, sent0, sent1, other0, other1 = pack(covariates, plan)
    rows_here = {}
    for chunk, kept, sent, other in ((1, kept1, sent1, other1), (0, kept0, sent0, other0)):
        passed = swap(other, to_other_side)
        rows_here[chunk] = [
            kept, passed, swap(sent, plan.by_rows()), swap(passed[1], plan.by_rows())
        ]

    near_totals, panel = make_group(near, far, pick_column, weightings)
    far_totals = swap(near_totals, plan.by_sums())
    totals = near_totals + far_totals
    for mask in range(8, n, 8):
        for more in (mask, mask | 4):
            totals = totals + swap(near_totals, plan.by_mask(more)[0::2])
    told = swap(totals, to_other_side[0::2])
    first, second, stats = make_panels(near, far, totals, told, pick_column, weightings)

    across, top, after = [], [], [rows_here[0][2]]
    for even, odd in group_moments(plan, rows_here[1], panel, [totals]):
        arrived = swap(odd, plan.by_sums())
        met = meet(pick_column, near_totals, far_totals, stats, even, arrived, after)
        for bit in plan.middle_bits:
            met = met[0::2] + swap(met[1::2], plan.by_mask(1 << bit))
        across.append(met)
        top.append(swap(met, plan.by_mask(1 << plan.top_bit))[0])
        after = []

    last = not plan.middle_bits
    sums = moments(plan, rows_here[0], first, second, stats, last, across)
    if last:
        even, odd = sums[0::2], sums[1::2]
        other_owner = [(d, pair ^ 1) for d, pair in plan.by_sums()]
        parts = [
            [even[0], top[0], swap(odd[0], plan.by_sums())],
            [swap(even[1] + top[1], to_other_side), swap(odd[1], other_owner)],
        ]
    else:
        even, odd = sums
        arrived = swap(odd, plan.by_sums())
        for bit in plan.middle_bits:
            odd = even[1::2] + arrived[1::2]
            even = even[0::2] + arrived[0::2]
            arrived = swap(odd, plan.by_mask(1 << bit))
        total = [even[side] + arrived[side] + top[side] for side in range(2)]
        parts = [[total[0]], [swap(total[1], to_other_side)]]
    return finish(plan, parts, pick_column, stats, weightings)


def solution(mesh):
    placed = (
        P(("groups", "pat"), "cov"),
        P(("groups", "pat"), None),
        P(("groups", "pat"), "cov"),
        P(),
    )
    body = functools.partial(on_device, mesh.shape["pat"], mesh.shape["cov"])
    return jax.shard_map(
        body, mesh=mesh, in_specs=placed, out_specs=P("groups", "cov", "pat"), check_vma=False
    )
```

```python
import functools

import jax
import jax.numpy as jnp
from jax import lax
from jax.experimental import pallas as pl
from jax.experimental.pallas import tpu as pltpu
from jax.sharding import PartitionSpec as P

LANES = 128


def round_up(value, multiple):
    return -(-value // multiple) * multiple


class Plan:
    def __init__(self, n, block):
        self.n = n
        self.block = block
        self.tiles = round_up(block, LANES) // LANES
        self.share = (self.tiles + 1) // 2
        self.width = self.share * LANES
        self.places = n // 4
        *self.middle_bits, self.top_bit = range(3, n.bit_length() - 1)

    def by_rows(self):
        return [(d, d ^ (2 + 2 * (d & 1))) for d in range(self.n)]

    def by_sums(self):
        return [(d, d ^ (4 - 2 * (d & 1))) for d in range(self.n)]

    def by_mask(self, mask):
        return [(d, d ^ mask) for d in range(self.n)]


def pack_kernel(
    plan, x_ref, kept0_ref, kept1_ref, sent0_ref, sent1_ref, other0_ref, other1_ref, x0_ref, x1_ref,
    sems,
):
    step = pl.program_id(0)
    me = lax.axis_index("pat")
    rows, half = x0_ref.shape
    last_tile = half // LANES - 1
    lane = lax.broadcasted_iota(jnp.int32, (rows, LANES), 1)

    def start_of(chunk):
        return ((me >> plan.top_bit) ^ chunk) * half

    def load(chunk, buffer):
        here = pl.ds(pl.multiple_of(start_of(chunk), LANES), half)
        return pltpu.make_async_copy(x_ref.at[:, here], buffer, sems.at[chunk])

    @pl.when(step == 0)
    def _():
        load(1, x1_ref).start()
        load(0, x0_ref).start()
        load(1, x1_ref).wait()

    @pl.when(step == plan.places)
    def _():
        load(0, x0_ref).wait()

    def tile(index):
        return pl.ds(pl.multiple_of(jnp.minimum(index, last_tile) * LANES, LANES), LANES)

    middle = len(plan.middle_bits)

    def fill(chunk, place, buffer, targets):
        for away in range(2):
            side = (me & 1) ^ away
            holder = me ^ away
            for sent in range(2):
                relative = (
                    (place >> (1 + middle))
                    | (sent << (1 + side))
                    | ((place & 1) << (2 - side))
                    | (((place >> 1) & ((1 << middle) - 1)) << 3)
                    | (chunk << plan.top_bit)
                )
                column = (holder ^ relative) * plan.block - start_of(chunk)
                first = column // LANES
                edge = (column - first * LANES) * (1 - side)
                head = buffer[:, tile(first + side * plan.share)]
                tail = buffer[:, tile(first + plan.tiles)]
                folded = jnp.where(lane >= edge, head.astype(jnp.float32), tail.astype(jnp.float32))
                target = targets[2].at[sent] if away else targets[sent]
                target[:, 0:LANES] = folded.astype(buffer.dtype)
                for slot in range(1, plan.share):
                    here = slice(slot * LANES, (slot + 1) * LANES)
                    target[:, here] = buffer[:, tile(first + side * plan.share + slot)]

    @pl.when(step < plan.places)
    def _():
        fill(1, step, x1_ref, (kept1_ref, sent1_ref, other1_ref))

    @pl.when(step >= plan.places)
    def _():
        fill(0, step - plan.places, x0_ref, (kept0_ref, sent0_ref, other0_ref))


def pack(covariates, plan):
    rows, columns = covariates.shape
    dtype = covariates.dtype
    length = plan.places * rows
    mine = jax.ShapeDtypeStruct((length, plan.width), dtype)
    other = jax.ShapeDtypeStruct((2, length, plan.width), dtype)
    last = plan.places - 1
    specs = []
    for index in (lambda s: jnp.maximum(s - plan.places, 0), lambda s: jnp.minimum(s, last)):
        specs.append((
            pl.BlockSpec((rows, plan.width), lambda s, index=index: (index(s), 0)),
            pl.BlockSpec((2, rows, plan.width), lambda s, index=index: (0, index(s), 0)),
        ))
    (mine0, other0), (mine1, other1) = specs
    return pl.pallas_call(
        functools.partial(pack_kernel, plan),
        grid=(2 * plan.places,),
        in_specs=[pl.BlockSpec(memory_space=pl.ANY)],
        out_specs=[mine0, mine1, mine0, mine1, other0, other1],
        out_shape=[mine] * 4 + [other] * 2,
        scratch_shapes=[
            pltpu.VMEM((rows, columns // 2), dtype),
            pltpu.VMEM((rows, columns // 2), dtype),
            pltpu.SemaphoreType.DMA((2,)),
        ],
        compiler_params=pltpu.CompilerParams(vmem_limit_bytes=58 << 20),
        cost_estimate=pl.CostEstimate(
            flops=0, bytes_accessed=4 * covariates.size, transcendentals=0
        ),
        name="pack",
    )(covariates)


def onehot_of(pick_ref, weightings, dtype):
    index = lax.broadcasted_iota(jnp.int32, (pick_ref.shape[0], weightings), 1)
    return jnp.where(index == pick_ref[...], 1.0, 0.0).astype(dtype)


def arm_columns(panel_ref, onehot):
    comps, weightings = onehot.shape
    weights = panel_ref[0:weightings, :]
    arms = panel_ref[weightings:weightings + comps, :].astype(jnp.float32)
    picked = jnp.dot(onehot, weights, preferred_element_type=jnp.float32)
    return weights, picked * arms, picked * (1.0 - arms)


def small_call(kernel, shapes, operands, after, name):
    vmem = pl.BlockSpec(memory_space=pltpu.VMEM)
    return pl.pallas_call(
        kernel,
        in_specs=[vmem] * len(operands) + [pl.BlockSpec(memory_space=pl.ANY)] * len(after),
        out_specs=[vmem] * len(shapes),
        out_shape=[jax.ShapeDtypeStruct(shape, dtype) for shape, dtype in shapes],
        compiler_params=pltpu.CompilerParams(vmem_limit_bytes=8 << 20),
        cost_estimate=pl.CostEstimate(flops=0, bytes_accessed=1 << 14, transcendentals=0),
        name=name,
    )(*operands, *after)


def lighter_of(totals):
    return jnp.where(totals[:, 0:1] <= totals[:, 1:2], 1.0, 0.0)


def lighter_panel(ref, members, onehot, light):
    comps, weightings = onehot.shape
    columns = []
    for place, member in enumerate(members):
        weights, target, other = arm_columns(member, onehot)
        here = slice(place * LANES, (place + 1) * LANES)
        lighter = light * target + (1.0 - light) * other
        ref[0:comps, here] = lighter.astype(jnp.bfloat16)
        ref[comps:comps + weightings, here] = weights
        columns.append((target, other))
    return columns


def members_of(near_ref, far_ref):
    return (near_ref.at[0], near_ref.at[1], far_ref.at[1], far_ref.at[0])


def group_kernel(weightings, pick_ref, near_ref, far_ref, totals_ref, panel_ref):
    onehot = onehot_of(pick_ref, weightings, jnp.bfloat16)
    target_sum, other_sum = 0.0, 0.0
    for member in members_of(near_ref, far_ref):
        _, target, other = arm_columns(member, onehot)
        target_sum += target
        other_sum += other
    lane = lax.broadcasted_iota(jnp.int32, totals_ref.shape, 1)
    totals = jnp.where(
        lane == 0,
        jnp.sum(target_sum, axis=1, keepdims=True),
        jnp.sum(other_sum, axis=1, keepdims=True),
    )
    totals_ref[...] = totals
    lighter_panel(panel_ref, members_of(near_ref, far_ref), onehot, lighter_of(totals))


def make_group(near, far, pick_column, weightings):
    comps = pick_column.shape[0]
    return small_call(
        functools.partial(group_kernel, weightings),
        [((comps, LANES), jnp.float32), ((comps + weightings, 4 * LANES), jnp.bfloat16)],
        [pick_column, near, far],
        [],
        "group",
    )


def panel_kernel(weightings, pick_ref, near_ref, far_ref, here_ref, told_ref, *refs):
    first_ref, second_ref, stats_ref = refs
    comps = pick_ref.shape[0]
    onehot = onehot_of(pick_ref, weightings, jnp.bfloat16)
    side = jnp.full(here_ref.shape, lax.axis_index("pat") & 1)
    totals = jnp.where(side == 1, here_ref[...], told_ref[...])
    light = lighter_of(totals)
    stats_ref[0] = jnp.broadcast_to(1.0 / totals[:, 0:1], (comps, LANES))
    stats_ref[1] = jnp.broadcast_to(1.0 / totals[:, 1:2], (comps, LANES))
    stats_ref[2] = jnp.broadcast_to(light, (comps, LANES))
    columns = lighter_panel(first_ref, members_of(near_ref, far_ref), onehot, light)
    for place, (target, other) in enumerate(columns):
        here = slice(place * LANES, (place + 1) * LANES)
        second_ref[0:comps, here] = target.astype(jnp.bfloat16)
        second_ref[comps:2 * comps, here] = other.astype(jnp.bfloat16)


def make_panels(near, far, totals, told, pick_column, weightings):
    comps = pick_column.shape[0]
    return small_call(
        functools.partial(panel_kernel, weightings),
        [
            ((comps + weightings, 4 * LANES), jnp.bfloat16),
            ((2 * comps, 4 * LANES), jnp.bfloat16),
            ((3, comps, LANES), jnp.float32),
        ],
        [pick_column, near, far, totals, told],
        [],
        "panels",
    )


def both_arms(sums, onehot, light):
    comps, weightings = onehot.shape
    lighter = sums[0:comps]
    both = jnp.dot(
        onehot,
        sums[comps:comps + weightings],
        precision=lax.Precision.HIGHEST,
        preferred_element_type=jnp.float32,
    )
    target = jnp.where(light, lighter, both - lighter)
    return target, jnp.where(light, both - lighter, lighter)


def meet_kernel(pick_ref, near_ref, far_ref, stats_ref, left_ref, right_ref, *refs):
    out_ref = refs[-1]
    comps = pick_ref.shape[0]
    rows = left_ref.shape[1] // 2
    onehot = onehot_of(pick_ref, rows - comps, jnp.float32)
    light = stats_ref[2][:, 0:1] > 0.5
    for block in range(left_ref.shape[0]):
        arms = []
        for moment in range(2):
            here = slice(moment * rows, (moment + 1) * rows)
            target, other = 0.0, 0.0
            for ref, totals_ref in ((left_ref, near_ref), (right_ref, far_ref)):
                more = both_arms(ref[block, here, :], onehot, lighter_of(totals_ref[...]) > 0.5)
                target, other = target + more[0], other + more[1]
            arms.append((target, other))
        out_ref[block, 0:comps, :] = jnp.where(light, arms[0][0], arms[0][1])
        out_ref[block, comps:rows, :] = (
            left_ref[block, comps:rows, :] + right_ref[block, comps:rows, :]
        )
        out_ref[block, rows:rows + comps, :] = (
            arms[1][0] * stats_ref[0][:, 0:1] + arms[1][1] * stats_ref[1][:, 0:1]
        )


def meet(pick_column, near_totals, far_totals, stats, left, right, after):
    blocks, rows, width = left.shape
    out = (blocks, rows // 2 + pick_column.shape[0], width)
    return small_call(
        meet_kernel,
        [(out, jnp.float32)],
        [pick_column, near_totals, far_totals, stats, left, right],
        after,
        "meet",
    )[0]


def whole_spec(shape):
    return pl.BlockSpec(shape, lambda s: (0,) * len(shape))


def moments_kernel(rows, split, *refs):
    kept_ref, passed_ref, *swapped_refs, first_ref, second_ref, stats_ref = refs[:7]
    outs = refs[-(2 if split is None else split):]
    first_rows = first_ref.shape[0]
    comps = second_ref.shape[0] // 2
    inverse_target = stats_ref[0][:, 0:1]
    inverse_other = stats_ref[1][:, 0:1]
    for place in range(swapped_refs[0].shape[0] // rows):
        here = slice(place * rows, (place + 1) * rows)
        x = jnp.concatenate(
            [kept_ref[here, :], passed_ref[0, here, :]]
            + [ref[here, :] for ref in swapped_refs],
            axis=0,
        )
        first = jnp.dot(first_ref[...], x, preferred_element_type=jnp.float32)
        squares = (x.astype(jnp.float32) * x.astype(jnp.float32)).astype(jnp.bfloat16)
        second = jnp.dot(second_ref[...], squares, preferred_element_type=jnp.float32)
        out = outs[place % 2].at[place // 2] if split is None else outs[place]
        out[0:first_rows, :] = first
        out[first_rows:first_rows + comps, :] = (
            second[0:comps] * inverse_target + second[comps:2 * comps] * inverse_other
        )


def group_moments_kernel(rows, count, *refs):
    kept_ref, passed_ref, *swapped_refs, panel_ref = refs[:5]
    outs = refs[-2 * count:]
    height = panel_ref.shape[0]
    places = kept_ref.shape[0] // rows
    for place in range(places):
        here = slice(place * rows, (place + 1) * rows)
        x = jnp.concatenate(
            [kept_ref[here, :], passed_ref[0, here, :]]
            + [ref[here, :] for ref in swapped_refs],
            axis=0,
        )
        squares = (x.astype(jnp.float32) * x.astype(jnp.float32)).astype(jnp.bfloat16)
        owner_side, middle = divmod(place // 2, places // 2 // count)
        out = outs[2 * owner_side + place % 2].at[middle]
        out[0:height, :] = jnp.dot(panel_ref[...], x, preferred_element_type=jnp.float32)
        out[height:2 * height, :] = jnp.dot(
            panel_ref[...], squares, preferred_element_type=jnp.float32
        )


def group_moments(plan, rows_here, panel, after):
    rows = panel.shape[1] // 4
    out = jax.ShapeDtypeStruct(
        (plan.places // 4, 2 * panel.shape[0], plan.width), jnp.float32
    )
    outs = pl.pallas_call(
        functools.partial(group_moments_kernel, rows, 2),
        in_specs=[pl.BlockSpec(memory_space=pltpu.VMEM)] * 5
        + [pl.BlockSpec(memory_space=pl.ANY)] * len(after),
        out_specs=[pl.BlockSpec(memory_space=pltpu.VMEM)] * 4,
        out_shape=[out] * 4,
        compiler_params=pltpu.CompilerParams(vmem_limit_bytes=20 << 20),
        cost_estimate=pl.CostEstimate(flops=0, bytes_accessed=6 << 20, transcendentals=0),
        name="group_moments",
    )(*rows_here, panel, *after)
    return outs[0:2], outs[2:4]


def moments(plan, rows_here, first, second, stats, split, after):
    rows = first.shape[1] // 4
    sums = (first.shape[0] + second.shape[0] // 2, plan.width)
    if split:
        out_shape = [jax.ShapeDtypeStruct(sums, jnp.float32)] * plan.places
    else:
        out_shape = [jax.ShapeDtypeStruct((plan.places // 2,) + sums, jnp.float32)] * 2
    return pl.pallas_call(
        functools.partial(moments_kernel, rows, plan.places if split else None),
        in_specs=[pl.BlockSpec(memory_space=pltpu.VMEM)] * 7
        + [pl.BlockSpec(memory_space=pl.ANY)] * len(after),
        out_specs=[pl.BlockSpec(memory_space=pltpu.VMEM)] * len(out_shape),
        out_shape=out_shape,
        compiler_params=pltpu.CompilerParams(vmem_limit_bytes=20 << 20),
        cost_estimate=pl.CostEstimate(flops=0, bytes_accessed=6 << 20, transcendentals=0),
        name="moments",
    )(*rows_here, first, second, stats, *after)


def finish_kernel(plan, weightings, counts, pick_ref, stats_ref, *refs):
    out_ref, ring_ref = refs[-2:]
    comps = pick_ref.shape[0]
    onehot = onehot_of(pick_ref, weightings, jnp.float32)
    inverse_target = stats_ref[0][:, 0:1]
    inverse_other = stats_ref[1][:, 0:1]
    light = stats_ref[2][:, 0:1] > 0.5
    me = lax.axis_index("pat")
    for away, count in enumerate(counts):
        sums = refs[0][...]
        for more in refs[1:count]:
            sums += more[...]
        refs = refs[count:]
        target, other = both_arms(sums, onehot, light)
        spread = sums[comps + weightings:2 * comps + weightings]
        mean_target = target * inverse_target
        mean_other = other * inverse_other
        variance = spread - mean_target * mean_target - mean_other * mean_other
        pooled = jnp.maximum(variance / 2.0, 0.01)
        balance = (mean_target - mean_other) / jnp.sqrt(pooled)
        for side in range(2):
            count = plan.tiles - plan.share if side else plan.share
            if count:
                lanes = slice(side * plan.width, side * plan.width + count * LANES)

                @pl.when((me & 1) ^ away == side)
                def _():
                    ring_ref[:, lanes] = balance[:, 0:count * LANES]
    width = plan.tiles * LANES
    shift = width - lax.rem(me * plan.block, LANES)
    out_ref[:, 0, :] = pltpu.roll(ring_ref[...], shift, 1)[:, 0:plan.block]


def finish(plan, parts, pick_column, stats, weightings):
    comps = pick_column.shape[0]
    operands = [array for part in parts for array in part]
    return pl.pallas_call(
        functools.partial(finish_kernel, plan, weightings, [len(part) for part in parts]),
        in_specs=[pl.BlockSpec(memory_space=pltpu.VMEM)] * (2 + len(operands)),
        out_specs=pl.BlockSpec(memory_space=pltpu.VMEM),
        out_shape=jax.ShapeDtypeStruct((comps, 1, plan.block), jnp.float32),
        scratch_shapes=[pltpu.VMEM((comps, plan.tiles * LANES), jnp.float32)],
        compiler_params=pltpu.CompilerParams(vmem_limit_bytes=12 << 20),
        cost_estimate=pl.CostEstimate(flops=0, bytes_accessed=1 << 14, transcendentals=0),
        name="finish",
    )(pick_column, stats, *operands)


def hold_kernel(*refs):
    del refs


def hold(array, after):
    any_space = pl.BlockSpec(memory_space=pl.ANY)
    return pl.pallas_call(
        hold_kernel,
        in_specs=[any_space] * (1 + len(after)),
        out_specs=any_space,
        out_shape=jax.ShapeDtypeStruct(array.shape, array.dtype),
        input_output_aliases={0: 0},
        compiler_params=pltpu.CompilerParams(vmem_limit_bytes=1 << 20),
        cost_estimate=pl.CostEstimate(flops=0, bytes_accessed=0, transcendentals=0),
        name="hold",
    )(array, *after)


def swap(array, pairs):
    return lax.ppermute(array, "pat", pairs)


def on_device(n, covs, covariates, weights, arms, pick):
    weightings = weights.shape[1]
    pick_column = pick.reshape(pick.shape[0], 1)
    plan = Plan(n, covariates.shape[1] // n)
    to_other_side = plan.by_mask(1)

    arm_rows = arms.T.astype(weights.dtype)
    if covs > 1:
        arm_rows = lax.all_gather(arm_rows, "cov", axis=0, tiled=True)
    mine = jnp.concatenate([weights.T, arm_rows], axis=0)
    near = jnp.stack([mine, swap(mine, to_other_side)])
    far = swap(near, [(pair ^ 1, d) for d, pair in plan.by_rows()])

    kept0, kept1, sent0, sent1, other0, other1 = pack(covariates, plan)
    near_totals, panel = make_group(near, far, pick_column, weightings)
    far_totals = swap(near_totals, plan.by_sums())
    totals = near_totals + far_totals
    for mask in range(8, n, 8):
        for more in (mask, mask | 2):
            totals = totals + swap(near_totals, plan.by_mask(more)[1::2])
    told = swap(totals, to_other_side[1::2])

    rows_here = {}
    for chunk, kept, sent, other, after in (
        (1, kept1, sent1, other1, []), (0, kept0, sent0, other0, [totals])
    ):
        passed = swap(other, to_other_side)
        forward = passed[1]
        if after:
            sent, forward = hold(sent, after), hold(forward, after)
        rows_here[chunk] = [
            kept, passed, swap(sent, plan.by_rows()), swap(forward, plan.by_rows())
        ]
    first, second, stats = make_panels(near, far, totals, told, pick_column, weightings)

    across, top, after = [], [], [rows_here[0][2]]
    for even, odd in group_moments(plan, rows_here[1], panel, [far_totals]):
        arrived = swap(odd, plan.by_sums())
        met = meet(pick_column, near_totals, far_totals, stats, even, arrived, after)
        for bit in plan.middle_bits:
            met = met[0::2] + swap(met[1::2], plan.by_mask(1 << bit))
        across.append(met)
        top.append(swap(met, plan.by_mask(1 << plan.top_bit))[0])
        after = []

    last = not plan.middle_bits
    sums = moments(plan, rows_here[0], first, second, stats, last, across)
    if last:
        even, odd = sums[0::2], sums[1::2]
        other_owner = [(d, pair ^ 1) for d, pair in plan.by_sums()]
        parts = [
            [even[0], top[0], swap(odd[0], plan.by_sums())],
            [swap(even[1] + top[1], to_other_side), swap(odd[1], other_owner)],
        ]
    else:
        even, odd = sums
        arrived = swap(odd, plan.by_sums())
        for bit in plan.middle_bits:
            odd = even[1::2] + arrived[1::2]
            even = even[0::2] + arrived[0::2]
            arrived = swap(odd, plan.by_mask(1 << bit))
        total = [even[side] + arrived[side] + top[side] for side in range(2)]
        parts = [[total[0]], [swap(total[1], to_other_side)]]
    return finish(plan, parts, pick_column, stats, weightings)


def solution(mesh):
    placed = (
        P(("groups", "pat"), "cov"),
        P(("groups", "pat"), None),
        P(("groups", "pat"), "cov"),
        P(),
    )
    body = functools.partial(on_device, mesh.shape["pat"], mesh.shape["cov"])
    return jax.shard_map(
        body, mesh=mesh, in_specs=placed, out_specs=P("groups", "cov", "pat"), check_vma=False
    )
```

```python
import functools

import jax
import jax.numpy as jnp
from jax import lax
from jax.experimental import pallas as pl
from jax.experimental.pallas import tpu as pltpu
from jax.sharding import PartitionSpec as P

LANES = 128


def round_up(value, multiple):
    return -(-value // multiple) * multiple


class Plan:
    def __init__(self, n, block):
        self.n = n
        self.block = block
        self.tiles = round_up(block, LANES) // LANES
        self.share = (self.tiles + 1) // 2
        self.width = self.share * LANES
        self.places = n // 4
        *self.middle_bits, self.top_bit = range(3, n.bit_length() - 1)

    def by_rows(self):
        return [(d, d ^ (2 + 2 * (d & 1))) for d in range(self.n)]

    def by_sums(self):
        return [(d, d ^ (4 - 2 * (d & 1))) for d in range(self.n)]

    def by_mask(self, mask):
        return [(d, d ^ mask) for d in range(self.n)]


def pack_kernel(
    plan, x_ref, kept0_ref, kept1_ref, sent0_ref, sent1_ref, other0_ref, other1_ref
):
    me = lax.axis_index("pat")
    rows, columns = x_ref.shape
    last_tile = columns // LANES - 1
    lane = lax.broadcasted_iota(jnp.int32, (rows, LANES), 1)
    middle = len(plan.middle_bits)

    def tile(index):
        return pl.ds(pl.multiple_of(jnp.minimum(index, last_tile) * LANES, LANES), LANES)

    def fill(place, chunk, targets):
        for away in range(2):
            side = (me & 1) ^ away
            holder = me ^ away
            for sent in range(2):
                relative = (
                    (place >> (1 + middle))
                    | (sent << (1 + side))
                    | ((place & 1) << (2 - side))
                    | (((place >> 1) & ((1 << middle) - 1)) << 3)
                    | (chunk << plan.top_bit)
                )
                column = (holder ^ relative) * plan.block
                first = column // LANES
                edge = (column - first * LANES) * (1 - side)
                head = x_ref[:, tile(first + side * plan.share)]
                tail = x_ref[:, tile(first + plan.tiles)]
                folded = jnp.where(lane >= edge, head.astype(jnp.float32), tail.astype(jnp.float32))
                target = targets[2].at[sent, place] if away else targets[sent].at[place]
                target[:, 0:LANES] = folded.astype(x_ref.dtype)
                for slot in range(1, plan.share):
                    here = slice(slot * LANES, (slot + 1) * LANES)
                    target[:, here] = x_ref[:, tile(first + side * plan.share + slot)]

    @pl.loop(0, plan.places)
    def _(place):
        fill(place, 1, (kept1_ref, sent1_ref, other1_ref))
        fill(place, 0, (kept0_ref, sent0_ref, other0_ref))


def pack(covariates, plan):
    rows, columns = covariates.shape
    dtype = covariates.dtype
    step = 32
    mine = jax.ShapeDtypeStruct((plan.places, rows, plan.width), dtype)
    other = jax.ShapeDtypeStruct((2, plan.places, rows, plan.width), dtype)
    mine_spec = pl.BlockSpec((plan.places, step, plan.width), lambda s: (0, s, 0))
    other_spec = pl.BlockSpec((2, plan.places, step, plan.width), lambda s: (0, 0, s, 0))
    outs = pl.pallas_call(
        functools.partial(pack_kernel, plan),
        grid=(rows // step,),
        in_specs=[pl.BlockSpec((step, columns), lambda s: (s, 0))],
        out_specs=[mine_spec] * 4 + [other_spec] * 2,
        out_shape=[mine] * 4 + [other] * 2,
        compiler_params=pltpu.CompilerParams(vmem_limit_bytes=58 << 20),
        cost_estimate=pl.CostEstimate(
            flops=0, bytes_accessed=4 * covariates.size, transcendentals=0
        ),
        name="pack",
    )(covariates)
    length = plan.places * rows
    return [out.reshape(length, plan.width) for out in outs[:4]] + [
        out.reshape(2, length, plan.width) for out in outs[4:]
    ]


def onehot_of(pick_ref, weightings, dtype):
    index = lax.broadcasted_iota(jnp.int32, (pick_ref.shape[0], weightings), 1)
    return jnp.where(index == pick_ref[...], 1.0, 0.0).astype(dtype)


def arm_columns(panel_ref, onehot):
    comps, weightings = onehot.shape
    weights = panel_ref[0:weightings, :]
    arms = panel_ref[weightings:weightings + comps, :].astype(jnp.float32)
    picked = jnp.dot(onehot, weights, preferred_element_type=jnp.float32)
    return weights, picked * arms, picked * (1.0 - arms)


def small_call(kernel, shapes, operands, after, name):
    vmem = pl.BlockSpec(memory_space=pltpu.VMEM)
    return pl.pallas_call(
        kernel,
        in_specs=[vmem] * len(operands) + [pl.BlockSpec(memory_space=pl.ANY)] * len(after),
        out_specs=[vmem] * len(shapes),
        out_shape=[jax.ShapeDtypeStruct(shape, dtype) for shape, dtype in shapes],
        compiler_params=pltpu.CompilerParams(vmem_limit_bytes=8 << 20),
        cost_estimate=pl.CostEstimate(flops=0, bytes_accessed=1 << 14, transcendentals=0),
        name=name,
    )(*operands, *after)


def lighter_of(totals):
    return jnp.where(totals[:, 0:1] <= totals[:, 1:2], 1.0, 0.0)


def lighter_panel(ref, members, onehot, light):
    comps, weightings = onehot.shape
    columns = []
    for place, member in enumerate(members):
        weights, target, other = arm_columns(member, onehot)
        here = slice(place * LANES, (place + 1) * LANES)
        lighter = light * target + (1.0 - light) * other
        ref[0:comps, here] = lighter.astype(jnp.bfloat16)
        ref[comps:comps + weightings, here] = weights
        columns.append((target, other))
    return columns


def members_of(near_ref, far_ref):
    return (near_ref.at[0], near_ref.at[1], far_ref.at[1], far_ref.at[0])


def group_kernel(weightings, pick_ref, near_ref, far_ref, totals_ref, panel_ref):
    onehot = onehot_of(pick_ref, weightings, jnp.bfloat16)
    target_sum, other_sum = 0.0, 0.0
    for member in members_of(near_ref, far_ref):
        _, target, other = arm_columns(member, onehot)
        target_sum += target
        other_sum += other
    lane = lax.broadcasted_iota(jnp.int32, totals_ref.shape, 1)
    totals = jnp.where(
        lane == 0,
        jnp.sum(target_sum, axis=1, keepdims=True),
        jnp.sum(other_sum, axis=1, keepdims=True),
    )
    totals_ref[...] = totals
    lighter_panel(panel_ref, members_of(near_ref, far_ref), onehot, lighter_of(totals))


def make_group(near, far, pick_column, weightings):
    comps = pick_column.shape[0]
    return small_call(
        functools.partial(group_kernel, weightings),
        [((comps, LANES), jnp.float32), ((comps + weightings, 4 * LANES), jnp.bfloat16)],
        [pick_column, near, far],
        [],
        "group",
    )


def panel_kernel(weightings, pick_ref, near_ref, far_ref, here_ref, told_ref, *refs):
    first_ref, second_ref, stats_ref = refs
    comps = pick_ref.shape[0]
    onehot = onehot_of(pick_ref, weightings, jnp.bfloat16)
    side = jnp.full(here_ref.shape, lax.axis_index("pat") & 1)
    totals = jnp.where(side == 0, here_ref[...], told_ref[...])
    light = lighter_of(totals)
    stats_ref[0] = jnp.broadcast_to(1.0 / totals[:, 0:1], (comps, LANES))
    stats_ref[1] = jnp.broadcast_to(1.0 / totals[:, 1:2], (comps, LANES))
    stats_ref[2] = jnp.broadcast_to(light, (comps, LANES))
    columns = lighter_panel(first_ref, members_of(near_ref, far_ref), onehot, light)
    for place, (target, other) in enumerate(columns):
        here = slice(place * LANES, (place + 1) * LANES)
        second_ref[0:comps, here] = target.astype(jnp.bfloat16)
        second_ref[comps:2 * comps, here] = other.astype(jnp.bfloat16)


def make_panels(near, far, totals, told, pick_column, weightings):
    comps = pick_column.shape[0]
    return small_call(
        functools.partial(panel_kernel, weightings),
        [
            ((comps + weightings, 4 * LANES), jnp.bfloat16),
            ((2 * comps, 4 * LANES), jnp.bfloat16),
            ((3, comps, LANES), jnp.float32),
        ],
        [pick_column, near, far, totals, told],
        [],
        "panels",
    )


def both_arms(sums, onehot, light):
    comps, weightings = onehot.shape
    lighter = sums[0:comps]
    both = jnp.dot(
        onehot,
        sums[comps:comps + weightings],
        precision=lax.Precision.HIGHEST,
        preferred_element_type=jnp.float32,
    )
    target = jnp.where(light, lighter, both - lighter)
    return target, jnp.where(light, both - lighter, lighter)


def meet_kernel(pick_ref, near_ref, far_ref, stats_ref, left_ref, right_ref, *refs):
    out_ref = refs[-1]
    comps = pick_ref.shape[0]
    rows = left_ref.shape[1] // 2
    onehot = onehot_of(pick_ref, rows - comps, jnp.float32)
    light = stats_ref[2][:, 0:1] > 0.5
    for block in range(left_ref.shape[0]):
        arms = []
        for moment in range(2):
            here = slice(moment * rows, (moment + 1) * rows)
            target, other = 0.0, 0.0
            for ref, totals_ref in ((left_ref, near_ref), (right_ref, far_ref)):
                more = both_arms(ref[block, here, :], onehot, lighter_of(totals_ref[...]) > 0.5)
                target, other = target + more[0], other + more[1]
            arms.append((target, other))
        out_ref[block, 0:comps, :] = jnp.where(light, arms[0][0], arms[0][1])
        out_ref[block, comps:rows, :] = (
            left_ref[block, comps:rows, :] + right_ref[block, comps:rows, :]
        )
        out_ref[block, rows:rows + comps, :] = (
            arms[1][0] * stats_ref[0][:, 0:1] + arms[1][1] * stats_ref[1][:, 0:1]
        )


def meet(pick_column, near_totals, far_totals, stats, left, right, after):
    blocks, rows, width = left.shape
    out = (blocks, rows // 2 + pick_column.shape[0], width)
    return small_call(
        meet_kernel,
        [(out, jnp.float32)],
        [pick_column, near_totals, far_totals, stats, left, right],
        after,
        "meet",
    )[0]


def whole_spec(shape):
    return pl.BlockSpec(shape, lambda s: (0,) * len(shape))


def moments_kernel(rows, split, *refs):
    kept_ref, passed_ref, *swapped_refs, first_ref, second_ref, stats_ref = refs[:7]
    outs = refs[-(2 if split is None else split):]
    first_rows = first_ref.shape[0]
    comps = second_ref.shape[0] // 2
    inverse_target = stats_ref[0][:, 0:1]
    inverse_other = stats_ref[1][:, 0:1]
    for place in range(swapped_refs[0].shape[0] // rows):
        here = slice(place * rows, (place + 1) * rows)
        x = jnp.concatenate(
            [kept_ref[here, :], passed_ref[0, here, :]]
            + [ref[here, :] for ref in swapped_refs],
            axis=0,
        )
        first = jnp.dot(first_ref[...], x, preferred_element_type=jnp.float32)
        squares = (x.astype(jnp.float32) * x.astype(jnp.float32)).astype(jnp.bfloat16)
        second = jnp.dot(second_ref[...], squares, preferred_element_type=jnp.float32)
        out = outs[place % 2].at[place // 2] if split is None else outs[place]
        out[0:first_rows, :] = first
        out[first_rows:first_rows + comps, :] = (
            second[0:comps] * inverse_target + second[comps:2 * comps] * inverse_other
        )


def group_moments_kernel(rows, count, *refs):
    kept_ref, passed_ref, *swapped_refs, panel_ref = refs[:5]
    outs = refs[-2 * count:]
    height = panel_ref.shape[0]
    places = kept_ref.shape[0] // rows
    for place in range(places):
        here = slice(place * rows, (place + 1) * rows)
        x = jnp.concatenate(
            [kept_ref[here, :], passed_ref[0, here, :]]
            + [ref[here, :] for ref in swapped_refs],
            axis=0,
        )
        squares = (x.astype(jnp.float32) * x.astype(jnp.float32)).astype(jnp.bfloat16)
        owner_side, middle = divmod(place // 2, places // 2 // count)
        out = outs[2 * owner_side + place % 2].at[middle]
        out[0:height, :] = jnp.dot(panel_ref[...], x, preferred_element_type=jnp.float32)
        out[height:2 * height, :] = jnp.dot(
            panel_ref[...], squares, preferred_element_type=jnp.float32
        )


def group_moments(plan, rows_here, panel, after):
    rows = panel.shape[1] // 4
    out = jax.ShapeDtypeStruct(
        (plan.places // 4, 2 * panel.shape[0], plan.width), jnp.float32
    )
    outs = pl.pallas_call(
        functools.partial(group_moments_kernel, rows, 2),
        in_specs=[pl.BlockSpec(memory_space=pltpu.VMEM)] * 5
        + [pl.BlockSpec(memory_space=pl.ANY)] * len(after),
        out_specs=[pl.BlockSpec(memory_space=pltpu.VMEM)] * 4,
        out_shape=[out] * 4,
        compiler_params=pltpu.CompilerParams(vmem_limit_bytes=20 << 20),
        cost_estimate=pl.CostEstimate(flops=0, bytes_accessed=6 << 20, transcendentals=0),
        name="group_moments",
    )(*rows_here, panel, *after)
    return outs[0:2], outs[2:4]


def moments(plan, rows_here, first, second, stats, split, after):
    rows = first.shape[1] // 4
    sums = (first.shape[0] + second.shape[0] // 2, plan.width)
    if split:
        out_shape = [jax.ShapeDtypeStruct(sums, jnp.float32)] * plan.places
    else:
        out_shape = [jax.ShapeDtypeStruct((plan.places // 2,) + sums, jnp.float32)] * 2
    return pl.pallas_call(
        functools.partial(moments_kernel, rows, plan.places if split else None),
        in_specs=[pl.BlockSpec(memory_space=pltpu.VMEM)] * 7
        + [pl.BlockSpec(memory_space=pl.ANY)] * len(after),
        out_specs=[pl.BlockSpec(memory_space=pltpu.VMEM)] * len(out_shape),
        out_shape=out_shape,
        compiler_params=pltpu.CompilerParams(vmem_limit_bytes=20 << 20),
        cost_estimate=pl.CostEstimate(flops=0, bytes_accessed=6 << 20, transcendentals=0),
        name="moments",
    )(*rows_here, first, second, stats, *after)


def finish_kernel(plan, weightings, counts, pick_ref, stats_ref, *refs):
    out_ref, ring_ref = refs[-2:]
    comps = pick_ref.shape[0]
    onehot = onehot_of(pick_ref, weightings, jnp.float32)
    inverse_target = stats_ref[0][:, 0:1]
    inverse_other = stats_ref[1][:, 0:1]
    light = stats_ref[2][:, 0:1] > 0.5
    me = lax.axis_index("pat")
    for away, count in enumerate(counts):
        sums = refs[0][...]
        for more in refs[1:count]:
            sums += more[...]
        refs = refs[count:]
        target, other = both_arms(sums, onehot, light)
        spread = sums[comps + weightings:2 * comps + weightings]
        mean_target = target * inverse_target
        mean_other = other * inverse_other
        variance = spread - mean_target * mean_target - mean_other * mean_other
        pooled = jnp.maximum(variance / 2.0, 0.01)
        balance = (mean_target - mean_other) / jnp.sqrt(pooled)
        for side in range(2):
            count = plan.tiles - plan.share if side else plan.share
            if count:
                lanes = slice(side * plan.width, side * plan.width + count * LANES)

                @pl.when((me & 1) ^ away == side)
                def _():
                    ring_ref[:, lanes] = balance[:, 0:count * LANES]
    width = plan.tiles * LANES
    shift = width - lax.rem(me * plan.block, LANES)
    out_ref[:, 0, :] = pltpu.roll(ring_ref[...], shift, 1)[:, 0:plan.block]


def finish(plan, parts, pick_column, stats, weightings):
    comps = pick_column.shape[0]
    operands = [array for part in parts for array in part]
    return pl.pallas_call(
        functools.partial(finish_kernel, plan, weightings, [len(part) for part in parts]),
        in_specs=[pl.BlockSpec(memory_space=pltpu.VMEM)] * (2 + len(operands)),
        out_specs=pl.BlockSpec(memory_space=pltpu.VMEM),
        out_shape=jax.ShapeDtypeStruct((comps, 1, plan.block), jnp.float32),
        scratch_shapes=[pltpu.VMEM((comps, plan.tiles * LANES), jnp.float32)],
        compiler_params=pltpu.CompilerParams(vmem_limit_bytes=12 << 20),
        cost_estimate=pl.CostEstimate(flops=0, bytes_accessed=1 << 14, transcendentals=0),
        name="finish",
    )(pick_column, stats, *operands)


def swap(array, pairs):
    return lax.ppermute(array, "pat", pairs)


def on_device(n, covs, covariates, weights, arms, pick):
    weightings = weights.shape[1]
    pick_column = pick.reshape(pick.shape[0], 1)
    plan = Plan(n, covariates.shape[1] // n)
    to_other_side = plan.by_mask(1)

    arm_rows = arms.T.astype(weights.dtype)
    if covs > 1:
        arm_rows = lax.all_gather(arm_rows, "cov", axis=0, tiled=True)
    mine = jnp.concatenate([weights.T, arm_rows], axis=0)
    near = jnp.stack([mine, swap(mine, to_other_side)])
    far = swap(near, [(pair ^ 1, d) for d, pair in plan.by_rows()])

    kept0, kept1, sent0, sent1, other0, other1 = pack(covariates, plan)
    rows_here = {}
    for chunk, kept, sent, other in ((1, kept1, sent1, other1), (0, kept0, sent0, other0)):
        passed = swap(other, to_other_side)
        rows_here[chunk] = [
            kept, passed, swap(sent, plan.by_rows()), swap(passed[1], plan.by_rows())
        ]

    near_totals, panel = make_group(near, far, pick_column, weightings)
    far_totals = swap(near_totals, plan.by_sums())
    totals = near_totals + far_totals
    for mask in range(8, n, 8):
        for more in (mask, mask | 4):
            totals = totals + swap(near_totals, plan.by_mask(more)[0::2])
    told = swap(totals, to_other_side[0::2])
    first, second, stats = make_panels(near, far, totals, told, pick_column, weightings)

    across, top, after = [], [], [rows_here[0][2]]
    for even, odd in group_moments(plan, rows_here[1], panel, [totals]):
        arrived = swap(odd, plan.by_sums())
        met = meet(pick_column, near_totals, far_totals, stats, even, arrived, after)
        for bit in plan.middle_bits:
            met = met[0::2] + swap(met[1::2], plan.by_mask(1 << bit))
        across.append(met)
        top.append(swap(met, plan.by_mask(1 << plan.top_bit))[0])
        after = []

    last = not plan.middle_bits
    sums = moments(plan, rows_here[0], first, second, stats, last, across)
    if last:
        even, odd = sums[0::2], sums[1::2]
        other_owner = [(d, pair ^ 1) for d, pair in plan.by_sums()]
        parts = [
            [even[0], top[0], swap(odd[0], plan.by_sums())],
            [swap(even[1] + top[1], to_other_side), swap(odd[1], other_owner)],
        ]
    else:
        even, odd = sums
        arrived = swap(odd, plan.by_sums())
        for bit in plan.middle_bits:
            odd = even[1::2] + arrived[1::2]
            even = even[0::2] + arrived[0::2]
            arrived = swap(odd, plan.by_mask(1 << bit))
        total = [even[side] + arrived[side] + top[side] for side in range(2)]
        parts = [[total[0]], [swap(total[1], to_other_side)]]
    return finish(plan, parts, pick_column, stats, weightings)


def solution(mesh):
    placed = (
        P(("groups", "pat"), "cov"),
        P(("groups", "pat"), None),
        P(("groups", "pat"), "cov"),
        P(),
    )
    body = functools.partial(on_device, mesh.shape["pat"], mesh.shape["cov"])
    return jax.shard_map(
        body, mesh=mesh, in_specs=placed, out_specs=P("groups", "cov", "pat"), check_vma=False
    )
```

```python
import functools

import jax
import jax.numpy as jnp
from jax import lax
from jax.experimental import pallas as pl
from jax.experimental.pallas import tpu as pltpu
from jax.sharding import PartitionSpec as P

LANES = 128


def round_up(value, multiple):
    return -(-value // multiple) * multiple


class Plan:
    def __init__(self, n, block):
        self.n = n
        self.block = block
        self.tiles = round_up(block, LANES) // LANES
        self.share = (self.tiles + 1) // 2
        self.width = self.share * LANES
        self.places = n // 4
        *self.middle_bits, self.top_bit = range(3, n.bit_length() - 1)

    def by_rows(self):
        return [(d, d ^ (2 + 2 * (d & 1))) for d in range(self.n)]

    def by_sums(self):
        return [(d, d ^ (4 - 2 * (d & 1))) for d in range(self.n)]

    def by_mask(self, mask):
        return [(d, d ^ mask) for d in range(self.n)]


def pack_kernel(
    plan, x_ref, kept0_ref, kept1_ref, sent0_ref, rest_ref, sent1_ref, other0_ref, other1_ref
):
    step = pl.program_id(0)
    me = lax.axis_index("pat")
    rows, columns = x_ref.shape
    last_tile = columns // LANES - 1
    lane = lax.broadcasted_iota(jnp.int32, (rows, LANES), 1)

    def tile(index):
        return pl.ds(pl.multiple_of(jnp.minimum(index, last_tile) * LANES, LANES), LANES)

    for away in range(2):
        side = (me & 1) ^ away
        holder = me ^ away
        for sent in range(2):
            for chunk in range(2):
                middle = len(plan.middle_bits)
                far_owner = step >> (1 + middle)
                way = side if chunk else side * (1 - far_owner)
                relative = (
                    far_owner
                    | (sent << (1 + way))
                    | ((step & 1) << (2 - way))
                    | (((step >> 1) & ((1 << middle) - 1)) << 3)
                    | (chunk << plan.top_bit)
                )
                column = (holder ^ relative) * plan.block
                first = column // LANES
                edge = (column - first * LANES) * (1 - side)
                head = x_ref[:, tile(first + side * plan.share)]
                tail = x_ref[:, tile(first + plan.tiles)]
                folded = jnp.where(lane >= edge, head.astype(jnp.float32), tail.astype(jnp.float32))

                def write(target):
                    target[:, 0:LANES] = folded.astype(x_ref.dtype)
                    for slot in range(1, plan.share):
                        here = slice(slot * LANES, (slot + 1) * LANES)
                        target[:, here] = x_ref[:, tile(first + side * plan.share + slot)]

                if away:
                    write((other0_ref, other1_ref)[chunk].at[sent])
                elif not sent:
                    write((kept0_ref, kept1_ref)[chunk])
                elif chunk:
                    write(sent1_ref)
                else:
                    for half, ref in enumerate((sent0_ref, rest_ref)):

                        @pl.when(far_owner == half)
                        def _():
                            write(ref)


def pack(covariates, plan):
    rows = covariates.shape[0]
    dtype = covariates.dtype
    length = plan.places * rows
    mine = jax.ShapeDtypeStruct((length, plan.width), dtype)
    other = jax.ShapeDtypeStruct((2, length, plan.width), dtype)
    mine_spec = pl.BlockSpec((rows, plan.width), lambda s: (s, 0))
    half = plan.places // 2
    part = jax.ShapeDtypeStruct((half * rows, plan.width), dtype)
    part_specs = [
        pl.BlockSpec((rows, plan.width), lambda s: (jnp.minimum(s, half - 1), 0)),
        pl.BlockSpec((rows, plan.width), lambda s: (jnp.maximum(s - half, 0), 0)),
    ]
    other_spec = pl.BlockSpec((2, rows, plan.width), lambda s: (0, s, 0))
    return pl.pallas_call(
        functools.partial(pack_kernel, plan),
        grid=(plan.places,),
        in_specs=[pl.BlockSpec(memory_space=pltpu.VMEM)],
        out_specs=[mine_spec] * 2 + part_specs + [mine_spec] + [other_spec] * 2,
        out_shape=[mine] * 2 + [part] * 2 + [mine] + [other] * 2,
        compiler_params=pltpu.CompilerParams(vmem_limit_bytes=12 << 20),
        cost_estimate=pl.CostEstimate(
            flops=0, bytes_accessed=4 * covariates.size, transcendentals=0
        ),
        name="pack",
    )(covariates)


def onehot_of(pick_ref, weightings, dtype):
    index = lax.broadcasted_iota(jnp.int32, (pick_ref.shape[0], weightings), 1)
    return jnp.where(index == pick_ref[...], 1.0, 0.0).astype(dtype)


def arm_columns(panel_ref, onehot):
    comps, weightings = onehot.shape
    weights = panel_ref[0:weightings, :]
    arms = panel_ref[weightings:weightings + comps, :].astype(jnp.float32)
    picked = jnp.dot(onehot, weights, preferred_element_type=jnp.float32)
    return weights, picked * arms, picked * (1.0 - arms)


def small_call(kernel, shapes, operands, after, name):
    vmem = pl.BlockSpec(memory_space=pltpu.VMEM)
    return pl.pallas_call(
        kernel,
        in_specs=[vmem] * len(operands) + [pl.BlockSpec(memory_space=pl.ANY)] * len(after),
        out_specs=[vmem] * len(shapes),
        out_shape=[jax.ShapeDtypeStruct(shape, dtype) for shape, dtype in shapes],
        compiler_params=pltpu.CompilerParams(vmem_limit_bytes=8 << 20),
        cost_estimate=pl.CostEstimate(flops=0, bytes_accessed=1 << 14, transcendentals=0),
        name=name,
    )(*operands, *after)


def lighter_of(totals):
    return jnp.where(totals[:, 0:1] <= totals[:, 1:2], 1.0, 0.0)


def lighter_panel(ref, members, onehot, light):
    comps, weightings = onehot.shape
    columns = []
    for place, member in enumerate(members):
        weights, target, other = arm_columns(member, onehot)
        here = slice(place * LANES, (place + 1) * LANES)
        lighter = light * target + (1.0 - light) * other
        ref[0:comps, here] = lighter.astype(jnp.bfloat16)
        ref[comps:comps + weightings, here] = weights
        columns.append((target, other))
    return columns


def members_of(near_ref, far_ref):
    return (near_ref.at[0], near_ref.at[1], far_ref.at[1], far_ref.at[0])


def group_kernel(weightings, pick_ref, near_ref, far_ref, *refs):
    totals_ref, panel_ref = refs[-2:]
    onehot = onehot_of(pick_ref, weightings, jnp.bfloat16)
    target_sum, other_sum = 0.0, 0.0
    for member in members_of(near_ref, far_ref):
        _, target, other = arm_columns(member, onehot)
        target_sum += target
        other_sum += other
    lane = lax.broadcasted_iota(jnp.int32, totals_ref.shape, 1)
    totals = jnp.where(
        lane == 0,
        jnp.sum(target_sum, axis=1, keepdims=True),
        jnp.sum(other_sum, axis=1, keepdims=True),
    )
    totals_ref[...] = totals
    lighter_panel(panel_ref, members_of(near_ref, far_ref), onehot, lighter_of(totals))


def make_group(near, far, pick_column, weightings, after):
    comps = pick_column.shape[0]
    return small_call(
        functools.partial(group_kernel, weightings),
        [((comps, LANES), jnp.float32), ((comps + weightings, 4 * LANES), jnp.bfloat16)],
        [pick_column, near, far],
        after,
        "group",
    )


def panel_kernel(weightings, pick_ref, near_ref, far_ref, here_ref, told_ref, *refs):
    first_ref, second_ref, stats_ref = refs
    comps = pick_ref.shape[0]
    onehot = onehot_of(pick_ref, weightings, jnp.bfloat16)
    side = jnp.full(here_ref.shape, lax.axis_index("pat") & 1)
    totals = jnp.where(side == 0, here_ref[...], told_ref[...])
    light = lighter_of(totals)
    stats_ref[0] = jnp.broadcast_to(1.0 / totals[:, 0:1], (comps, LANES))
    stats_ref[1] = jnp.broadcast_to(1.0 / totals[:, 1:2], (comps, LANES))
    stats_ref[2] = jnp.broadcast_to(light, (comps, LANES))
    columns = lighter_panel(first_ref, members_of(near_ref, far_ref), onehot, light)
    for place, (target, other) in enumerate(columns):
        here = slice(place * LANES, (place + 1) * LANES)
        second_ref[0:comps, here] = target.astype(jnp.bfloat16)
        second_ref[comps:2 * comps, here] = other.astype(jnp.bfloat16)


def make_panels(near, far, totals, told, pick_column, weightings):
    comps = pick_column.shape[0]
    return small_call(
        functools.partial(panel_kernel, weightings),
        [
            ((comps + weightings, 4 * LANES), jnp.bfloat16),
            ((2 * comps, 4 * LANES), jnp.bfloat16),
            ((3, comps, LANES), jnp.float32),
        ],
        [pick_column, near, far, totals, told],
        [],
        "panels",
    )


def rest_kernel(weightings, pick_ref, near_ref, far_ref, stats_ref, first_ref, second_ref):
    comps = pick_ref.shape[0]
    onehot = onehot_of(pick_ref, weightings, jnp.bfloat16)
    light = stats_ref[2][:, 0:1]
    columns = lighter_panel(first_ref, members_of(near_ref, far_ref), onehot, light)
    for place, (target, other) in enumerate(columns):
        here = slice(place * LANES, (place + 1) * LANES)
        second_ref[0:comps, here] = target.astype(jnp.bfloat16)
        second_ref[comps:2 * comps, here] = other.astype(jnp.bfloat16)


def rest_panels(near, far, stats, pick_column, weightings):
    comps = pick_column.shape[0]
    return small_call(
        functools.partial(rest_kernel, weightings),
        [
            ((comps + weightings, 4 * LANES), jnp.bfloat16),
            ((2 * comps, 4 * LANES), jnp.bfloat16),
        ],
        [pick_column, near, far, stats],
        [],
        "rest_panels",
    )


def both_arms(sums, onehot, light):
    comps, weightings = onehot.shape
    lighter = sums[0:comps]
    both = jnp.dot(
        onehot,
        sums[comps:comps + weightings],
        precision=lax.Precision.HIGHEST,
        preferred_element_type=jnp.float32,
    )
    target = jnp.where(light, lighter, both - lighter)
    return target, jnp.where(light, both - lighter, lighter)


def meet_kernel(pick_ref, near_ref, far_ref, stats_ref, left_ref, right_ref, *refs):
    out_ref = refs[-1]
    comps = pick_ref.shape[0]
    rows = left_ref.shape[1] // 2
    onehot = onehot_of(pick_ref, rows - comps, jnp.float32)
    light = stats_ref[2][:, 0:1] > 0.5
    for block in range(left_ref.shape[0]):
        arms = []
        for moment in range(2):
            here = slice(moment * rows, (moment + 1) * rows)
            target, other = 0.0, 0.0
            for ref, totals_ref in ((left_ref, near_ref), (right_ref, far_ref)):
                more = both_arms(ref[block, here, :], onehot, lighter_of(totals_ref[...]) > 0.5)
                target, other = target + more[0], other + more[1]
            arms.append((target, other))
        out_ref[block, 0:comps, :] = jnp.where(light, arms[0][0], arms[0][1])
        out_ref[block, comps:rows, :] = (
            left_ref[block, comps:rows, :] + right_ref[block, comps:rows, :]
        )
        out_ref[block, rows:rows + comps, :] = (
            arms[1][0] * stats_ref[0][:, 0:1] + arms[1][1] * stats_ref[1][:, 0:1]
        )


def meet(pick_column, near_totals, far_totals, stats, left, right, after):
    blocks, rows, width = left.shape
    out = (blocks, rows // 2 + pick_column.shape[0], width)
    return small_call(
        meet_kernel,
        [(out, jnp.float32)],
        [pick_column, near_totals, far_totals, stats, left, right],
        after,
        "meet",
    )[0]


def whole_spec(shape):
    return pl.BlockSpec(shape, lambda s: (0,) * len(shape))


def group_moments_kernel(rows, count, *refs):
    kept_ref, passed_ref, *swapped_refs, panel_ref = refs[:5]
    outs = refs[-2 * count:]
    height = panel_ref.shape[0]
    places = kept_ref.shape[0] // rows
    for place in range(places):
        here = slice(place * rows, (place + 1) * rows)
        x = jnp.concatenate(
            [kept_ref[here, :], passed_ref[0, here, :]]
            + [ref[here, :] for ref in swapped_refs],
            axis=0,
        )
        squares = (x.astype(jnp.float32) * x.astype(jnp.float32)).astype(jnp.bfloat16)
        owner_side, middle = divmod(place // 2, places // 2 // count)
        out = outs[2 * owner_side + place % 2].at[middle]
        out[0:height, :] = jnp.dot(panel_ref[...], x, preferred_element_type=jnp.float32)
        out[height:2 * height, :] = jnp.dot(
            panel_ref[...], squares, preferred_element_type=jnp.float32
        )


def group_moments(plan, rows_here, panel, after):
    rows = panel.shape[1] // 4
    out = jax.ShapeDtypeStruct(
        (plan.places // 4, 2 * panel.shape[0], plan.width), jnp.float32
    )
    outs = pl.pallas_call(
        functools.partial(group_moments_kernel, rows, 2),
        in_specs=[pl.BlockSpec(memory_space=pltpu.VMEM)] * 5
        + [pl.BlockSpec(memory_space=pl.ANY)] * len(after),
        out_specs=[pl.BlockSpec(memory_space=pltpu.VMEM)] * 4,
        out_shape=[out] * 4,
        compiler_params=pltpu.CompilerParams(vmem_limit_bytes=20 << 20),
        cost_estimate=pl.CostEstimate(flops=0, bytes_accessed=6 << 20, transcendentals=0),
        name="group_moments",
    )(*rows_here, panel, *after)
    return outs[0:2], outs[2:4]


def moments_kernel(rows, half, kept_ref, passed_ref, swapped_ref, *refs):
    first_ref, second_ref, stats_ref = refs[:3]
    outs = refs[-2:]
    first_rows = first_ref.shape[0]
    comps = second_ref.shape[0] // 2
    inverse_target = stats_ref[0][:, 0:1]
    inverse_other = stats_ref[1][:, 0:1]
    places = swapped_ref.shape[1] // rows
    for place in range(places):
        here = slice(place * rows, (place + 1) * rows)
        there = slice((half * places + place) * rows, (half * places + place + 1) * rows)
        x = jnp.concatenate(
            [
                kept_ref[there, :],
                passed_ref[0, there, :],
                swapped_ref[0, here, :],
                swapped_ref[1, here, :],
            ],
            axis=0,
        )
        first = jnp.dot(first_ref[...], x, preferred_element_type=jnp.float32)
        squares = (x.astype(jnp.float32) * x.astype(jnp.float32)).astype(jnp.bfloat16)
        second = jnp.dot(second_ref[...], squares, preferred_element_type=jnp.float32)
        out = outs[place % 2].at[place // 2]
        out[0:first_rows, :] = first
        out[first_rows:first_rows + comps, :] = (
            second[0:comps] * inverse_target + second[comps:2 * comps] * inverse_other
        )


def moments(plan, half, kept, passed, swapped, first, second, stats, after):
    rows = first.shape[1] // 4
    out_rows = first.shape[0] + second.shape[0] // 2
    out = jax.ShapeDtypeStruct((plan.places // 4, out_rows, plan.width), jnp.float32)
    return pl.pallas_call(
        functools.partial(moments_kernel, rows, half),
        in_specs=[pl.BlockSpec(memory_space=pltpu.VMEM)] * 6
        + [pl.BlockSpec(memory_space=pl.ANY)] * len(after),
        out_specs=[pl.BlockSpec(memory_space=pltpu.VMEM)] * 2,
        out_shape=[out] * 2,
        compiler_params=pltpu.CompilerParams(vmem_limit_bytes=20 << 20),
        cost_estimate=pl.CostEstimate(flops=0, bytes_accessed=3 << 20, transcendentals=0),
        name="moments",
    )(kept, passed, swapped, first, second, stats, *after)


def finish_kernel(plan, weightings, counts, pick_ref, stats_ref, *refs):
    out_ref, ring_ref = refs[-2:]
    comps = pick_ref.shape[0]
    onehot = onehot_of(pick_ref, weightings, jnp.float32)
    inverse_target = stats_ref[0][:, 0:1]
    inverse_other = stats_ref[1][:, 0:1]
    light = stats_ref[2][:, 0:1] > 0.5
    me = lax.axis_index("pat")
    for away, count in enumerate(counts):
        sums = refs[0][...]
        for more in refs[1:count]:
            sums += more[...]
        refs = refs[count:]
        target, other = both_arms(sums, onehot, light)
        spread = sums[comps + weightings:2 * comps + weightings]
        mean_target = target * inverse_target
        mean_other = other * inverse_other
        variance = spread - mean_target * mean_target - mean_other * mean_other
        pooled = jnp.maximum(variance / 2.0, 0.01)
        balance = (mean_target - mean_other) / jnp.sqrt(pooled)
        for side in range(2):
            count = plan.tiles - plan.share if side else plan.share
            if count:
                lanes = slice(side * plan.width, side * plan.width + count * LANES)

                @pl.when((me & 1) ^ away == side)
                def _():
                    ring_ref[:, lanes] = balance[:, 0:count * LANES]
    width = plan.tiles * LANES
    shift = width - lax.rem(me * plan.block, LANES)
    out_ref[:, 0, :] = pltpu.roll(ring_ref[...], shift, 1)[:, 0:plan.block]


def finish(plan, parts, pick_column, stats, weightings):
    comps = pick_column.shape[0]
    operands = [array for part in parts for array in part]
    return pl.pallas_call(
        functools.partial(finish_kernel, plan, weightings, [len(part) for part in parts]),
        in_specs=[pl.BlockSpec(memory_space=pltpu.VMEM)] * (2 + len(operands)),
        out_specs=pl.BlockSpec(memory_space=pltpu.VMEM),
        out_shape=jax.ShapeDtypeStruct((comps, 1, plan.block), jnp.float32),
        scratch_shapes=[pltpu.VMEM((comps, plan.tiles * LANES), jnp.float32)],
        compiler_params=pltpu.CompilerParams(vmem_limit_bytes=12 << 20),
        cost_estimate=pl.CostEstimate(flops=0, bytes_accessed=1 << 14, transcendentals=0),
        name="finish",
    )(pick_column, stats, *operands)


def hold_kernel(*refs):
    del refs


def hold(array, after):
    any_space = pl.BlockSpec(memory_space=pl.ANY)
    return pl.pallas_call(
        hold_kernel,
        in_specs=[any_space] * (1 + len(after)),
        out_specs=any_space,
        out_shape=jax.ShapeDtypeStruct(array.shape, array.dtype),
        input_output_aliases={0: 0},
        compiler_params=pltpu.CompilerParams(vmem_limit_bytes=1 << 20),
        cost_estimate=pl.CostEstimate(flops=0, bytes_accessed=0, transcendentals=0),
        name="hold",
    )(array, *after)


def swap(array, pairs):
    return lax.ppermute(array, "pat", pairs)


def on_device(n, covs, covariates, weights, arms, pick):
    weightings = weights.shape[1]
    pick_column = pick.reshape(pick.shape[0], 1)
    plan = Plan(n, covariates.shape[1] // n)
    to_other_side = plan.by_mask(1)

    arm_rows = arms.T.astype(weights.dtype)
    if covs > 1:
        arm_rows = lax.all_gather(arm_rows, "cov", axis=0, tiled=True)
    mine = jnp.concatenate([weights.T, arm_rows], axis=0)
    kept0, kept1, sent0, rest, sent1, other0, other1 = pack(covariates, plan)
    passed1 = swap(other1, to_other_side)
    rows1 = [kept1, passed1, swap(sent1, plan.by_rows()), swap(passed1[1], plan.by_rows())]
    passed0 = swap(other0, to_other_side)
    length = rest.shape[0]
    swapped0 = swap(jnp.stack([sent0, passed0[1, :length]]), plan.by_rows())

    near = jnp.stack([mine, swap(hold(mine, [passed1]), to_other_side)])
    far = swap(near, [(pair ^ 1, d) for d, pair in plan.by_rows()])

    far_rest = swap(near, plan.by_mask(3))

    near_totals, panel = make_group(near, far, pick_column, weightings, [far_rest, rows1[2]])
    far_totals = swap(near_totals, plan.by_sums())
    totals = near_totals + far_totals
    for mask in range(8, n, 8):
        for more in (mask, mask | 4):
            totals = totals + swap(near_totals, plan.by_mask(more)[0::2])
    told = swap(totals, to_other_side[0::2])
    first, second, stats = make_panels(near, far, totals, told, pick_column, weightings)

    across, top, after = [], [], [swapped0]
    sums = group_moments(plan, rows1, panel, [totals])
    for even, odd in sums:
        arrived = swap(odd, plan.by_sums())
        met = meet(pick_column, near_totals, far_totals, stats, even, arrived, after)
        for bit in plan.middle_bits:
            met = met[0::2] + swap(met[1::2], plan.by_mask(1 << bit))
        across.append(met)
        top.append(swap(met, plan.by_mask(1 << plan.top_bit))[0])
        after = []

    rest = hold(jnp.stack([rest, passed0[1, length:]]), [sums[0][0]])
    swapped_rest = swap(rest, plan.by_mask(2))
    first_rest, second_rest = rest_panels(near, far_rest, stats, pick_column, weightings)

    even, odd = moments(
        plan, 0, kept0, passed0, swapped0, first, second, stats, across
    )
    even_rest, odd_rest = moments(
        plan, 1, kept0, passed0, swapped_rest, first_rest, second_rest, stats, [even]
    )
    if plan.middle_bits:
        for half, pairs in ((0, plan.by_sums()), (1, plan.by_mask(4))):
            here, there = ((even, odd), (even_rest, odd_rest))[half]
            met = here + swap(there, pairs)
            for bit in plan.middle_bits:
                met = met[0::2] + swap(met[1::2], plan.by_mask(1 << bit))
            top[half] = top[half] + met[0]
        parts = [[top[0]], [swap(top[1], to_other_side)]]
    else:
        parts = [
            [even[0], top[0], swap(odd, plan.by_sums())[0]],
            [swap(even_rest[0] + top[1], to_other_side), swap(odd_rest, plan.by_mask(5))[0]],
        ]
    return finish(plan, parts, pick_column, stats, weightings)


def solution(mesh):
    placed = (
        P(("groups", "pat"), "cov"),
        P(("groups", "pat"), None),
        P(("groups", "pat"), "cov"),
        P(),
    )
    body = functools.partial(on_device, mesh.shape["pat"], mesh.shape["cov"])
    return jax.shard_map(
        body, mesh=mesh, in_specs=placed, out_specs=P("groups", "cov", "pat"), check_vma=False
    )
```

```python
import functools

import jax
import jax.numpy as jnp
from jax import lax
from jax.experimental import pallas as pl
from jax.experimental.pallas import tpu as pltpu
from jax.sharding import PartitionSpec as P

LANES = 128


def round_up(value, multiple):
    return -(-value // multiple) * multiple


class Plan:
    def __init__(self, n, block):
        self.n = n
        self.block = block
        self.tiles = round_up(block, LANES) // LANES
        self.share = (self.tiles + 1) // 2
        self.width = self.share * LANES
        self.places = n // 4
        *self.middle_bits, self.top_bit = range(3, n.bit_length() - 1)

    def by_rows(self):
        return [(d, d ^ (2 + 2 * (d & 1))) for d in range(self.n)]

    def by_sums(self):
        return [(d, d ^ (4 - 2 * (d & 1))) for d in range(self.n)]

    def by_mask(self, mask):
        return [(d, d ^ mask) for d in range(self.n)]


def pack_kernel(
    plan, x_ref, kept0_ref, kept1_ref, sent0_ref, sent1_ref, other0_ref, other1_ref
):
    me = lax.axis_index("pat")
    rows, columns = x_ref.shape
    last_tile = columns // LANES - 1
    lane = lax.broadcasted_iota(jnp.int32, (rows, LANES), 1)

    def tile(index):
        return pl.ds(pl.multiple_of(jnp.minimum(index, last_tile) * LANES, LANES), LANES)

    @pl.loop(0, plan.places)
    def _(step):
        here = pl.ds(pl.multiple_of(step * rows, rows), rows)
        for away in range(2):
            side = (me & 1) ^ away
            holder = me ^ away
            for sent in range(2):
                for chunk in range(2):
                    middle = len(plan.middle_bits)
                    relative = (
                        (step >> (1 + middle))
                        | (sent << (1 + side))
                        | ((step & 1) << (2 - side))
                        | (((step >> 1) & ((1 << middle) - 1)) << 3)
                        | (chunk << plan.top_bit)
                    )
                    column = (holder ^ relative) * plan.block
                    first = column // LANES
                    edge = (column - first * LANES) * (1 - side)
                    head = x_ref[:, tile(first + side * plan.share)]
                    tail = x_ref[:, tile(first + plan.tiles)]
                    folded = jnp.where(lane >= edge, head.astype(jnp.float32), tail.astype(jnp.float32))
                    if away:
                        target = (other0_ref, other1_ref)[chunk].at[sent, here]
                    elif sent:
                        target = (sent0_ref, sent1_ref)[chunk].at[here]
                    else:
                        target = (kept0_ref, kept1_ref)[chunk].at[here]
                    target[:, 0:LANES] = folded.astype(x_ref.dtype)
                    for slot in range(1, plan.share):
                        lanes = slice(slot * LANES, (slot + 1) * LANES)
                        target[:, lanes] = x_ref[:, tile(first + side * plan.share + slot)]


def pack(covariates, plan):
    rows = covariates.shape[0]
    dtype = covariates.dtype
    length = plan.places * rows
    mine = jax.ShapeDtypeStruct((length, plan.width), dtype)
    other = jax.ShapeDtypeStruct((2, length, plan.width), dtype)
    return pl.pallas_call(
        functools.partial(pack_kernel, plan),
        in_specs=[pl.BlockSpec(memory_space=pltpu.VMEM)],
        out_specs=[pl.BlockSpec(memory_space=pltpu.VMEM)] * 6,
        out_shape=[mine] * 4 + [other] * 2,
        compiler_params=pltpu.CompilerParams(vmem_limit_bytes=8 << 20),
        cost_estimate=pl.CostEstimate(
            flops=0, bytes_accessed=4 * covariates.size, transcendentals=0
        ),
        name="pack",
    )(covariates)


def onehot_of(pick_ref, weightings, dtype):
    index = lax.broadcasted_iota(jnp.int32, (pick_ref.shape[0], weightings), 1)
    return jnp.where(index == pick_ref[...], 1.0, 0.0).astype(dtype)


def arm_columns(panel_ref, onehot):
    comps, weightings = onehot.shape
    weights = panel_ref[0:weightings, :]
    arms = panel_ref[weightings:weightings + comps, :].astype(jnp.float32)
    picked = jnp.dot(onehot, weights, preferred_element_type=jnp.float32)
    return weights, picked * arms, picked * (1.0 - arms)


def small_call(kernel, shapes, operands, after, name):
    vmem = pl.BlockSpec(memory_space=pltpu.VMEM)
    return pl.pallas_call(
        kernel,
        in_specs=[vmem] * len(operands) + [pl.BlockSpec(memory_space=pl.ANY)] * len(after),
        out_specs=[vmem] * len(shapes),
        out_shape=[jax.ShapeDtypeStruct(shape, dtype) for shape, dtype in shapes],
        compiler_params=pltpu.CompilerParams(vmem_limit_bytes=8 << 20),
        cost_estimate=pl.CostEstimate(flops=0, bytes_accessed=1 << 14, transcendentals=0),
        name=name,
    )(*operands, *after)


def lighter_of(totals):
    return jnp.where(totals[:, 0:1] <= totals[:, 1:2], 1.0, 0.0)


def lighter_panel(ref, members, onehot, light):
    comps, weightings = onehot.shape
    columns = []
    for place, member in enumerate(members):
        weights, target, other = arm_columns(member, onehot)
        here = slice(place * LANES, (place + 1) * LANES)
        lighter = light * target + (1.0 - light) * other
        ref[0:comps, here] = lighter.astype(jnp.bfloat16)
        ref[comps:comps + weightings, here] = weights
        columns.append((target, other))
    return columns


def members_of(near_ref, far_ref):
    return (near_ref.at[0], near_ref.at[1], far_ref.at[1], far_ref.at[0])


def group_kernel(weightings, pick_ref, near_ref, far_ref, totals_ref, panel_ref):
    onehot = onehot_of(pick_ref, weightings, jnp.bfloat16)
    target_sum, other_sum = 0.0, 0.0
    for member in members_of(near_ref, far_ref):
        _, target, other = arm_columns(member, onehot)
        target_sum += target
        other_sum += other
    lane = lax.broadcasted_iota(jnp.int32, totals_ref.shape, 1)
    totals = jnp.where(
        lane == 0,
        jnp.sum(target_sum, axis=1, keepdims=True),
        jnp.sum(other_sum, axis=1, keepdims=True),
    )
    totals_ref[...] = totals
    lighter_panel(panel_ref, members_of(near_ref, far_ref), onehot, lighter_of(totals))


def make_group(near, far, pick_column, weightings):
    comps = pick_column.shape[0]
    return small_call(
        functools.partial(group_kernel, weightings),
        [((comps, LANES), jnp.float32), ((comps + weightings, 4 * LANES), jnp.bfloat16)],
        [pick_column, near, far],
        [],
        "group",
    )


def panel_kernel(weightings, pick_ref, near_ref, far_ref, here_ref, told_ref, *refs):
    first_ref, second_ref, stats_ref = refs
    comps = pick_ref.shape[0]
    onehot = onehot_of(pick_ref, weightings, jnp.bfloat16)
    side = jnp.full(here_ref.shape, lax.axis_index("pat") & 1)
    totals = jnp.where(side == 0, here_ref[...], told_ref[...])
    light = lighter_of(totals)
    stats_ref[0] = jnp.broadcast_to(1.0 / totals[:, 0:1], (comps, LANES))
    stats_ref[1] = jnp.broadcast_to(1.0 / totals[:, 1:2], (comps, LANES))
    stats_ref[2] = jnp.broadcast_to(light, (comps, LANES))
    columns = lighter_panel(first_ref, members_of(near_ref, far_ref), onehot, light)
    for place, (target, other) in enumerate(columns):
        here = slice(place * LANES, (place + 1) * LANES)
        second_ref[0:comps, here] = target.astype(jnp.bfloat16)
        second_ref[comps:2 * comps, here] = other.astype(jnp.bfloat16)


def make_panels(near, far, totals, told, pick_column, weightings):
    comps = pick_column.shape[0]
    return small_call(
        functools.partial(panel_kernel, weightings),
        [
            ((comps + weightings, 4 * LANES), jnp.bfloat16),
            ((2 * comps, 4 * LANES), jnp.bfloat16),
            ((3, comps, LANES), jnp.float32),
        ],
        [pick_column, near, far, totals, told],
        [],
        "panels",
    )


def both_arms(sums, onehot, light):
    comps, weightings = onehot.shape
    lighter = sums[0:comps]
    both = jnp.dot(
        onehot,
        sums[comps:comps + weightings],
        precision=lax.Precision.HIGHEST,
        preferred_element_type=jnp.float32,
    )
    target = jnp.where(light, lighter, both - lighter)
    return target, jnp.where(light, both - lighter, lighter)


def meet_kernel(pick_ref, near_ref, far_ref, stats_ref, left_ref, right_ref, *refs):
    out_ref = refs[-1]
    comps = pick_ref.shape[0]
    rows = left_ref.shape[1] // 2
    onehot = onehot_of(pick_ref, rows - comps, jnp.float32)
    light = stats_ref[2][:, 0:1] > 0.5
    for block in range(left_ref.shape[0]):
        arms = []
        for moment in range(2):
            here = slice(moment * rows, (moment + 1) * rows)
            target, other = 0.0, 0.0
            for ref, totals_ref in ((left_ref, near_ref), (right_ref, far_ref)):
                more = both_arms(ref[block, here, :], onehot, lighter_of(totals_ref[...]) > 0.5)
                target, other = target + more[0], other + more[1]
            arms.append((target, other))
        out_ref[block, 0:comps, :] = jnp.where(light, arms[0][0], arms[0][1])
        out_ref[block, comps:rows, :] = (
            left_ref[block, comps:rows, :] + right_ref[block, comps:rows, :]
        )
        out_ref[block, rows:rows + comps, :] = (
            arms[1][0] * stats_ref[0][:, 0:1] + arms[1][1] * stats_ref[1][:, 0:1]
        )


def meet(pick_column, near_totals, far_totals, stats, left, right, after):
    blocks, rows, width = left.shape
    out = (blocks, rows // 2 + pick_column.shape[0], width)
    return small_call(
        meet_kernel,
        [(out, jnp.float32)],
        [pick_column, near_totals, far_totals, stats, left, right],
        after,
        "meet",
    )[0]


def whole_spec(shape):
    return pl.BlockSpec(shape, lambda s: (0,) * len(shape))


def moments_kernel(rows, split, *refs):
    kept_ref, passed_ref, *swapped_refs, first_ref, second_ref, stats_ref = refs[:7]
    outs = refs[-(2 if split is None else split):]
    first_rows = first_ref.shape[0]
    comps = second_ref.shape[0] // 2
    inverse_target = stats_ref[0][:, 0:1]
    inverse_other = stats_ref[1][:, 0:1]
    for place in range(swapped_refs[0].shape[0] // rows):
        here = slice(place * rows, (place + 1) * rows)
        x = jnp.concatenate(
            [kept_ref[here, :], passed_ref[0, here, :]]
            + [ref[here, :] for ref in swapped_refs],
            axis=0,
        )
        first = jnp.dot(first_ref[...], x, preferred_element_type=jnp.float32)
        squares = (x.astype(jnp.float32) * x.astype(jnp.float32)).astype(jnp.bfloat16)
        second = jnp.dot(second_ref[...], squares, preferred_element_type=jnp.float32)
        out = outs[place % 2].at[place // 2] if split is None else outs[place]
        out[0:first_rows, :] = first
        out[first_rows:first_rows + comps, :] = (
            second[0:comps] * inverse_target + second[comps:2 * comps] * inverse_other
        )


def group_moments_kernel(rows, count, *refs):
    kept_ref, passed_ref, *swapped_refs, panel_ref = refs[:5]
    outs = refs[-2 * count:]
    height = panel_ref.shape[0]
    places = kept_ref.shape[0] // rows
    for place in range(places):
        here = slice(place * rows, (place + 1) * rows)
        x = jnp.concatenate(
            [kept_ref[here, :], passed_ref[0, here, :]]
            + [ref[here, :] for ref in swapped_refs],
            axis=0,
        )
        squares = (x.astype(jnp.float32) * x.astype(jnp.float32)).astype(jnp.bfloat16)
        owner_side, middle = divmod(place // 2, places // 2 // count)
        out = outs[2 * owner_side + place % 2].at[middle]
        out[0:height, :] = jnp.dot(panel_ref[...], x, preferred_element_type=jnp.float32)
        out[height:2 * height, :] = jnp.dot(
            panel_ref[...], squares, preferred_element_type=jnp.float32
        )


def group_moments(plan, rows_here, panel, after):
    rows = panel.shape[1] // 4
    out = jax.ShapeDtypeStruct(
        (plan.places // 4, 2 * panel.shape[0], plan.width), jnp.float32
    )
    outs = pl.pallas_call(
        functools.partial(group_moments_kernel, rows, 2),
        in_specs=[pl.BlockSpec(memory_space=pltpu.VMEM)] * 5
        + [pl.BlockSpec(memory_space=pl.ANY)] * len(after),
        out_specs=[pl.BlockSpec(memory_space=pltpu.VMEM)] * 4,
        out_shape=[out] * 4,
        compiler_params=pltpu.CompilerParams(vmem_limit_bytes=10 << 20),
        cost_estimate=pl.CostEstimate(flops=0, bytes_accessed=6 << 20, transcendentals=0),
        name="group_moments",
    )(*rows_here, panel, *after)
    return outs[0:2], outs[2:4]


def moments(plan, rows_here, first, second, stats, split, after):
    rows = first.shape[1] // 4
    sums = (first.shape[0] + second.shape[0] // 2, plan.width)
    if split:
        out_shape = [jax.ShapeDtypeStruct(sums, jnp.float32)] * plan.places
    else:
        out_shape = [jax.ShapeDtypeStruct((plan.places // 2,) + sums, jnp.float32)] * 2
    return pl.pallas_call(
        functools.partial(moments_kernel, rows, plan.places if split else None),
        in_specs=[pl.BlockSpec(memory_space=pltpu.VMEM)] * 7
        + [pl.BlockSpec(memory_space=pl.ANY)] * len(after),
        out_specs=[pl.BlockSpec(memory_space=pltpu.VMEM)] * len(out_shape),
        out_shape=out_shape,
        compiler_params=pltpu.CompilerParams(vmem_limit_bytes=10 << 20),
        cost_estimate=pl.CostEstimate(flops=0, bytes_accessed=6 << 20, transcendentals=0),
        name="moments",
    )(*rows_here, first, second, stats, *after)


def finish_kernel(plan, weightings, counts, pick_ref, stats_ref, *refs):
    out_ref, ring_ref = refs[-2:]
    comps = pick_ref.shape[0]
    onehot = onehot_of(pick_ref, weightings, jnp.float32)
    inverse_target = stats_ref[0][:, 0:1]
    inverse_other = stats_ref[1][:, 0:1]
    light = stats_ref[2][:, 0:1] > 0.5
    me = lax.axis_index("pat")
    for away, count in enumerate(counts):
        sums = refs[0][...]
        for more in refs[1:count]:
            sums += more[...]
        refs = refs[count:]
        target, other = both_arms(sums, onehot, light)
        spread = sums[comps + weightings:2 * comps + weightings]
        mean_target = target * inverse_target
        mean_other = other * inverse_other
        variance = spread - mean_target * mean_target - mean_other * mean_other
        pooled = jnp.maximum(variance / 2.0, 0.01)
        balance = (mean_target - mean_other) / jnp.sqrt(pooled)
        for side in range(2):
            count = plan.tiles - plan.share if side else plan.share
            if count:
                lanes = slice(side * plan.width, side * plan.width + count * LANES)

                @pl.when((me & 1) ^ away == side)
                def _():
                    ring_ref[:, lanes] = balance[:, 0:count * LANES]
    width = plan.tiles * LANES
    shift = width - lax.rem(me * plan.block, LANES)
    out_ref[:, 0, :] = pltpu.roll(ring_ref[...], shift, 1)[:, 0:plan.block]


def finish(plan, parts, pick_column, stats, weightings):
    comps = pick_column.shape[0]
    operands = [array for part in parts for array in part]
    return pl.pallas_call(
        functools.partial(finish_kernel, plan, weightings, [len(part) for part in parts]),
        in_specs=[pl.BlockSpec(memory_space=pltpu.VMEM)] * (2 + len(operands)),
        out_specs=pl.BlockSpec(memory_space=pltpu.VMEM),
        out_shape=jax.ShapeDtypeStruct((comps, 1, plan.block), jnp.float32),
        scratch_shapes=[pltpu.VMEM((comps, plan.tiles * LANES), jnp.float32)],
        compiler_params=pltpu.CompilerParams(vmem_limit_bytes=8 << 20),
        cost_estimate=pl.CostEstimate(flops=0, bytes_accessed=1 << 14, transcendentals=0),
        name="finish",
    )(pick_column, stats, *operands)


def swap(array, pairs):
    return lax.ppermute(array, "pat", pairs)


def on_device(n, covs, covariates, weights, arms, pick):
    weightings = weights.shape[1]
    pick_column = pick.reshape(pick.shape[0], 1)
    plan = Plan(n, covariates.shape[1] // n)
    to_other_side = plan.by_mask(1)

    arm_rows = arms.T.astype(weights.dtype)
    if covs > 1:
        arm_rows = lax.all_gather(arm_rows, "cov", axis=0, tiled=True)
    mine = jnp.concatenate([weights.T, arm_rows], axis=0)
    near = jnp.stack([mine, swap(mine, to_other_side)])
    far = swap(near, [(pair ^ 1, d) for d, pair in plan.by_rows()])

    kept0, kept1, sent0, sent1, other0, other1 = pack(covariates, plan)
    rows_here = {}
    for chunk, kept, sent, other in ((1, kept1, sent1, other1), (0, kept0, sent0, other0)):
        passed = swap(other, to_other_side)
        rows_here[chunk] = [
            kept, passed, swap(sent, plan.by_rows()), swap(passed[1], plan.by_rows())
        ]

    near_totals, panel = make_group(near, far, pick_column, weightings)
    far_totals = swap(near_totals, plan.by_sums())
    totals = near_totals + far_totals
    for mask in range(8, n, 8):
        for more in (mask, mask | 4):
            totals = totals + swap(near_totals, plan.by_mask(more)[0::2])
    told = swap(totals, to_other_side[0::2])
    first, second, stats = make_panels(near, far, totals, told, pick_column, weightings)

    across, top, after = [], [], [rows_here[0][2]]
    for even, odd in group_moments(plan, rows_here[1], panel, [totals]):
        arrived = swap(odd, plan.by_sums())
        met = meet(pick_column, near_totals, far_totals, stats, even, arrived, after)
        for bit in plan.middle_bits:
            met = met[0::2] + swap(met[1::2], plan.by_mask(1 << bit))
        across.append(met)
        top.append(swap(met, plan.by_mask(1 << plan.top_bit))[0])
        after = []

    last = not plan.middle_bits
    sums = moments(plan, rows_here[0], first, second, stats, last, across)
    if last:
        even, odd = sums[0::2], sums[1::2]
        other_owner = [(d, pair ^ 1) for d, pair in plan.by_sums()]
        parts = [
            [even[0], top[0], swap(odd[0], plan.by_sums())],
            [swap(even[1] + top[1], to_other_side), swap(odd[1], other_owner)],
        ]
    else:
        even, odd = sums
        arrived = swap(odd, plan.by_sums())
        for bit in plan.middle_bits:
            odd = even[1::2] + arrived[1::2]
            even = even[0::2] + arrived[0::2]
            arrived = swap(odd, plan.by_mask(1 << bit))
        total = [even[side] + arrived[side] + top[side] for side in range(2)]
        parts = [[total[0]], [swap(total[1], to_other_side)]]
    return finish(plan, parts, pick_column, stats, weightings)


def solution(mesh):
    placed = (
        P(("groups", "pat"), "cov"),
        P(("groups", "pat"), None),
        P(("groups", "pat"), "cov"),
        P(),
    )
    body = functools.partial(on_device, mesh.shape["pat"], mesh.shape["cov"])
    return jax.shard_map(
        body, mesh=mesh, in_specs=placed, out_specs=P("groups", "cov", "pat"), check_vma=False
    )
```

```python
import functools

import jax
import jax.numpy as jnp
from jax import lax
from jax.experimental import pallas as pl
from jax.experimental.pallas import tpu as pltpu
from jax.sharding import PartitionSpec as P

LANES = 128


def round_up(value, multiple):
    return -(-value // multiple) * multiple


class Plan:
    def __init__(self, n, block):
        self.n = n
        self.block = block
        self.tiles = round_up(block, LANES) // LANES
        self.share = (self.tiles + 1) // 2
        self.width = self.share * LANES
        self.places = n // 4
        *self.middle_bits, self.top_bit = range(3, n.bit_length() - 1)

    def by_rows(self):
        return [(d, d ^ (2 + 2 * (d & 1))) for d in range(self.n)]

    def by_sums(self):
        return [(d, d ^ (4 - 2 * (d & 1))) for d in range(self.n)]

    def by_mask(self, mask):
        return [(d, d ^ mask) for d in range(self.n)]


def pack_kernel(
    plan, x_ref, kept0_ref, kept1_ref, sent0_ref, sent1_ref, other0_ref, other1_ref
):
    step = pl.program_id(0)
    me = lax.axis_index("pat")
    rows, columns = x_ref.shape
    last_tile = columns // LANES - 1
    lane = lax.broadcasted_iota(jnp.int32, (rows, LANES), 1)

    def tile(index):
        return pl.ds(pl.multiple_of(jnp.minimum(index, last_tile) * LANES, LANES), LANES)

    for away in range(2):
        side = (me & 1) ^ away
        holder = me ^ away
        for sent in range(2):
            for chunk in range(2):
                middle = len(plan.middle_bits)
                relative = (
                    (step >> (1 + middle))
                    | (sent << (1 + side))
                    | ((step & 1) << (2 - side))
                    | (((step >> 1) & ((1 << middle) - 1)) << 3)
                    | (chunk << plan.top_bit)
                )
                column = (holder ^ relative) * plan.block
                first = column // LANES
                edge = (column - first * LANES) * (1 - side)
                head = x_ref[:, tile(first + side * plan.share)]
                tail = x_ref[:, tile(first + plan.tiles)]
                folded = jnp.where(lane >= edge, head.astype(jnp.float32), tail.astype(jnp.float32))
                if away:
                    target = (other0_ref, other1_ref)[chunk].at[sent]
                elif sent:
                    target = (sent0_ref, sent1_ref)[chunk]
                else:
                    target = (kept0_ref, kept1_ref)[chunk]
                target[:, 0:LANES] = folded.astype(x_ref.dtype)
                for slot in range(1, plan.share):
                    here = slice(slot * LANES, (slot + 1) * LANES)
                    target[:, here] = x_ref[:, tile(first + side * plan.share + slot)]


def pack(covariates, plan):
    rows = covariates.shape[0]
    dtype = covariates.dtype
    length = plan.places * rows
    mine = jax.ShapeDtypeStruct((length, plan.width), dtype)
    other = jax.ShapeDtypeStruct((2, length, plan.width), dtype)
    mine_spec = pl.BlockSpec((rows, plan.width), lambda s: (s, 0))
    other_spec = pl.BlockSpec((2, rows, plan.width), lambda s: (0, s, 0))
    return pl.pallas_call(
        functools.partial(pack_kernel, plan),
        grid=(plan.places,),
        in_specs=[pl.BlockSpec(memory_space=pltpu.VMEM)],
        out_specs=[mine_spec] * 4 + [other_spec] * 2,
        out_shape=[mine] * 4 + [other] * 2,
        compiler_params=pltpu.CompilerParams(vmem_limit_bytes=12 << 20),
        cost_estimate=pl.CostEstimate(
            flops=0, bytes_accessed=4 * covariates.size, transcendentals=0
        ),
        name="pack",
    )(covariates)


def onehot_of(pick_ref, weightings, dtype):
    index = lax.broadcasted_iota(jnp.int32, (pick_ref.shape[0], weightings), 1)
    return jnp.where(index == pick_ref[...], 1.0, 0.0).astype(dtype)


def arm_columns(panel_ref, onehot):
    comps, weightings = onehot.shape
    weights = panel_ref[0:weightings, :]
    arms = panel_ref[weightings:weightings + comps, :].astype(jnp.float32)
    picked = jnp.dot(onehot, weights, preferred_element_type=jnp.float32)
    return weights, picked * arms, picked * (1.0 - arms)


def small_call(kernel, shapes, operands, after, name):
    vmem = pl.BlockSpec(memory_space=pltpu.VMEM)
    return pl.pallas_call(
        kernel,
        in_specs=[vmem] * len(operands) + [pl.BlockSpec(memory_space=pl.ANY)] * len(after),
        out_specs=[vmem] * len(shapes),
        out_shape=[jax.ShapeDtypeStruct(shape, dtype) for shape, dtype in shapes],
        compiler_params=pltpu.CompilerParams(vmem_limit_bytes=8 << 20),
        cost_estimate=pl.CostEstimate(flops=0, bytes_accessed=1 << 14, transcendentals=0),
        name=name,
    )(*operands, *after)


def lighter_of(totals):
    return jnp.where(totals[:, 0:1] <= totals[:, 1:2], 1.0, 0.0)


def lighter_panel(ref, members, onehot, light):
    comps, weightings = onehot.shape
    columns = []
    for place, member in enumerate(members):
        weights, target, other = arm_columns(member, onehot)
        here = slice(place * LANES, (place + 1) * LANES)
        lighter = light * target + (1.0 - light) * other
        ref[0:comps, here] = lighter.astype(jnp.bfloat16)
        ref[comps:comps + weightings, here] = weights
        columns.append((target, other))
    return columns


def members_of(near_ref, far_ref):
    return (near_ref.at[0], near_ref.at[1], far_ref.at[1], far_ref.at[0])


def group_kernel(weightings, pick_ref, near_ref, far_ref, totals_ref, panel_ref):
    onehot = onehot_of(pick_ref, weightings, jnp.bfloat16)
    target_sum, other_sum = 0.0, 0.0
    for member in members_of(near_ref, far_ref):
        _, target, other = arm_columns(member, onehot)
        target_sum += target
        other_sum += other
    lane = lax.broadcasted_iota(jnp.int32, totals_ref.shape, 1)
    totals = jnp.where(
        lane == 0,
        jnp.sum(target_sum, axis=1, keepdims=True),
        jnp.sum(other_sum, axis=1, keepdims=True),
    )
    totals_ref[...] = totals
    lighter_panel(panel_ref, members_of(near_ref, far_ref), onehot, lighter_of(totals))


def make_group(near, far, pick_column, weightings):
    comps = pick_column.shape[0]
    return small_call(
        functools.partial(group_kernel, weightings),
        [((comps, LANES), jnp.float32), ((comps + weightings, 4 * LANES), jnp.bfloat16)],
        [pick_column, near, far],
        [],
        "group",
    )


def panel_kernel(weightings, pick_ref, near_ref, far_ref, here_ref, told_ref, *refs):
    first_ref, second_ref, stats_ref = refs
    comps = pick_ref.shape[0]
    onehot = onehot_of(pick_ref, weightings, jnp.bfloat16)
    side = jnp.full(here_ref.shape, lax.axis_index("pat") & 1)
    totals = jnp.where(side == 0, here_ref[...], told_ref[...])
    light = lighter_of(totals)
    stats_ref[0] = jnp.broadcast_to(1.0 / totals[:, 0:1], (comps, LANES))
    stats_ref[1] = jnp.broadcast_to(1.0 / totals[:, 1:2], (comps, LANES))
    stats_ref[2] = jnp.broadcast_to(light, (comps, LANES))
    columns = lighter_panel(first_ref, members_of(near_ref, far_ref), onehot, light)
    for place, (target, other) in enumerate(columns):
        here = slice(place * LANES, (place + 1) * LANES)
        second_ref[0:comps, here] = target.astype(jnp.bfloat16)
        second_ref[comps:2 * comps, here] = other.astype(jnp.bfloat16)


def make_panels(near, far, totals, told, pick_column, weightings):
    comps = pick_column.shape[0]
    return small_call(
        functools.partial(panel_kernel, weightings),
        [
            ((comps + weightings, 4 * LANES), jnp.bfloat16),
            ((2 * comps, 4 * LANES), jnp.bfloat16),
            ((3, comps, LANES), jnp.float32),
        ],
        [pick_column, near, far, totals, told],
        [],
        "panels",
    )


def both_arms(sums, onehot, light):
    comps, weightings = onehot.shape
    lighter = sums[0:comps]
    both = jnp.dot(
        onehot,
        sums[comps:comps + weightings],
        precision=lax.Precision.HIGHEST,
        preferred_element_type=jnp.float32,
    )
    target = jnp.where(light, lighter, both - lighter)
    return target, jnp.where(light, both - lighter, lighter)


def meet_kernel(pick_ref, near_ref, far_ref, stats_ref, left_ref, right_ref, *refs):
    out_ref = refs[-1]
    comps = pick_ref.shape[0]
    rows = left_ref.shape[1] // 2
    onehot = onehot_of(pick_ref, rows - comps, jnp.float32)
    light = stats_ref[2][:, 0:1] > 0.5
    for block in range(left_ref.shape[0]):
        arms = []
        for moment in range(2):
            here = slice(moment * rows, (moment + 1) * rows)
            target, other = 0.0, 0.0
            for ref, totals_ref in ((left_ref, near_ref), (right_ref, far_ref)):
                more = both_arms(ref[block, here, :], onehot, lighter_of(totals_ref[...]) > 0.5)
                target, other = target + more[0], other + more[1]
            arms.append((target, other))
        out_ref[block, 0:comps, :] = jnp.where(light, arms[0][0], arms[0][1])
        out_ref[block, comps:rows, :] = (
            left_ref[block, comps:rows, :] + right_ref[block, comps:rows, :]
        )
        out_ref[block, rows:rows + comps, :] = (
            arms[1][0] * stats_ref[0][:, 0:1] + arms[1][1] * stats_ref[1][:, 0:1]
        )


def meet(pick_column, near_totals, far_totals, stats, left, right, after):
    blocks, rows, width = left.shape
    out = (blocks, rows // 2 + pick_column.shape[0], width)
    return small_call(
        meet_kernel,
        [(out, jnp.float32)],
        [pick_column, near_totals, far_totals, stats, left, right],
        after,
        "meet",
    )[0]


def whole_spec(shape):
    return pl.BlockSpec(shape, lambda s: (0,) * len(shape))


def moments_kernel(rows, split, *refs):
    kept_ref, passed_ref, *swapped_refs, first_ref, second_ref, stats_ref = refs[:7]
    outs = refs[-(2 if split is None else split):]
    first_rows = first_ref.shape[0]
    comps = second_ref.shape[0] // 2
    inverse_target = stats_ref[0][:, 0:1]
    inverse_other = stats_ref[1][:, 0:1]
    for place in range(swapped_refs[0].shape[0] // rows):
        here = slice(place * rows, (place + 1) * rows)
        x = jnp.concatenate(
            [kept_ref[here, :], passed_ref[0, here, :]]
            + [ref[here, :] for ref in swapped_refs],
            axis=0,
        )
        first = jnp.dot(first_ref[...], x, preferred_element_type=jnp.float32)
        squares = (x.astype(jnp.float32) * x.astype(jnp.float32)).astype(jnp.bfloat16)
        second = jnp.dot(second_ref[...], squares, preferred_element_type=jnp.float32)
        out = outs[place % 2].at[place // 2] if split is None else outs[place]
        out[0:first_rows, :] = first
        out[first_rows:first_rows + comps, :] = (
            second[0:comps] * inverse_target + second[comps:2 * comps] * inverse_other
        )


def group_moments_kernel(rows, count, *refs):
    kept_ref, passed_ref, *swapped_refs, panel_ref = refs[:5]
    outs = refs[-2 * count:]
    height = panel_ref.shape[0]
    places = kept_ref.shape[0] // rows
    for place in range(places):
        here = slice(place * rows, (place + 1) * rows)
        x = jnp.concatenate(
            [kept_ref[here, :], passed_ref[0, here, :]]
            + [ref[here, :] for ref in swapped_refs],
            axis=0,
        )
        squares = (x.astype(jnp.float32) * x.astype(jnp.float32)).astype(jnp.bfloat16)
        owner_side, middle = divmod(place // 2, places // 2 // count)
        out = outs[2 * owner_side + place % 2].at[middle]
        out[0:height, :] = jnp.dot(panel_ref[...], x, preferred_element_type=jnp.float32)
        out[height:2 * height, :] = jnp.dot(
            panel_ref[...], squares, preferred_element_type=jnp.float32
        )


def group_moments(plan, rows_here, panel, after):
    rows = panel.shape[1] // 4
    out = jax.ShapeDtypeStruct(
        (plan.places // 4, 2 * panel.shape[0], plan.width), jnp.float32
    )
    outs = pl.pallas_call(
        functools.partial(group_moments_kernel, rows, 2),
        in_specs=[pl.BlockSpec(memory_space=pltpu.VMEM)] * 5
        + [pl.BlockSpec(memory_space=pl.ANY)] * len(after),
        out_specs=[pl.BlockSpec(memory_space=pltpu.VMEM)] * 4,
        out_shape=[out] * 4,
        compiler_params=pltpu.CompilerParams(vmem_limit_bytes=20 << 20),
        cost_estimate=pl.CostEstimate(flops=0, bytes_accessed=6 << 20, transcendentals=0),
        name="group_moments",
    )(*rows_here, panel, *after)
    return outs[0:2], outs[2:4]


def moments(plan, rows_here, first, second, stats, split, after):
    rows = first.shape[1] // 4
    sums = (first.shape[0] + second.shape[0] // 2, plan.width)
    if split:
        out_shape = [jax.ShapeDtypeStruct(sums, jnp.float32)] * plan.places
    else:
        out_shape = [jax.ShapeDtypeStruct((plan.places // 2,) + sums, jnp.float32)] * 2
    return pl.pallas_call(
        functools.partial(moments_kernel, rows, plan.places if split else None),
        in_specs=[pl.BlockSpec(memory_space=pltpu.VMEM)] * 7
        + [pl.BlockSpec(memory_space=pl.ANY)] * len(after),
        out_specs=[pl.BlockSpec(memory_space=pltpu.VMEM)] * len(out_shape),
        out_shape=out_shape,
        compiler_params=pltpu.CompilerParams(vmem_limit_bytes=20 << 20),
        cost_estimate=pl.CostEstimate(flops=0, bytes_accessed=6 << 20, transcendentals=0),
        name="moments",
    )(*rows_here, first, second, stats, *after)


def finish_kernel(plan, weightings, counts, pick_ref, stats_ref, *refs):
    out_ref, ring_ref = refs[-2:]
    comps = pick_ref.shape[0]
    onehot = onehot_of(pick_ref, weightings, jnp.float32)
    inverse_target = stats_ref[0][:, 0:1]
    inverse_other = stats_ref[1][:, 0:1]
    light = stats_ref[2][:, 0:1] > 0.5
    me = lax.axis_index("pat")
    for away, count in enumerate(counts):
        sums = refs[0][...]
        for more in refs[1:count]:
            sums += more[...]
        refs = refs[count:]
        target, other = both_arms(sums, onehot, light)
        spread = sums[comps + weightings:2 * comps + weightings]
        mean_target = target * inverse_target
        mean_other = other * inverse_other
        variance = spread - mean_target * mean_target - mean_other * mean_other
        pooled = jnp.maximum(variance / 2.0, 0.01)
        balance = (mean_target - mean_other) / jnp.sqrt(pooled)
        for side in range(2):
            count = plan.tiles - plan.share if side else plan.share
            if count:
                lanes = slice(side * plan.width, side * plan.width + count * LANES)

                @pl.when((me & 1) ^ away == side)
                def _():
                    ring_ref[:, lanes] = balance[:, 0:count * LANES]
    width = plan.tiles * LANES
    shift = width - lax.rem(me * plan.block, LANES)
    out_ref[:, 0, :] = pltpu.roll(ring_ref[...], shift, 1)[:, 0:plan.block]


def finish(plan, parts, pick_column, stats, weightings):
    comps = pick_column.shape[0]
    operands = [array for part in parts for array in part]
    return pl.pallas_call(
        functools.partial(finish_kernel, plan, weightings, [len(part) for part in parts]),
        in_specs=[pl.BlockSpec(memory_space=pltpu.VMEM)] * (2 + len(operands)),
        out_specs=pl.BlockSpec(memory_space=pltpu.VMEM),
        out_shape=jax.ShapeDtypeStruct((comps, 1, plan.block), jnp.float32),
        scratch_shapes=[pltpu.VMEM((comps, plan.tiles * LANES), jnp.float32)],
        compiler_params=pltpu.CompilerParams(vmem_limit_bytes=12 << 20),
        cost_estimate=pl.CostEstimate(flops=0, bytes_accessed=1 << 14, transcendentals=0),
        name="finish",
    )(pick_column, stats, *operands)


def swap(array, pairs):
    return lax.ppermute(array, "pat", pairs)


def on_device(n, covs, covariates, weights, arms, pick):
    weightings = weights.shape[1]
    pick_column = pick.reshape(pick.shape[0], 1)
    plan = Plan(n, covariates.shape[1] // n)
    to_other_side = plan.by_mask(1)

    arm_rows = arms.T.astype(weights.dtype)
    if covs > 1:
        arm_rows = lax.all_gather(arm_rows, "cov", axis=0, tiled=True)
    mine = jnp.concatenate([weights.T, arm_rows], axis=0)
    near = jnp.stack([mine, swap(mine, to_other_side)])
    far = swap(near, [(pair ^ 1, d) for d, pair in plan.by_rows()])

    kept0, kept1, sent0, sent1, other0, other1 = pack(covariates, plan)
    rows_here = {}
    for chunk, kept, sent, other in ((1, kept1, sent1, other1), (0, kept0, sent0, other0)):
        passed = swap(other, to_other_side)
        rows_here[chunk] = [
            kept, passed, swap(sent, plan.by_rows()), swap(passed[1], plan.by_rows())
        ]

    near_totals, panel = make_group(near, far, pick_column, weightings)
    far_totals = swap(near_totals, plan.by_sums())
    totals = near_totals + far_totals
    for bit in plan.middle_bits + [plan.top_bit]:
        totals = totals + swap(totals, plan.by_mask(1 << bit)[0::2])
    told = swap(totals, to_other_side[0::2])
    first, second, stats = make_panels(near, far, totals, told, pick_column, weightings)

    across, top, after = [], [], [rows_here[0][2]]
    for even, odd in group_moments(plan, rows_here[1], panel, [totals]):
        arrived = swap(odd, plan.by_sums())
        met = meet(pick_column, near_totals, far_totals, stats, even, arrived, after)
        for bit in plan.middle_bits:
            met = met[0::2] + swap(met[1::2], plan.by_mask(1 << bit))
        across.append(met)
        top.append(swap(met, plan.by_mask(1 << plan.top_bit))[0])
        after = []

    last = not plan.middle_bits
    sums = moments(plan, rows_here[0], first, second, stats, last, across)
    if last:
        even, odd = sums[0::2], sums[1::2]
        other_owner = [(d, pair ^ 1) for d, pair in plan.by_sums()]
        parts = [
            [even[0], top[0], swap(odd[0], plan.by_sums())],
            [swap(even[1] + top[1], to_other_side), swap(odd[1], other_owner)],
        ]
    else:
        even, odd = sums
        arrived = swap(odd, plan.by_sums())
        for bit in plan.middle_bits:
            odd = even[1::2] + arrived[1::2]
            even = even[0::2] + arrived[0::2]
            arrived = swap(odd, plan.by_mask(1 << bit))
        total = [even[side] + arrived[side] + top[side] for side in range(2)]
        parts = [[total[0]], [swap(total[1], to_other_side)]]
    return finish(plan, parts, pick_column, stats, weightings)


def solution(mesh):
    placed = (
        P(("groups", "pat"), "cov"),
        P(("groups", "pat"), None),
        P(("groups", "pat"), "cov"),
        P(),
    )
    body = functools.partial(on_device, mesh.shape["pat"], mesh.shape["cov"])
    return jax.shard_map(
        body, mesh=mesh, in_specs=placed, out_specs=P("groups", "cov", "pat"), check_vma=False
    )
```

```python
import functools

import jax
import jax.numpy as jnp
from jax import lax
from jax.experimental import pallas as pl
from jax.experimental.pallas import tpu as pltpu
from jax.sharding import PartitionSpec as P

LANES = 128


def round_up(value, multiple):
    return -(-value // multiple) * multiple


class Plan:
    def __init__(self, n, block):
        self.n = n
        self.block = block
        self.tiles = round_up(block, LANES) // LANES
        self.share = (self.tiles + 1) // 2
        self.width = self.share * LANES
        self.places = n // 4
        *self.middle_bits, self.top_bit = range(3, n.bit_length() - 1)

    def by_rows(self):
        return [(d, d ^ (2 + 2 * (d & 1))) for d in range(self.n)]

    def by_sums(self):
        return [(d, d ^ (4 - 2 * (d & 1))) for d in range(self.n)]

    def by_mask(self, mask):
        return [(d, d ^ mask) for d in range(self.n)]


def pack_kernel(
    plan, x_ref, kept0_ref, kept1_ref, sent0_ref, sent1_ref, other0_ref, other1_ref
):
    step = pl.program_id(0)
    me = lax.axis_index("pat")
    rows, columns = x_ref.shape
    last_tile = columns // LANES - 1
    lane = lax.broadcasted_iota(jnp.int32, (rows, LANES), 1)

    def tile(index):
        return pl.ds(pl.multiple_of(jnp.minimum(index, last_tile) * LANES, LANES), LANES)

    for away in range(2):
        side = (me & 1) ^ away
        holder = me ^ away
        for sent in range(2):
            for chunk in range(2):
                middle = len(plan.middle_bits)
                relative = (
                    (step >> (1 + middle))
                    | (sent << (1 + side))
                    | ((step & 1) << (2 - side))
                    | (((step >> 1) & ((1 << middle) - 1)) << 3)
                    | (chunk << plan.top_bit)
                )
                column = (holder ^ relative) * plan.block
                first = column // LANES
                edge = (column - first * LANES) * (1 - side)
                head = x_ref[:, tile(first + side * plan.share)]
                tail = x_ref[:, tile(first + plan.tiles)]
                folded = jnp.where(lane >= edge, head.astype(jnp.float32), tail.astype(jnp.float32))
                if away:
                    target = (other0_ref, other1_ref)[chunk].at[sent]
                elif sent:
                    target = (sent0_ref, sent1_ref)[chunk]
                else:
                    target = (kept0_ref, kept1_ref)[chunk]
                target[:, 0:LANES] = folded.astype(x_ref.dtype)
                for slot in range(1, plan.share):
                    here = slice(slot * LANES, (slot + 1) * LANES)
                    target[:, here] = x_ref[:, tile(first + side * plan.share + slot)]


def pack(covariates, plan):
    rows = covariates.shape[0]
    dtype = covariates.dtype
    length = plan.places * rows
    mine = jax.ShapeDtypeStruct((length, plan.width), dtype)
    other = jax.ShapeDtypeStruct((2, length, plan.width), dtype)
    mine_spec = pl.BlockSpec((rows, plan.width), lambda s: (s, 0))
    other_spec = pl.BlockSpec((2, rows, plan.width), lambda s: (0, s, 0))
    return pl.pallas_call(
        functools.partial(pack_kernel, plan),
        grid=(plan.places,),
        in_specs=[pl.BlockSpec(memory_space=pltpu.VMEM)],
        out_specs=[mine_spec] * 4 + [other_spec] * 2,
        out_shape=[mine] * 4 + [other] * 2,
        compiler_params=pltpu.CompilerParams(vmem_limit_bytes=12 << 20),
        cost_estimate=pl.CostEstimate(
            flops=0, bytes_accessed=4 * covariates.size, transcendentals=0
        ),
        name="pack",
    )(covariates)


def onehot_of(pick_ref, weightings, dtype):
    index = lax.broadcasted_iota(jnp.int32, (pick_ref.shape[0], weightings), 1)
    return jnp.where(index == pick_ref[...], 1.0, 0.0).astype(dtype)


def arm_columns(panel_ref, onehot):
    comps, weightings = onehot.shape
    weights = panel_ref[0:weightings, :]
    arms = panel_ref[weightings:weightings + comps, :].astype(jnp.float32)
    picked = jnp.dot(onehot, weights, preferred_element_type=jnp.float32)
    return weights, picked * arms, picked * (1.0 - arms)


def small_call(kernel, shapes, operands, after, name):
    vmem = pl.BlockSpec(memory_space=pltpu.VMEM)
    return pl.pallas_call(
        kernel,
        in_specs=[vmem] * len(operands) + [pl.BlockSpec(memory_space=pl.ANY)] * len(after),
        out_specs=[vmem] * len(shapes),
        out_shape=[jax.ShapeDtypeStruct(shape, dtype) for shape, dtype in shapes],
        compiler_params=pltpu.CompilerParams(vmem_limit_bytes=8 << 20),
        cost_estimate=pl.CostEstimate(flops=0, bytes_accessed=1 << 14, transcendentals=0),
        name=name,
    )(*operands, *after)


def lighter_of(totals):
    return jnp.where(totals[:, 0:1] <= totals[:, 1:2], 1.0, 0.0)


def lighter_panel(ref, members, onehot, light):
    comps, weightings = onehot.shape
    columns = []
    for place, member in enumerate(members):
        weights, target, other = arm_columns(member, onehot)
        here = slice(place * LANES, (place + 1) * LANES)
        lighter = light * target + (1.0 - light) * other
        ref[0:comps, here] = lighter.astype(jnp.bfloat16)
        ref[comps:comps + weightings, here] = weights
        columns.append((target, other))
    return columns


def members_of(near_ref, far_ref):
    return (near_ref.at[0], near_ref.at[1], far_ref.at[1], far_ref.at[0])


def group_kernel(weightings, pick_ref, near_ref, far_ref, totals_ref, panel_ref):
    onehot = onehot_of(pick_ref, weightings, jnp.bfloat16)
    target_sum, other_sum = 0.0, 0.0
    for member in members_of(near_ref, far_ref):
        _, target, other = arm_columns(member, onehot)
        target_sum += target
        other_sum += other
    lane = lax.broadcasted_iota(jnp.int32, totals_ref.shape, 1)
    totals = jnp.where(
        lane == 0,
        jnp.sum(target_sum, axis=1, keepdims=True),
        jnp.sum(other_sum, axis=1, keepdims=True),
    )
    totals_ref[...] = totals
    lighter_panel(panel_ref, members_of(near_ref, far_ref), onehot, lighter_of(totals))


def make_group(near, far, pick_column, weightings):
    comps = pick_column.shape[0]
    return small_call(
        functools.partial(group_kernel, weightings),
        [((comps, LANES), jnp.float32), ((comps + weightings, 4 * LANES), jnp.bfloat16)],
        [pick_column, near, far],
        [],
        "group",
    )


def panel_kernel(weightings, pick_ref, near_ref, far_ref, here_ref, told_ref, *refs):
    first_ref, second_ref, stats_ref = refs
    comps = pick_ref.shape[0]
    onehot = onehot_of(pick_ref, weightings, jnp.bfloat16)
    side = jnp.full(here_ref.shape, lax.axis_index("pat") & 1)
    totals = jnp.where(side == 0, here_ref[...], told_ref[...])
    light = lighter_of(totals)
    stats_ref[0] = jnp.broadcast_to(1.0 / totals[:, 0:1], (comps, LANES))
    stats_ref[1] = jnp.broadcast_to(1.0 / totals[:, 1:2], (comps, LANES))
    stats_ref[2] = jnp.broadcast_to(light, (comps, LANES))
    columns = lighter_panel(first_ref, members_of(near_ref, far_ref), onehot, light)
    for place, (target, other) in enumerate(columns):
        here = slice(place * LANES, (place + 1) * LANES)
        second_ref[0:comps, here] = target.astype(jnp.bfloat16)
        second_ref[comps:2 * comps, here] = other.astype(jnp.bfloat16)


def make_panels(near, far, totals, told, pick_column, weightings):
    comps = pick_column.shape[0]
    return small_call(
        functools.partial(panel_kernel, weightings),
        [
            ((comps + weightings, 4 * LANES), jnp.bfloat16),
            ((2 * comps, 4 * LANES), jnp.bfloat16),
            ((3, comps, LANES), jnp.float32),
        ],
        [pick_column, near, far, totals, told],
        [],
        "panels",
    )


def both_arms(sums, onehot, light):
    comps, weightings = onehot.shape
    lighter = sums[0:comps]
    both = jnp.dot(
        onehot,
        sums[comps:comps + weightings],
        precision=lax.Precision.HIGHEST,
        preferred_element_type=jnp.float32,
    )
    target = jnp.where(light, lighter, both - lighter)
    return target, jnp.where(light, both - lighter, lighter)


def meet_kernel(pick_ref, near_ref, far_ref, stats_ref, left_ref, right_ref, *refs):
    out_ref = refs[-1]
    comps = pick_ref.shape[0]
    rows = left_ref.shape[1] // 2
    onehot = onehot_of(pick_ref, rows - comps, jnp.float32)
    light = stats_ref[2][:, 0:1] > 0.5
    for block in range(left_ref.shape[0]):
        arms = []
        for moment in range(2):
            here = slice(moment * rows, (moment + 1) * rows)
            target, other = 0.0, 0.0
            for ref, totals_ref in ((left_ref, near_ref), (right_ref, far_ref)):
                more = both_arms(ref[block, here, :], onehot, lighter_of(totals_ref[...]) > 0.5)
                target, other = target + more[0], other + more[1]
            arms.append((target, other))
        out_ref[block, 0:comps, :] = jnp.where(light, arms[0][0], arms[0][1])
        out_ref[block, comps:rows, :] = (
            left_ref[block, comps:rows, :] + right_ref[block, comps:rows, :]
        )
        out_ref[block, rows:rows + comps, :] = (
            arms[1][0] * stats_ref[0][:, 0:1] + arms[1][1] * stats_ref[1][:, 0:1]
        )


def meet(pick_column, near_totals, far_totals, stats, left, right, after):
    blocks, rows, width = left.shape
    out = (blocks, rows // 2 + pick_column.shape[0], width)
    return small_call(
        meet_kernel,
        [(out, jnp.float32)],
        [pick_column, near_totals, far_totals, stats, left, right],
        after,
        "meet",
    )[0]


def whole_spec(shape):
    return pl.BlockSpec(shape, lambda s: (0,) * len(shape))


def moments_kernel(rows, split, *refs):
    kept_ref, passed_ref, *swapped_refs, first_ref, second_ref, stats_ref = refs[:7]
    outs = refs[-(2 if split is None else split):]
    first_rows = first_ref.shape[0]
    comps = second_ref.shape[0] // 2
    inverse_target = stats_ref[0][:, 0:1]
    inverse_other = stats_ref[1][:, 0:1]
    for place in range(swapped_refs[0].shape[0] // rows):
        here = slice(place * rows, (place + 1) * rows)
        x = jnp.concatenate(
            [kept_ref[here, :], passed_ref[0, here, :]]
            + [ref[here, :] for ref in swapped_refs],
            axis=0,
        )
        first = jnp.dot(first_ref[...], x, preferred_element_type=jnp.float32)
        squares = (x.astype(jnp.float32) * x.astype(jnp.float32)).astype(jnp.bfloat16)
        second = jnp.dot(second_ref[...], squares, preferred_element_type=jnp.float32)
        out = outs[place % 2].at[place // 2] if split is None else outs[place]
        out[0:first_rows, :] = first
        out[first_rows:first_rows + comps, :] = (
            second[0:comps] * inverse_target + second[comps:2 * comps] * inverse_other
        )


def group_moments_kernel(rows, count, *refs):
    kept_ref, passed_ref, *swapped_refs, panel_ref = refs[:5]
    outs = refs[-2 * count:]
    height = panel_ref.shape[0]
    places = kept_ref.shape[0] // rows
    for place in range(places):
        here = slice(place * rows, (place + 1) * rows)
        x = jnp.concatenate(
            [kept_ref[here, :], passed_ref[0, here, :]]
            + [ref[here, :] for ref in swapped_refs],
            axis=0,
        )
        squares = (x.astype(jnp.float32) * x.astype(jnp.float32)).astype(jnp.bfloat16)
        owner_side, middle = divmod(place // 2, places // 2 // count)
        out = outs[2 * owner_side + place % 2].at[middle]
        out[0:height, :] = jnp.dot(panel_ref[...], x, preferred_element_type=jnp.float32)
        out[height:2 * height, :] = jnp.dot(
            panel_ref[...], squares, preferred_element_type=jnp.float32
        )


def group_moments(plan, rows_here, panel, after):
    rows = panel.shape[1] // 4
    out = jax.ShapeDtypeStruct(
        (plan.places // 4, 2 * panel.shape[0], plan.width), jnp.float32
    )
    outs = pl.pallas_call(
        functools.partial(group_moments_kernel, rows, 2),
        in_specs=[pl.BlockSpec(memory_space=pltpu.VMEM)] * 5
        + [pl.BlockSpec(memory_space=pl.ANY)] * len(after),
        out_specs=[pl.BlockSpec(memory_space=pltpu.VMEM)] * 4,
        out_shape=[out] * 4,
        compiler_params=pltpu.CompilerParams(vmem_limit_bytes=20 << 20),
        cost_estimate=pl.CostEstimate(flops=0, bytes_accessed=6 << 20, transcendentals=0),
        name="group_moments",
    )(*rows_here, panel, *after)
    return outs[0:2], outs[2:4]


def moments(plan, rows_here, first, second, stats, split, after):
    rows = first.shape[1] // 4
    sums = (first.shape[0] + second.shape[0] // 2, plan.width)
    if split:
        out_shape = [jax.ShapeDtypeStruct(sums, jnp.float32)] * plan.places
    else:
        out_shape = [jax.ShapeDtypeStruct((plan.places // 2,) + sums, jnp.float32)] * 2
    return pl.pallas_call(
        functools.partial(moments_kernel, rows, plan.places if split else None),
        in_specs=[pl.BlockSpec(memory_space=pltpu.VMEM)] * 7
        + [pl.BlockSpec(memory_space=pl.ANY)] * len(after),
        out_specs=[pl.BlockSpec(memory_space=pltpu.VMEM)] * len(out_shape),
        out_shape=out_shape,
        compiler_params=pltpu.CompilerParams(vmem_limit_bytes=20 << 20),
        cost_estimate=pl.CostEstimate(flops=0, bytes_accessed=6 << 20, transcendentals=0),
        name="moments",
    )(*rows_here, first, second, stats, *after)


def finish_kernel(plan, weightings, counts, pick_ref, stats_ref, *refs):
    out_ref, ring_ref = refs[-2:]
    comps = pick_ref.shape[0]
    onehot = onehot_of(pick_ref, weightings, jnp.float32)
    inverse_target = stats_ref[0][:, 0:1]
    inverse_other = stats_ref[1][:, 0:1]
    light = stats_ref[2][:, 0:1] > 0.5
    me = lax.axis_index("pat")
    for away, count in enumerate(counts):
        sums = refs[0][...]
        for more in refs[1:count]:
            sums += more[...]
        refs = refs[count:]
        target, other = both_arms(sums, onehot, light)
        spread = sums[comps + weightings:2 * comps + weightings]
        mean_target = target * inverse_target
        mean_other = other * inverse_other
        variance = spread - mean_target * mean_target - mean_other * mean_other
        pooled = jnp.maximum(variance / 2.0, 0.01)
        balance = (mean_target - mean_other) / jnp.sqrt(pooled)
        for side in range(2):
            count = plan.tiles - plan.share if side else plan.share
            if count:
                lanes = slice(side * plan.width, side * plan.width + count * LANES)

                @pl.when((me & 1) ^ away == side)
                def _():
                    ring_ref[:, lanes] = balance[:, 0:count * LANES]
    width = plan.tiles * LANES
    shift = width - lax.rem(me * plan.block, LANES)
    out_ref[:, 0, :] = pltpu.roll(ring_ref[...], shift, 1)[:, 0:plan.block]


def finish(plan, parts, pick_column, stats, weightings):
    comps = pick_column.shape[0]
    operands = [array for part in parts for array in part]
    return pl.pallas_call(
        functools.partial(finish_kernel, plan, weightings, [len(part) for part in parts]),
        in_specs=[pl.BlockSpec(memory_space=pltpu.VMEM)] * (2 + len(operands)),
        out_specs=pl.BlockSpec(memory_space=pltpu.VMEM),
        out_shape=jax.ShapeDtypeStruct((comps, 1, plan.block), jnp.float32),
        scratch_shapes=[pltpu.VMEM((comps, plan.tiles * LANES), jnp.float32)],
        compiler_params=pltpu.CompilerParams(vmem_limit_bytes=12 << 20),
        cost_estimate=pl.CostEstimate(flops=0, bytes_accessed=1 << 14, transcendentals=0),
        name="finish",
    )(pick_column, stats, *operands)


def hold_kernel(*refs):
    del refs


def hold(array, after):
    any_space = pl.BlockSpec(memory_space=pl.ANY)
    return pl.pallas_call(
        hold_kernel,
        in_specs=[any_space] * (1 + len(after)),
        out_specs=any_space,
        out_shape=jax.ShapeDtypeStruct(array.shape, array.dtype),
        input_output_aliases={0: 0},
        compiler_params=pltpu.CompilerParams(vmem_limit_bytes=1 << 20),
        cost_estimate=pl.CostEstimate(flops=0, bytes_accessed=0, transcendentals=0),
        name="hold",
    )(array, *after)


def swap(array, pairs):
    return lax.ppermute(array, "pat", pairs)


def on_device(n, covs, covariates, weights, arms, pick):
    weightings = weights.shape[1]
    pick_column = pick.reshape(pick.shape[0], 1)
    plan = Plan(n, covariates.shape[1] // n)
    to_other_side = plan.by_mask(1)

    arm_rows = arms.T.astype(weights.dtype)
    if covs > 1:
        arm_rows = lax.all_gather(arm_rows, "cov", axis=0, tiled=True)
    mine = jnp.concatenate([weights.T, arm_rows], axis=0)
    near = jnp.stack([mine, swap(mine, to_other_side)])
    far = swap(near, [(pair ^ 1, d) for d, pair in plan.by_rows()])

    kept0, kept1, sent0, sent1, other0, other1 = pack(covariates, plan)
    rows_here, forward = {}, {}
    for chunk, kept, sent, other in ((1, kept1, sent1, other1), (0, kept0, sent0, other0)):
        passed = swap(other, to_other_side)
        rows_here[chunk] = [kept, passed, swap(sent, plan.by_rows())]
        forward[chunk] = passed[1]
    rows_here[1].append(swap(forward[1], plan.by_rows()))

    near_totals, panel = make_group(near, far, pick_column, weightings)
    far_totals = swap(near_totals, plan.by_sums())
    totals = near_totals + far_totals
    for bit in plan.middle_bits + [plan.top_bit]:
        totals = totals + swap(totals, plan.by_mask(1 << bit)[0::2])
    told = swap(totals, to_other_side[0::2])
    first, second, stats = make_panels(near, far, totals, told, pick_column, weightings)

    across, top, came = [], [], []
    for even, odd in group_moments(plan, rows_here[1], panel, [totals]):
        arrived = swap(odd, plan.by_sums())
        met = meet(pick_column, near_totals, far_totals, stats, even, arrived, [rows_here[0][2]])
        came.append(arrived)
        for bit in plan.middle_bits:
            met = met[0::2] + swap(met[1::2], plan.by_mask(1 << bit))
        across.append(met)
        top.append(swap(met, plan.by_mask(1 << plan.top_bit))[0])

    rows_here[0].append(swap(hold(forward[0], [across[1]]), plan.by_rows()))

    last = not plan.middle_bits
    sums = moments(plan, rows_here[0], first, second, stats, last, across)
    if last:
        even, odd = sums[0::2], sums[1::2]
        other_owner = [(d, pair ^ 1) for d, pair in plan.by_sums()]
        parts = [
            [even[0], top[0], swap(odd[0], plan.by_sums())],
            [swap(even[1] + top[1], to_other_side), swap(odd[1], other_owner)],
        ]
    else:
        even, odd = sums
        arrived = swap(odd, plan.by_sums())
        for bit in plan.middle_bits:
            odd = even[1::2] + arrived[1::2]
            even = even[0::2] + arrived[0::2]
            arrived = swap(odd, plan.by_mask(1 << bit))
        total = [even[side] + arrived[side] + top[side] for side in range(2)]
        parts = [[total[0]], [swap(total[1], to_other_side)]]
    return finish(plan, parts, pick_column, stats, weightings)


def solution(mesh):
    placed = (
        P(("groups", "pat"), "cov"),
        P(("groups", "pat"), None),
        P(("groups", "pat"), "cov"),
        P(),
    )
    body = functools.partial(on_device, mesh.shape["pat"], mesh.shape["cov"])
    return jax.shard_map(
        body, mesh=mesh, in_specs=placed, out_specs=P("groups", "cov", "pat"), check_vma=False
    )
```

```python
import functools

import jax
import jax.numpy as jnp
from jax import lax
from jax.experimental import pallas as pl
from jax.experimental.pallas import tpu as pltpu
from jax.sharding import PartitionSpec as P

LANES = 128


def round_up(value, multiple):
    return -(-value // multiple) * multiple


class Plan:
    def __init__(self, n, block):
        self.n = n
        self.block = block
        self.tiles = round_up(block, LANES) // LANES
        self.share = (self.tiles + 1) // 2
        self.width = self.share * LANES
        self.places = n // 4
        *self.middle_bits, self.top_bit = range(3, n.bit_length() - 1)

    def by_rows(self):
        return [(d, d ^ (2 + 2 * (d & 1))) for d in range(self.n)]

    def by_sums(self):
        return [(d, d ^ (4 - 2 * (d & 1))) for d in range(self.n)]

    def by_mask(self, mask):
        return [(d, d ^ mask) for d in range(self.n)]


def pack_kernel(
    plan, x_ref, kept0_ref, kept1_ref, sent0_ref, sent1_ref, other0_ref, other1_ref
):
    step = pl.program_id(0)
    me = lax.axis_index("pat")
    rows, columns = x_ref.shape
    last_tile = columns // LANES - 1
    lane = lax.broadcasted_iota(jnp.int32, (rows, LANES), 1)

    def tile(index):
        return pl.ds(pl.multiple_of(jnp.minimum(index, last_tile) * LANES, LANES), LANES)

    for away in range(2):
        side = (me & 1) ^ away
        holder = me ^ away
        for sent in range(2):
            for chunk in range(2):
                middle = len(plan.middle_bits)
                relative = (
                    (step >> (1 + middle))
                    | (sent << (1 + side))
                    | ((step & 1) << (2 - side))
                    | (((step >> 1) & ((1 << middle) - 1)) << 3)
                    | (chunk << plan.top_bit)
                )
                column = (holder ^ relative) * plan.block
                first = column // LANES
                edge = (column - first * LANES) * (1 - side)
                head = x_ref[:, tile(first + side * plan.share)]
                tail = x_ref[:, tile(first + plan.tiles)]
                folded = jnp.where(lane >= edge, head.astype(jnp.float32), tail.astype(jnp.float32))
                if away:
                    target = (other0_ref, other1_ref)[chunk].at[sent]
                elif sent:
                    target = (sent0_ref, sent1_ref)[chunk]
                else:
                    target = (kept0_ref, kept1_ref)[chunk]
                target[:, 0:LANES] = folded.astype(x_ref.dtype)
                for slot in range(1, plan.share):
                    here = slice(slot * LANES, (slot + 1) * LANES)
                    target[:, here] = x_ref[:, tile(first + side * plan.share + slot)]


def pack(covariates, plan):
    rows = covariates.shape[0]
    dtype = covariates.dtype
    length = plan.places * rows
    mine = jax.ShapeDtypeStruct((length, plan.width), dtype)
    other = jax.ShapeDtypeStruct((2, length, plan.width), dtype)
    mine_spec = pl.BlockSpec((rows, plan.width), lambda s: (s, 0))
    other_spec = pl.BlockSpec((2, rows, plan.width), lambda s: (0, s, 0))
    return pl.pallas_call(
        functools.partial(pack_kernel, plan),
        grid=(plan.places,),
        in_specs=[pl.BlockSpec(memory_space=pltpu.VMEM)],
        out_specs=[mine_spec] * 4 + [other_spec] * 2,
        out_shape=[mine] * 4 + [other] * 2,
        compiler_params=pltpu.CompilerParams(vmem_limit_bytes=12 << 20),
        cost_estimate=pl.CostEstimate(
            flops=0, bytes_accessed=4 * covariates.size, transcendentals=0
        ),
        name="pack",
    )(covariates)


def onehot_of(pick_ref, weightings, dtype):
    index = lax.broadcasted_iota(jnp.int32, (pick_ref.shape[0], weightings), 1)
    return jnp.where(index == pick_ref[...], 1.0, 0.0).astype(dtype)


def arm_columns(panel_ref, onehot):
    comps, weightings = onehot.shape
    weights = panel_ref[0:weightings, :]
    arms = panel_ref[weightings:weightings + comps, :].astype(jnp.float32)
    picked = jnp.dot(onehot, weights, preferred_element_type=jnp.float32)
    return weights, picked * arms, picked * (1.0 - arms)


def small_call(kernel, shapes, operands, after, name):
    vmem = pl.BlockSpec(memory_space=pltpu.VMEM)
    return pl.pallas_call(
        kernel,
        in_specs=[vmem] * len(operands) + [pl.BlockSpec(memory_space=pl.ANY)] * len(after),
        out_specs=[vmem] * len(shapes),
        out_shape=[jax.ShapeDtypeStruct(shape, dtype) for shape, dtype in shapes],
        compiler_params=pltpu.CompilerParams(vmem_limit_bytes=8 << 20),
        cost_estimate=pl.CostEstimate(flops=0, bytes_accessed=1 << 14, transcendentals=0),
        name=name,
    )(*operands, *after)


def lighter_of(totals):
    return jnp.where(totals[:, 0:1] <= totals[:, 1:2], 1.0, 0.0)


def lighter_panel(ref, members, onehot, light):
    comps, weightings = onehot.shape
    columns = []
    for place, member in enumerate(members):
        weights, target, other = arm_columns(member, onehot)
        here = slice(place * LANES, (place + 1) * LANES)
        lighter = light * target + (1.0 - light) * other
        ref[0:comps, here] = lighter.astype(jnp.bfloat16)
        ref[comps:comps + weightings, here] = weights
        columns.append((target, other))
    return columns


def members_of(near_ref, far_ref):
    return (near_ref.at[0], near_ref.at[1], far_ref.at[1], far_ref.at[0])


def group_kernel(weightings, pick_ref, near_ref, far_ref, totals_ref, panel_ref):
    onehot = onehot_of(pick_ref, weightings, jnp.bfloat16)
    target_sum, other_sum = 0.0, 0.0
    for member in members_of(near_ref, far_ref):
        _, target, other = arm_columns(member, onehot)
        target_sum += target
        other_sum += other
    lane = lax.broadcasted_iota(jnp.int32, totals_ref.shape, 1)
    totals = jnp.where(
        lane == 0,
        jnp.sum(target_sum, axis=1, keepdims=True),
        jnp.sum(other_sum, axis=1, keepdims=True),
    )
    totals_ref[...] = totals
    lighter_panel(panel_ref, members_of(near_ref, far_ref), onehot, lighter_of(totals))


def make_group(near, far, pick_column, weightings):
    comps = pick_column.shape[0]
    return small_call(
        functools.partial(group_kernel, weightings),
        [((comps, LANES), jnp.float32), ((comps + weightings, 4 * LANES), jnp.bfloat16)],
        [pick_column, near, far],
        [],
        "group",
    )


def panel_kernel(weightings, pick_ref, near_ref, far_ref, here_ref, told_ref, *refs):
    first_ref, second_ref, stats_ref = refs
    comps = pick_ref.shape[0]
    onehot = onehot_of(pick_ref, weightings, jnp.bfloat16)
    side = jnp.full(here_ref.shape, lax.axis_index("pat") & 1)
    totals = jnp.where(side == 0, here_ref[...], told_ref[...])
    light = lighter_of(totals)
    stats_ref[0] = jnp.broadcast_to(1.0 / totals[:, 0:1], (comps, LANES))
    stats_ref[1] = jnp.broadcast_to(1.0 / totals[:, 1:2], (comps, LANES))
    stats_ref[2] = jnp.broadcast_to(light, (comps, LANES))
    columns = lighter_panel(first_ref, members_of(near_ref, far_ref), onehot, light)
    for place, (target, other) in enumerate(columns):
        here = slice(place * LANES, (place + 1) * LANES)
        second_ref[0:comps, here] = target.astype(jnp.bfloat16)
        second_ref[comps:2 * comps, here] = other.astype(jnp.bfloat16)


def make_panels(near, far, totals, told, pick_column, weightings):
    comps = pick_column.shape[0]
    return small_call(
        functools.partial(panel_kernel, weightings),
        [
            ((comps + weightings, 4 * LANES), jnp.bfloat16),
            ((2 * comps, 4 * LANES), jnp.bfloat16),
            ((3, comps, LANES), jnp.float32),
        ],
        [pick_column, near, far, totals, told],
        [],
        "panels",
    )


def both_arms(sums, onehot, light):
    comps, weightings = onehot.shape
    lighter = sums[0:comps]
    both = jnp.dot(
        onehot,
        sums[comps:comps + weightings],
        precision=lax.Precision.HIGHEST,
        preferred_element_type=jnp.float32,
    )
    target = jnp.where(light, lighter, both - lighter)
    return target, jnp.where(light, both - lighter, lighter)


def meet_kernel(pick_ref, near_ref, far_ref, stats_ref, left_ref, right_ref, *refs):
    out_ref = refs[-1]
    comps = pick_ref.shape[0]
    rows = left_ref.shape[1] // 2
    onehot = onehot_of(pick_ref, rows - comps, jnp.float32)
    light = stats_ref[2][:, 0:1] > 0.5
    for block in range(left_ref.shape[0]):
        arms = []
        for moment in range(2):
            here = slice(moment * rows, (moment + 1) * rows)
            target, other = 0.0, 0.0
            for ref, totals_ref in ((left_ref, near_ref), (right_ref, far_ref)):
                more = both_arms(ref[block, here, :], onehot, lighter_of(totals_ref[...]) > 0.5)
                target, other = target + more[0], other + more[1]
            arms.append((target, other))
        out_ref[block, 0:comps, :] = jnp.where(light, arms[0][0], arms[0][1])
        out_ref[block, comps:rows, :] = (
            left_ref[block, comps:rows, :] + right_ref[block, comps:rows, :]
        )
        out_ref[block, rows:rows + comps, :] = (
            arms[1][0] * stats_ref[0][:, 0:1] + arms[1][1] * stats_ref[1][:, 0:1]
        )


def meet(pick_column, near_totals, far_totals, stats, left, right, after):
    blocks, rows, width = left.shape
    out = (blocks, rows // 2 + pick_column.shape[0], width)
    return small_call(
        meet_kernel,
        [(out, jnp.float32)],
        [pick_column, near_totals, far_totals, stats, left, right],
        after,
        "meet",
    )[0]


def whole_spec(shape):
    return pl.BlockSpec(shape, lambda s: (0,) * len(shape))


def moments_kernel(rows, split, *refs):
    kept_ref, passed_ref, *swapped_refs, first_ref, second_ref, stats_ref = refs[:7]
    outs = refs[-(2 if split is None else split):]
    first_rows = first_ref.shape[0]
    comps = second_ref.shape[0] // 2
    inverse_target = stats_ref[0][:, 0:1]
    inverse_other = stats_ref[1][:, 0:1]
    for place in range(swapped_refs[0].shape[0] // rows):
        here = slice(place * rows, (place + 1) * rows)
        x = jnp.concatenate(
            [kept_ref[here, :], passed_ref[0, here, :]]
            + [ref[here, :] for ref in swapped_refs],
            axis=0,
        )
        first = jnp.dot(first_ref[...], x, preferred_element_type=jnp.float32)
        squares = (x.astype(jnp.float32) * x.astype(jnp.float32)).astype(jnp.bfloat16)
        second = jnp.dot(second_ref[...], squares, preferred_element_type=jnp.float32)
        out = outs[place % 2].at[place // 2] if split is None else outs[place]
        out[0:first_rows, :] = first
        out[first_rows:first_rows + comps, :] = (
            second[0:comps] * inverse_target + second[comps:2 * comps] * inverse_other
        )


def group_moments_kernel(rows, count, *refs):
    kept_ref, passed_ref, *swapped_refs, panel_ref = refs[:5]
    outs = refs[-2 * count:]
    height = panel_ref.shape[0]
    places = kept_ref.shape[0] // rows
    for place in range(places):
        here = slice(place * rows, (place + 1) * rows)
        x = jnp.concatenate(
            [kept_ref[here, :], passed_ref[0, here, :]]
            + [ref[here, :] for ref in swapped_refs],
            axis=0,
        )
        squares = (x.astype(jnp.float32) * x.astype(jnp.float32)).astype(jnp.bfloat16)
        owner_side, middle = divmod(place // 2, places // 2 // count)
        out = outs[2 * owner_side + place % 2].at[middle]
        out[0:height, :] = jnp.dot(panel_ref[...], x, preferred_element_type=jnp.float32)
        out[height:2 * height, :] = jnp.dot(
            panel_ref[...], squares, preferred_element_type=jnp.float32
        )


def group_moments(plan, rows_here, panel, after):
    rows = panel.shape[1] // 4
    out = jax.ShapeDtypeStruct(
        (plan.places // 4, 2 * panel.shape[0], plan.width), jnp.float32
    )
    outs = pl.pallas_call(
        functools.partial(group_moments_kernel, rows, 2),
        in_specs=[pl.BlockSpec(memory_space=pltpu.VMEM)] * 5
        + [pl.BlockSpec(memory_space=pl.ANY)] * len(after),
        out_specs=[pl.BlockSpec(memory_space=pltpu.VMEM)] * 4,
        out_shape=[out] * 4,
        compiler_params=pltpu.CompilerParams(vmem_limit_bytes=10 << 20),
        cost_estimate=pl.CostEstimate(flops=0, bytes_accessed=6 << 20, transcendentals=0),
        name="group_moments",
    )(*rows_here, panel, *after)
    return outs[0:2], outs[2:4]


def moments(plan, rows_here, first, second, stats, split, after):
    rows = first.shape[1] // 4
    sums = (first.shape[0] + second.shape[0] // 2, plan.width)
    if split:
        out_shape = [jax.ShapeDtypeStruct(sums, jnp.float32)] * plan.places
    else:
        out_shape = [jax.ShapeDtypeStruct((plan.places // 2,) + sums, jnp.float32)] * 2
    return pl.pallas_call(
        functools.partial(moments_kernel, rows, plan.places if split else None),
        in_specs=[pl.BlockSpec(memory_space=pltpu.VMEM)] * 7
        + [pl.BlockSpec(memory_space=pl.ANY)] * len(after),
        out_specs=[pl.BlockSpec(memory_space=pltpu.VMEM)] * len(out_shape),
        out_shape=out_shape,
        compiler_params=pltpu.CompilerParams(vmem_limit_bytes=10 << 20),
        cost_estimate=pl.CostEstimate(flops=0, bytes_accessed=6 << 20, transcendentals=0),
        name="moments",
    )(*rows_here, first, second, stats, *after)


def finish_kernel(plan, weightings, counts, pick_ref, stats_ref, *refs):
    out_ref, ring_ref = refs[-2:]
    comps = pick_ref.shape[0]
    onehot = onehot_of(pick_ref, weightings, jnp.float32)
    inverse_target = stats_ref[0][:, 0:1]
    inverse_other = stats_ref[1][:, 0:1]
    light = stats_ref[2][:, 0:1] > 0.5
    me = lax.axis_index("pat")
    for away, count in enumerate(counts):
        sums = refs[0][...]
        for more in refs[1:count]:
            sums += more[...]
        refs = refs[count:]
        target, other = both_arms(sums, onehot, light)
        spread = sums[comps + weightings:2 * comps + weightings]
        mean_target = target * inverse_target
        mean_other = other * inverse_other
        variance = spread - mean_target * mean_target - mean_other * mean_other
        pooled = jnp.maximum(variance / 2.0, 0.01)
        balance = (mean_target - mean_other) / jnp.sqrt(pooled)
        for side in range(2):
            count = plan.tiles - plan.share if side else plan.share
            if count:
                lanes = slice(side * plan.width, side * plan.width + count * LANES)

                @pl.when((me & 1) ^ away == side)
                def _():
                    ring_ref[:, lanes] = balance[:, 0:count * LANES]
    width = plan.tiles * LANES
    shift = width - lax.rem(me * plan.block, LANES)
    out_ref[:, 0, :] = pltpu.roll(ring_ref[...], shift, 1)[:, 0:plan.block]


def finish(plan, parts, pick_column, stats, weightings):
    comps = pick_column.shape[0]
    operands = [array for part in parts for array in part]
    return pl.pallas_call(
        functools.partial(finish_kernel, plan, weightings, [len(part) for part in parts]),
        in_specs=[pl.BlockSpec(memory_space=pltpu.VMEM)] * (2 + len(operands)),
        out_specs=pl.BlockSpec(memory_space=pltpu.VMEM),
        out_shape=jax.ShapeDtypeStruct((comps, 1, plan.block), jnp.float32),
        scratch_shapes=[pltpu.VMEM((comps, plan.tiles * LANES), jnp.float32)],
        compiler_params=pltpu.CompilerParams(vmem_limit_bytes=12 << 20),
        cost_estimate=pl.CostEstimate(flops=0, bytes_accessed=1 << 14, transcendentals=0),
        name="finish",
    )(pick_column, stats, *operands)


def swap(array, pairs):
    return lax.ppermute(array, "pat", pairs)


def on_device(n, covs, covariates, weights, arms, pick):
    weightings = weights.shape[1]
    pick_column = pick.reshape(pick.shape[0], 1)
    plan = Plan(n, covariates.shape[1] // n)
    to_other_side = plan.by_mask(1)

    arm_rows = arms.T.astype(weights.dtype)
    if covs > 1:
        arm_rows = lax.all_gather(arm_rows, "cov", axis=0, tiled=True)
    mine = jnp.concatenate([weights.T, arm_rows], axis=0)
    near = jnp.stack([mine, swap(mine, to_other_side)])
    far = swap(near, [(pair ^ 1, d) for d, pair in plan.by_rows()])

    kept0, kept1, sent0, sent1, other0, other1 = pack(covariates, plan)
    rows_here = {}
    for chunk, kept, sent, other in ((1, kept1, sent1, other1), (0, kept0, sent0, other0)):
        passed = swap(other, to_other_side)
        rows_here[chunk] = [
            kept, passed, swap(sent, plan.by_rows()), swap(passed[1], plan.by_rows())
        ]

    near_totals, panel = make_group(near, far, pick_column, weightings)
    far_totals = swap(near_totals, plan.by_sums())
    totals = near_totals + far_totals
    for bit in plan.middle_bits + [plan.top_bit]:
        totals = totals + swap(totals, plan.by_mask(1 << bit)[0::2])
    told = swap(totals, to_other_side[0::2])
    first, second, stats = make_panels(near, far, totals, told, pick_column, weightings)

    across, top, after = [], [], [rows_here[0][2]]
    for even, odd in group_moments(plan, rows_here[1], panel, [totals]):
        arrived = swap(odd, plan.by_sums())
        met = meet(pick_column, near_totals, far_totals, stats, even, arrived, after)
        for bit in plan.middle_bits:
            met = met[0::2] + swap(met[1::2], plan.by_mask(1 << bit))
        across.append(met)
        top.append(swap(met, plan.by_mask(1 << plan.top_bit))[0])
        after = []

    last = not plan.middle_bits
    sums = moments(plan, rows_here[0], first, second, stats, last, across)
    if last:
        even, odd = sums[0::2], sums[1::2]
        other_owner = [(d, pair ^ 1) for d, pair in plan.by_sums()]
        parts = [
            [even[0], top[0], swap(odd[0], plan.by_sums())],
            [swap(even[1] + top[1], to_other_side), swap(odd[1], other_owner)],
        ]
    else:
        even, odd = sums
        arrived = swap(odd, plan.by_sums())
        for bit in plan.middle_bits:
            odd = even[1::2] + arrived[1::2]
            even = even[0::2] + arrived[0::2]
            arrived = swap(odd, plan.by_mask(1 << bit))
        total = [even[side] + arrived[side] + top[side] for side in range(2)]
        parts = [[total[0]], [swap(total[1], to_other_side)]]
    return finish(plan, parts, pick_column, stats, weightings)


def solution(mesh):
    placed = (
        P(("groups", "pat"), "cov"),
        P(("groups", "pat"), None),
        P(("groups", "pat"), "cov"),
        P(),
    )
    body = functools.partial(on_device, mesh.shape["pat"], mesh.shape["cov"])
    return jax.shard_map(
        body, mesh=mesh, in_specs=placed, out_specs=P("groups", "cov", "pat"), check_vma=False
    )
```

```python
import functools

import jax
import jax.numpy as jnp
from jax import lax
from jax.experimental import pallas as pl
from jax.experimental.pallas import tpu as pltpu
from jax.sharding import PartitionSpec as P

LANES = 128


def round_up(value, multiple):
    return -(-value // multiple) * multiple


class Plan:
    def __init__(self, n, block):
        self.n = n
        self.block = block
        self.tiles = round_up(block, LANES) // LANES
        self.share = (self.tiles + 1) // 2
        self.width = self.share * LANES
        self.places = n // 4
        *self.middle_bits, self.top_bit = range(3, n.bit_length() - 1)

    def by_rows(self):
        return [(d, d ^ (2 + 2 * (d & 1))) for d in range(self.n)]

    def by_sums(self):
        return [(d, d ^ (4 - 2 * (d & 1))) for d in range(self.n)]

    def by_mask(self, mask):
        return [(d, d ^ mask) for d in range(self.n)]


def pack_kernel(
    plan, x_ref, kept0_ref, kept1_ref, sent0_ref, sent1_ref, other0_ref, stay1_ref, pass1_ref
):
    step = pl.program_id(0)
    me = lax.axis_index("pat")
    rows, columns = x_ref.shape
    last_tile = columns // LANES - 1
    lane = lax.broadcasted_iota(jnp.int32, (rows, LANES), 1)

    def tile(index):
        return pl.ds(pl.multiple_of(jnp.minimum(index, last_tile) * LANES, LANES), LANES)

    for away in range(2):
        side = (me & 1) ^ away
        holder = me ^ away
        for sent in range(2):
            for chunk in range(2):
                middle = len(plan.middle_bits)
                relative = (
                    (step >> (1 + middle))
                    | (sent << (1 + side))
                    | ((step & 1) << (2 - side))
                    | (((step >> 1) & ((1 << middle) - 1)) << 3)
                    | (chunk << plan.top_bit)
                )
                column = (holder ^ relative) * plan.block
                first = column // LANES
                edge = (column - first * LANES) * (1 - side)
                head = x_ref[:, tile(first + side * plan.share)]
                tail = x_ref[:, tile(first + plan.tiles)]
                folded = jnp.where(lane >= edge, head.astype(jnp.float32), tail.astype(jnp.float32))
                if away:
                    target = (stay1_ref, pass1_ref)[sent] if chunk else other0_ref.at[sent]
                elif sent:
                    target = (sent0_ref, sent1_ref)[chunk]
                else:
                    target = (kept0_ref, kept1_ref)[chunk]
                target[:, 0:LANES] = folded.astype(x_ref.dtype)
                for slot in range(1, plan.share):
                    here = slice(slot * LANES, (slot + 1) * LANES)
                    target[:, here] = x_ref[:, tile(first + side * plan.share + slot)]


def pack(covariates, plan):
    rows = covariates.shape[0]
    dtype = covariates.dtype
    length = plan.places * rows
    mine = jax.ShapeDtypeStruct((length, plan.width), dtype)
    other = jax.ShapeDtypeStruct((2, length, plan.width), dtype)
    mine_spec = pl.BlockSpec((rows, plan.width), lambda s: (s, 0))
    other_spec = pl.BlockSpec((2, rows, plan.width), lambda s: (0, s, 0))
    return pl.pallas_call(
        functools.partial(pack_kernel, plan),
        grid=(plan.places,),
        in_specs=[pl.BlockSpec(memory_space=pltpu.VMEM)],
        out_specs=[mine_spec] * 4 + [other_spec] + [mine_spec] * 2,
        out_shape=[mine] * 4 + [other] + [mine] * 2,
        compiler_params=pltpu.CompilerParams(vmem_limit_bytes=12 << 20),
        cost_estimate=pl.CostEstimate(
            flops=0, bytes_accessed=4 * covariates.size, transcendentals=0
        ),
        name="pack",
    )(covariates)


def onehot_of(pick_ref, weightings, dtype):
    index = lax.broadcasted_iota(jnp.int32, (pick_ref.shape[0], weightings), 1)
    return jnp.where(index == pick_ref[...], 1.0, 0.0).astype(dtype)


def arm_columns(panel_ref, onehot):
    comps, weightings = onehot.shape
    weights = panel_ref[0:weightings, :]
    arms = panel_ref[weightings:weightings + comps, :].astype(jnp.float32)
    picked = jnp.dot(onehot, weights, preferred_element_type=jnp.float32)
    return weights, picked * arms, picked * (1.0 - arms)


def small_call(kernel, shapes, operands, after, name):
    vmem = pl.BlockSpec(memory_space=pltpu.VMEM)
    return pl.pallas_call(
        kernel,
        in_specs=[vmem] * len(operands) + [pl.BlockSpec(memory_space=pl.ANY)] * len(after),
        out_specs=[vmem] * len(shapes),
        out_shape=[jax.ShapeDtypeStruct(shape, dtype) for shape, dtype in shapes],
        compiler_params=pltpu.CompilerParams(vmem_limit_bytes=8 << 20),
        cost_estimate=pl.CostEstimate(flops=0, bytes_accessed=1 << 14, transcendentals=0),
        name=name,
    )(*operands, *after)


def lighter_of(totals):
    return jnp.where(totals[:, 0:1] <= totals[:, 1:2], 1.0, 0.0)


def lighter_panel(ref, members, onehot, light):
    comps, weightings = onehot.shape
    columns = []
    for place, member in enumerate(members):
        weights, target, other = arm_columns(member, onehot)
        here = slice(place * LANES, (place + 1) * LANES)
        lighter = light * target + (1.0 - light) * other
        ref[0:comps, here] = lighter.astype(jnp.bfloat16)
        ref[comps:comps + weightings, here] = weights
        columns.append((target, other))
    return columns


def members_of(near_ref, far_ref):
    return (near_ref.at[0], near_ref.at[1], far_ref.at[1], far_ref.at[0])


def group_kernel(weightings, pick_ref, near_ref, far_ref, totals_ref, panel_ref):
    onehot = onehot_of(pick_ref, weightings, jnp.bfloat16)
    target_sum, other_sum = 0.0, 0.0
    for member in members_of(near_ref, far_ref):
        _, target, other = arm_columns(member, onehot)
        target_sum += target
        other_sum += other
    lane = lax.broadcasted_iota(jnp.int32, totals_ref.shape, 1)
    totals = jnp.where(
        lane == 0,
        jnp.sum(target_sum, axis=1, keepdims=True),
        jnp.sum(other_sum, axis=1, keepdims=True),
    )
    totals_ref[...] = totals
    lighter_panel(panel_ref, members_of(near_ref, far_ref), onehot, lighter_of(totals))


def make_group(near, far, pick_column, weightings):
    comps = pick_column.shape[0]
    return small_call(
        functools.partial(group_kernel, weightings),
        [((comps, LANES), jnp.float32), ((comps + weightings, 4 * LANES), jnp.bfloat16)],
        [pick_column, near, far],
        [],
        "group",
    )


def panel_kernel(weightings, pick_ref, near_ref, far_ref, here_ref, told_ref, *refs):
    first_ref, second_ref, stats_ref = refs
    comps = pick_ref.shape[0]
    onehot = onehot_of(pick_ref, weightings, jnp.bfloat16)
    side = jnp.full(here_ref.shape, lax.axis_index("pat") & 1)
    totals = jnp.where(side == 0, here_ref[...], told_ref[...])
    light = lighter_of(totals)
    stats_ref[0] = jnp.broadcast_to(1.0 / totals[:, 0:1], (comps, LANES))
    stats_ref[1] = jnp.broadcast_to(1.0 / totals[:, 1:2], (comps, LANES))
    stats_ref[2] = jnp.broadcast_to(light, (comps, LANES))
    columns = lighter_panel(first_ref, members_of(near_ref, far_ref), onehot, light)
    for place, (target, other) in enumerate(columns):
        here = slice(place * LANES, (place + 1) * LANES)
        second_ref[0:comps, here] = target.astype(jnp.bfloat16)
        second_ref[comps:2 * comps, here] = other.astype(jnp.bfloat16)


def make_panels(near, far, totals, told, pick_column, weightings):
    comps = pick_column.shape[0]
    return small_call(
        functools.partial(panel_kernel, weightings),
        [
            ((comps + weightings, 4 * LANES), jnp.bfloat16),
            ((2 * comps, 4 * LANES), jnp.bfloat16),
            ((3, comps, LANES), jnp.float32),
        ],
        [pick_column, near, far, totals, told],
        [],
        "panels",
    )


def both_arms(sums, onehot, light):
    comps, weightings = onehot.shape
    lighter = sums[0:comps]
    both = jnp.dot(
        onehot,
        sums[comps:comps + weightings],
        precision=lax.Precision.HIGHEST,
        preferred_element_type=jnp.float32,
    )
    target = jnp.where(light, lighter, both - lighter)
    return target, jnp.where(light, both - lighter, lighter)


def meet_kernel(pick_ref, near_ref, far_ref, stats_ref, left_ref, right_ref, *refs):
    out_ref = refs[-1]
    comps = pick_ref.shape[0]
    rows = left_ref.shape[1] // 2
    onehot = onehot_of(pick_ref, rows - comps, jnp.float32)
    light = stats_ref[2][:, 0:1] > 0.5
    for block in range(left_ref.shape[0]):
        arms = []
        for moment in range(2):
            here = slice(moment * rows, (moment + 1) * rows)
            target, other = 0.0, 0.0
            for ref, totals_ref in ((left_ref, near_ref), (right_ref, far_ref)):
                more = both_arms(ref[block, here, :], onehot, lighter_of(totals_ref[...]) > 0.5)
                target, other = target + more[0], other + more[1]
            arms.append((target, other))
        out_ref[block, 0:comps, :] = jnp.where(light, arms[0][0], arms[0][1])
        out_ref[block, comps:rows, :] = (
            left_ref[block, comps:rows, :] + right_ref[block, comps:rows, :]
        )
        out_ref[block, rows:rows + comps, :] = (
            arms[1][0] * stats_ref[0][:, 0:1] + arms[1][1] * stats_ref[1][:, 0:1]
        )


def meet(pick_column, near_totals, far_totals, stats, left, right, after):
    blocks, rows, width = left.shape
    out = (blocks, rows // 2 + pick_column.shape[0], width)
    return small_call(
        meet_kernel,
        [(out, jnp.float32)],
        [pick_column, near_totals, far_totals, stats, left, right],
        after,
        "meet",
    )[0]


def whole_spec(shape):
    return pl.BlockSpec(shape, lambda s: (0,) * len(shape))


def moments_kernel(rows, split, *refs):
    kept_ref, passed_ref, *swapped_refs, first_ref, second_ref, stats_ref = refs[:7]
    outs = refs[-(2 if split is None else split):]
    first_rows = first_ref.shape[0]
    comps = second_ref.shape[0] // 2
    inverse_target = stats_ref[0][:, 0:1]
    inverse_other = stats_ref[1][:, 0:1]
    for place in range(swapped_refs[0].shape[0] // rows):
        here = slice(place * rows, (place + 1) * rows)
        x = jnp.concatenate(
            [kept_ref[here, :], passed_ref[0, here, :]]
            + [ref[here, :] for ref in swapped_refs],
            axis=0,
        )
        first = jnp.dot(first_ref[...], x, preferred_element_type=jnp.float32)
        squares = (x.astype(jnp.float32) * x.astype(jnp.float32)).astype(jnp.bfloat16)
        second = jnp.dot(second_ref[...], squares, preferred_element_type=jnp.float32)
        out = outs[place % 2].at[place // 2] if split is None else outs[place]
        out[0:first_rows, :] = first
        out[first_rows:first_rows + comps, :] = (
            second[0:comps] * inverse_target + second[comps:2 * comps] * inverse_other
        )


def group_moments_kernel(rows, count, *refs):
    kept_ref, passed_ref, *swapped_refs, panel_ref = refs[:5]
    outs = refs[-2 * count:]
    height = panel_ref.shape[0]
    places = kept_ref.shape[0] // rows
    for place in range(places):
        here = slice(place * rows, (place + 1) * rows)
        x = jnp.concatenate(
            [kept_ref[here, :], passed_ref[0, here, :]]
            + [ref[here, :] for ref in swapped_refs],
            axis=0,
        )
        squares = (x.astype(jnp.float32) * x.astype(jnp.float32)).astype(jnp.bfloat16)
        owner_side, middle = divmod(place // 2, places // 2 // count)
        out = outs[2 * owner_side + place % 2].at[middle]
        out[0:height, :] = jnp.dot(panel_ref[...], x, preferred_element_type=jnp.float32)
        out[height:2 * height, :] = jnp.dot(
            panel_ref[...], squares, preferred_element_type=jnp.float32
        )


def group_moments(plan, rows_here, panel, after):
    rows = panel.shape[1] // 4
    out = jax.ShapeDtypeStruct(
        (plan.places // 4, 2 * panel.shape[0], plan.width), jnp.float32
    )
    outs = pl.pallas_call(
        functools.partial(group_moments_kernel, rows, 2),
        in_specs=[pl.BlockSpec(memory_space=pltpu.VMEM)] * 5
        + [pl.BlockSpec(memory_space=pl.ANY)] * len(after),
        out_specs=[pl.BlockSpec(memory_space=pltpu.VMEM)] * 4,
        out_shape=[out] * 4,
        compiler_params=pltpu.CompilerParams(vmem_limit_bytes=10 << 20),
        cost_estimate=pl.CostEstimate(flops=0, bytes_accessed=6 << 20, transcendentals=0),
        name="group_moments",
    )(*rows_here, panel, *after)
    return outs[0:2], outs[2:4]


def moments(plan, rows_here, first, second, stats, split, after):
    rows = first.shape[1] // 4
    sums = (first.shape[0] + second.shape[0] // 2, plan.width)
    if split:
        out_shape = [jax.ShapeDtypeStruct(sums, jnp.float32)] * plan.places
    else:
        out_shape = [jax.ShapeDtypeStruct((plan.places // 2,) + sums, jnp.float32)] * 2
    return pl.pallas_call(
        functools.partial(moments_kernel, rows, plan.places if split else None),
        in_specs=[pl.BlockSpec(memory_space=pltpu.VMEM)] * 7
        + [pl.BlockSpec(memory_space=pl.ANY)] * len(after),
        out_specs=[pl.BlockSpec(memory_space=pltpu.VMEM)] * len(out_shape),
        out_shape=out_shape,
        compiler_params=pltpu.CompilerParams(vmem_limit_bytes=10 << 20),
        cost_estimate=pl.CostEstimate(flops=0, bytes_accessed=6 << 20, transcendentals=0),
        name="moments",
    )(*rows_here, first, second, stats, *after)


def finish_kernel(plan, weightings, counts, pick_ref, stats_ref, *refs):
    out_ref, ring_ref = refs[-2:]
    comps = pick_ref.shape[0]
    onehot = onehot_of(pick_ref, weightings, jnp.float32)
    inverse_target = stats_ref[0][:, 0:1]
    inverse_other = stats_ref[1][:, 0:1]
    light = stats_ref[2][:, 0:1] > 0.5
    me = lax.axis_index("pat")
    for away, count in enumerate(counts):
        sums = refs[0][...]
        for more in refs[1:count]:
            sums += more[...]
        refs = refs[count:]
        target, other = both_arms(sums, onehot, light)
        spread = sums[comps + weightings:2 * comps + weightings]
        mean_target = target * inverse_target
        mean_other = other * inverse_other
        variance = spread - mean_target * mean_target - mean_other * mean_other
        pooled = jnp.maximum(variance / 2.0, 0.01)
        balance = (mean_target - mean_other) / jnp.sqrt(pooled)
        for side in range(2):
            count = plan.tiles - plan.share if side else plan.share
            if count:
                lanes = slice(side * plan.width, side * plan.width + count * LANES)

                @pl.when((me & 1) ^ away == side)
                def _():
                    ring_ref[:, lanes] = balance[:, 0:count * LANES]
    width = plan.tiles * LANES
    shift = width - lax.rem(me * plan.block, LANES)
    out_ref[:, 0, :] = pltpu.roll(ring_ref[...], shift, 1)[:, 0:plan.block]


def finish(plan, parts, pick_column, stats, weightings):
    comps = pick_column.shape[0]
    operands = [array for part in parts for array in part]
    return pl.pallas_call(
        functools.partial(finish_kernel, plan, weightings, [len(part) for part in parts]),
        in_specs=[pl.BlockSpec(memory_space=pltpu.VMEM)] * (2 + len(operands)),
        out_specs=pl.BlockSpec(memory_space=pltpu.VMEM),
        out_shape=jax.ShapeDtypeStruct((comps, 1, plan.block), jnp.float32),
        scratch_shapes=[pltpu.VMEM((comps, plan.tiles * LANES), jnp.float32)],
        compiler_params=pltpu.CompilerParams(vmem_limit_bytes=12 << 20),
        cost_estimate=pl.CostEstimate(flops=0, bytes_accessed=1 << 14, transcendentals=0),
        name="finish",
    )(pick_column, stats, *operands)


def swap(array, pairs):
    return lax.ppermute(array, "pat", pairs)


def on_device(n, covs, covariates, weights, arms, pick):
    weightings = weights.shape[1]
    pick_column = pick.reshape(pick.shape[0], 1)
    plan = Plan(n, covariates.shape[1] // n)
    to_other_side = plan.by_mask(1)

    arm_rows = arms.T.astype(weights.dtype)
    if covs > 1:
        arm_rows = lax.all_gather(arm_rows, "cov", axis=0, tiled=True)
    mine = jnp.concatenate([weights.T, arm_rows], axis=0)
    near = jnp.stack([mine, swap(mine, to_other_side)])
    far = swap(near, [(pair ^ 1, d) for d, pair in plan.by_rows()])

    kept0, kept1, sent0, sent1, other0, stay1, pass1 = pack(covariates, plan)
    forward = swap(pass1, to_other_side)
    rows_here = {
        1: [
            kept1,
            swap(stay1[None], to_other_side),
            swap(sent1, plan.by_rows()),
            swap(forward, plan.by_rows()),
        ]
    }
    passed = swap(other0, to_other_side)
    rows_here[0] = [
        kept0, passed, swap(sent0, plan.by_rows()), swap(passed[1], plan.by_rows())
    ]

    near_totals, panel = make_group(near, far, pick_column, weightings)
    far_totals = swap(near_totals, plan.by_sums())
    totals = near_totals + far_totals
    for bit in plan.middle_bits + [plan.top_bit]:
        totals = totals + swap(totals, plan.by_mask(1 << bit)[0::2])
    told = swap(totals, to_other_side[0::2])
    first, second, stats = make_panels(near, far, totals, told, pick_column, weightings)

    across, top, after = [], [], [rows_here[0][2]]
    for even, odd in group_moments(plan, rows_here[1], panel, [totals]):
        arrived = swap(odd, plan.by_sums())
        met = meet(pick_column, near_totals, far_totals, stats, even, arrived, after)
        for bit in plan.middle_bits:
            met = met[0::2] + swap(met[1::2], plan.by_mask(1 << bit))
        across.append(met)
        top.append(swap(met, plan.by_mask(1 << plan.top_bit))[0])
        after = []

    last = not plan.middle_bits
    sums = moments(plan, rows_here[0], first, second, stats, last, across)
    if last:
        even, odd = sums[0::2], sums[1::2]
        other_owner = [(d, pair ^ 1) for d, pair in plan.by_sums()]
        parts = [
            [even[0], top[0], swap(odd[0], plan.by_sums())],
            [swap(even[1] + top[1], to_other_side), swap(odd[1], other_owner)],
        ]
    else:
        even, odd = sums
        arrived = swap(odd, plan.by_sums())
        for bit in plan.middle_bits:
            odd = even[1::2] + arrived[1::2]
            even = even[0::2] + arrived[0::2]
            arrived = swap(odd, plan.by_mask(1 << bit))
        total = [even[side] + arrived[side] + top[side] for side in range(2)]
        parts = [[total[0]], [swap(total[1], to_other_side)]]
    return finish(plan, parts, pick_column, stats, weightings)


def solution(mesh):
    placed = (
        P(("groups", "pat"), "cov"),
        P(("groups", "pat"), None),
        P(("groups", "pat"), "cov"),
        P(),
    )
    body = functools.partial(on_device, mesh.shape["pat"], mesh.shape["cov"])
    return jax.shard_map(
        body, mesh=mesh, in_specs=placed, out_specs=P("groups", "cov", "pat"), check_vma=False
    )
```
